32 devices in a mesh: date: 4 (over x, core), band: 8 (over z, y).
Axes of the slice: x: 2, y: 2, z: 4, core: 2. Of those that a mesh axis runs over, the one named last changes fastest.
Arguments:
- model_prognosis: bfloat16 [8, 2, 5, 32, 360], P('date', None, None, 'band'), may hold values from -6 to 6
- analysis_truth: bfloat16 [8, 2, 5, 128, 1440], P('date', None, None, 'band'), may hold values from -6 to 6
- expected_normal: bfloat16 [2, 5, 128, 1440], P(None, None, 'band'), may hold values from -5 to 5
- parallel_first_indices: int32 [128], P('band'), may hold values from -2 to 30, as said below
- parallel_blend_factors: float32 [128, 4], P('band'), may hold values from 0.05 to 0.5
- meridian_first_indices: int32 [1440], replicated, may hold values from 0 to 359, as said below
- meridian_blend_factors: bfloat16 [4, 1440], replicated, may hold values from 0.049804688 to 0.5
Outputs:
- sq_error: float32 [2, 5, 128, 1440], P(None, None, ('band', 'date'))
- anom_product: float32 [2, 5, 128, 1440], P(None, None, ('band', 'date'))
The draws below stay inside these ranges and needn't reach their ends.
Inputs may be any that keep to these rules, and one draw needn't show every extreme that they name: `parallel_first_indices`: fine row r's stencil starts at coarse row r // 4 - 2 or r // 4 - 1. `meridian_first_indices`: fine longitude x's stencil starts at coarse longitude (x // 4 - 1) or (x // 4), taken modulo 360.
All inputs are finite; a program needn't handle non-finite values.
Results may differ from the reference program's by a relative error of at most 0.0015.
Values may be sent and summed in bfloat16 or wider, within the bound.
No kernel may reach another device: no remote copies, remote signals or barrier semaphores. Data moves between devices by JAX's collectives and lax.ppermute only.
A program may use at most 64 MiB of HBM per device.

```python
import jax
import jax.numpy as jnp
from jax import lax

ASSESSED_QUANTS = 5
OUTLOOK_OFFSETS = 2
SPARSE_EASTINGS = 360
DENSE_EASTINGS = 1440
SPARSE_NORTHINGS = 32
DENSE_NORTHINGS = 128
ISSUE_MOMENTS = 8


def stencil_start(key, count):
    positions = jnp.arange(count, dtype=jnp.int32)
    extra = jax.random.randint(key, (count,), 0, 2, dtype=jnp.int32)
    extra = jnp.where(positions % 4 == 0, 0, jnp.where(positions % 4 == 3, 1, extra))
    return positions // 4 + extra


def draw_parallel_first_indices(key, part):
    return stencil_start(jax.random.fold_in(key, 11), DENSE_NORTHINGS) - 2


def draw_meridian_first_indices(key, part):
    return (stencil_start(jax.random.fold_in(key, 23), DENSE_EASTINGS) - 1) % SPARSE_EASTINGS


def level_of(stream_key, extent, pieces, smallest, high):
    level = 1.0
    for dim, blocks in pieces:
        steps = jax.random.uniform(jax.random.fold_in(jax.random.fold_in(stream_key, 6), dim), (blocks,), jnp.float32, smallest / len(pieces), high / len(pieces))
        level = level * jnp.repeat(jnp.exp(steps), extent[dim] // blocks).reshape((-1,) + (1,) * (len(extent) - 1 - dim))
    return level


def bell_draw(key, extent, deviation, limit, cuts=(), held_as=jnp.bfloat16):
    entries = jax.random.normal(key, extent, jnp.float32) * deviation
    if len(cuts) > 0:
        entries = level_of(key, extent, cuts, -0.22, 0.18) * entries
    return jnp.clip(entries, min=-limit, max=limit).astype(held_as)


def setup_inputs(seed: int = 0) -> dict:
    splits = jax.random.split(jax.random.key(seed), 8)
    model_prognosis = bell_draw(splits[0], (ISSUE_MOMENTS, OUTLOOK_OFFSETS, ASSESSED_QUANTS, SPARSE_NORTHINGS, SPARSE_EASTINGS), 1.0, 6.0, ((0, 4), (3, 8)))
    analysis_truth = bell_draw(splits[1], (ISSUE_MOMENTS, OUTLOOK_OFFSETS, ASSESSED_QUANTS, DENSE_NORTHINGS, DENSE_EASTINGS), 1.0, 6.0, ((0, 4), (3, 8)))
    expected_normal = bell_draw(splits[2], (OUTLOOK_OFFSETS, ASSESSED_QUANTS, DENSE_NORTHINGS, DENSE_EASTINGS), 0.7, 5.0, ((2, 8),))
    parallel_first_indices = draw_parallel_first_indices(jax.random.fold_in(splits[7], 71), 0)
    parallel_blend_factors = jnp.clip(0.05 + 0.45 * jax.random.uniform(splits[4], (DENSE_NORTHINGS, 4), jnp.float32) ** level_of(splits[4], (DENSE_NORTHINGS, 4), ((0, 8),), -0.2, 0.2), 0.05, 0.5)
    meridian_first_indices = draw_meridian_first_indices(jax.random.fold_in(splits[7], 71), 0)
    meridian_blend_factors = jnp.clip(jax.random.uniform(splits[6], (4, DENSE_EASTINGS), jnp.float32, 0.049804688, 0.5), 0.049804688, 0.5).astype(jnp.bfloat16)
    return dict(model_prognosis=model_prognosis, analysis_truth=analysis_truth, expected_normal=expected_normal, parallel_first_indices=parallel_first_indices, parallel_blend_factors=parallel_blend_factors, meridian_first_indices=meridian_first_indices, meridian_blend_factors=meridian_blend_factors)


def reference(model_prognosis, analysis_truth, expected_normal, parallel_first_indices, parallel_blend_factors, meridian_first_indices, meridian_blend_factors):
    climate = expected_normal.astype(jnp.float32)
    weights_lon = meridian_blend_factors.astype(jnp.float32)

    def issue_instance(loop_accumulator, argument_bundle):
        fields, actual_bf = argument_bundle
        fields32 = fields.astype(jnp.float32)
        through_axis = jnp.zeros(fields.shape[:-1] + (DENSE_EASTINGS,), jnp.float32)
        for stencil in range(4):
            columns = ((meridian_first_indices + stencil) % SPARSE_EASTINGS).astype(jnp.int32)
            through_axis = through_axis + weights_lon[stencil] * jnp.take(fields32, columns, axis=3)
        widened_grid = jnp.pad(through_axis, ((0, 0), (0, 0), (2, 2), (0, 0)))
        fine = jnp.zeros(through_axis.shape[:2] + (DENSE_NORTHINGS, DENSE_EASTINGS), jnp.float32)
        for stencil in range(4):
            rows_index = (parallel_first_indices + 2 + stencil).astype(jnp.int32)
            fine = fine + parallel_blend_factors[:, stencil][:, None] * jnp.take(widened_grid, rows_index, axis=2)
        actual = actual_bf.astype(jnp.float32)
        error_map = fine - actual
        fcst_anom = fine - climate
        true_anom = actual - climate
        return (loop_accumulator[0] + error_map * error_map, loop_accumulator[1] + fcst_anom * true_anom), None

    blank_seed_arrays = jnp.zeros((OUTLOOK_OFFSETS, ASSESSED_QUANTS, DENSE_NORTHINGS, DENSE_EASTINGS), jnp.float32)
    prefix_additions, discarded_result = lax.scan(issue_instance, (blank_seed_arrays, blank_seed_arrays), (model_prognosis, analysis_truth))
    return prefix_additions[0] / ISSUE_MOMENTS, prefix_additions[1] / ISSUE_MOMENTS
```

```python
import functools

import jax
import jax.numpy as jnp
from jax import lax
from jax.experimental import pallas as pl
from jax.experimental.pallas import tpu as pltpu
from jax.sharding import PartitionSpec as P

TAPS = 4
LANES = 128
WIDE = 256
CARRY_SCALE = 16.0


def edges_kernel(own_ref, kept_ref, cross_ref, pair_ref):
    even = lax.rem(lax.axis_index("band"), 2) == 0
    for index in range(own_ref.shape[0]):
        kept_ref[index] = own_ref[index]
        rows = own_ref[index].astype(jnp.float32)
        bottom, top = rows[:2], rows[rows.shape[0] - 2 :]
        pair_ref[index] = jnp.where(even, top, bottom).astype(jnp.bfloat16)
        cross_ref[index] = jnp.where(even, bottom, top).astype(jnp.bfloat16)


def taps_kernel(tap_ref):
    row = lax.broadcasted_iota(jnp.int32, tap_ref.shape, 0)
    tap_ref[...] = row - lax.broadcasted_iota(jnp.int32, tap_ref.shape, 1) // 4


def fill_tables(tap_ref, lon_ref, table_ref):
    dense = lon_ref.shape[1]
    for tile in range(pl.cdiv(dense, WIDE)):
        low_x = tile * WIDE
        width = min(WIDE, dense - low_x)
        base = low_x // 4 % LANES
        rows = width // 4 + 8
        depth_here = LANES if base + rows <= LANES else 2 * LANES
        columns = slice(low_x, low_x + width)
        offset = tap_ref[:rows, :width] - lon_ref[TAPS : TAPS + 1, columns].astype(jnp.int32)
        block = jnp.zeros((rows, width), jnp.float32)
        for tap in range(TAPS):
            block = jnp.where(offset == tap, lon_ref[tap : tap + 1, columns], block)
        parts = [block]
        if base:
            parts.insert(0, jnp.zeros((base, width), jnp.float32))
        if depth_here > base + rows:
            parts.append(jnp.zeros((depth_here - base - rows, width), jnp.float32))
        table_ref[tile, :depth_here, :width] = jnp.concatenate(parts, axis=0).astype(jnp.bfloat16)


def widened(lhs_ref, table_ref, tile, low_x, width):
    base = low_x // 4 % LANES
    begin = low_x // 4 - base
    depth = LANES if base + width // 4 + 8 <= LANES else 2 * LANES
    lhs = jnp.concatenate([lhs_ref[0, :, begin : begin + depth], lhs_ref[1, :, begin : begin + depth]], axis=1)
    table = table_ref[tile, :depth, :width]
    return jnp.dot(lhs, jnp.concatenate([table, table], axis=0), preferred_element_type=jnp.float32)


def wrapped_rows(rows, depth):
    sparse = rows.shape[1]
    filler = jnp.zeros((rows.shape[0], depth - sparse - 4), jnp.float32)
    return jnp.concatenate([rows[:, sparse - 1 :], rows, rows[:, :3], filler], axis=1)


def error_kernel(
    own_ref,
    cross_ref,
    pair_ref,
    truth_ref,
    tap_ref,
    lon_ref,
    lat_ref,
    out_ref,
    fine_ref,
    lhs_ref,
    table_ref,
):
    fields, coarse_rows, sparse = own_ref.shape
    _, fine_rows, dense = truth_ref.shape
    pairs = out_ref.shape[2]
    dates = fields // pairs
    ratio = fine_rows // coarse_rows
    span = 8 // ratio
    depth = lhs_ref.shape[2]
    tiles = pl.cdiv(dense, WIDE)
    band = lax.axis_index("band")
    even = lax.rem(band, 2) == 0
    lowest = band == 0
    highest = band == lax.axis_size("band") - 1

    fill_tables(tap_ref, lon_ref, table_ref)

    weights = lat_ref[...].T
    lat = [
        [
            jnp.broadcast_to(weights[8 * group : 8 * group + 8, tap : tap + 1], (8, LANES))
            for tap in range(TAPS + 1)
        ]
        for group in range(fine_rows // 8)
    ]
    lat = [[jnp.concatenate([w] * (depth // LANES), axis=1) for w in group] for group in lat]

    upper_half = lax.broadcasted_iota(jnp.int32, (8, depth), 0) < ratio
    for pair in range(pairs):
        for date in range(dates):
            index = date * pairs + pair
            paired = pair_ref[index].astype(jnp.float32)
            crossed = cross_ref[index].astype(jnp.float32)
            low = jnp.where(lowest, 0.0, jnp.where(even, crossed, paired))
            high = jnp.where(highest, 0.0, jnp.where(even, paired, crossed))
            rows8 = jnp.concatenate([low, own_ref[index].astype(jnp.float32), high], axis=0)
            wrapped = wrapped_rows(rows8, depth)
            spread = [jnp.broadcast_to(wrapped[i : i + 1], (8, depth)) for i in range(coarse_rows + 4)]
            mixed = [jnp.where(upper_half, spread[i], spread[i + 1]) for i in range(coarse_rows + 3)]
            both = []
            for group in range(fine_rows // 8):
                total = lat[group][0] * mixed[span * group]
                for tap in range(1, TAPS + 1):
                    total = total + lat[group][tap] * mixed[span * group + tap]
                both.append(total)
            both = jnp.concatenate(both, axis=0)
            upper = both.astype(jnp.bfloat16)
            rest = (both - upper.astype(jnp.float32)).astype(jnp.bfloat16)
            at = (pair * dates + date) * fine_rows
            lhs_ref[0, at : at + fine_rows, :] = upper
            lhs_ref[1, at : at + fine_rows, :] = rest

    for tile in range(tiles):
        low_x = tile * WIDE
        width = min(WIDE, dense - low_x)
        columns = slice(low_x, low_x + width)
        fine_ref[:, columns] = widened(lhs_ref, table_ref, tile, low_x, width)
        for pair in range(pairs):
            total = 0.0
            for date in range(dates):
                at = (pair * dates + date) * fine_rows
                actual = truth_ref[date * pairs + pair, :, columns].astype(jnp.float32)
                error = fine_ref[at : at + fine_rows, columns] - actual
                total = total + error * error
            store_by_owner(out_ref, pair, columns, total)


def store_by_owner(out_ref, pair, columns, values):
    _, halves, _, owned, _ = out_ref.shape
    for owner in range(2 * halves):
        out_ref[owner % 2, owner // 2, pair, :, columns] = values[owner * owned : (owner + 1) * owned]


def anomaly_kernel(fine_ref, truth_ref, normal_ref, out_ref):
    fields, fine_rows, dense = truth_ref.shape
    pairs = normal_ref.shape[0]
    dates = fields // pairs
    for low_x in range(0, dense, WIDE):
        columns = slice(low_x, min(low_x + WIDE, dense))
        for pair in range(pairs):
            normal = normal_ref[pair, :, columns].astype(jnp.float32)
            total = 0.0
            for date in range(dates):
                at = (pair * dates + date) * fine_rows
                actual = truth_ref[date * pairs + pair, :, columns].astype(jnp.float32)
                total = total + (fine_ref[at : at + fine_rows, columns] - normal) * (actual - normal)
            store_by_owner(out_ref, pair, columns, total)


def edge_rows(own):
    fields, _, sparse = own.shape
    vmem = pl.BlockSpec(memory_space=pltpu.VMEM)
    edges = jax.ShapeDtypeStruct((fields, 2, sparse), jnp.bfloat16)
    return pl.pallas_call(
        edges_kernel,
        out_shape=[jax.ShapeDtypeStruct(own.shape, own.dtype), edges, edges],
        in_specs=[vmem],
        out_specs=[vmem] * 3,
        compiler_params=pltpu.CompilerParams(vmem_limit_bytes=8 * 1024 * 1024),
        cost_estimate=pl.CostEstimate(flops=100_000_000, bytes_accessed=200_000, transcendentals=0),
    )(own)


def lat_tap_weights(starts, weights, first_coarse, ratio):
    rows = starts.shape[0]
    late = starts > first_coarse + lax.iota(jnp.int32, rows) // ratio - 2
    by_tap = weights.T
    early = jnp.pad(by_tap, ((0, 8 - TAPS), (0, LANES - rows)))
    shifted = jnp.pad(by_tap, ((1, 7 - TAPS), (0, LANES - rows)))
    return jnp.where(jnp.pad(late, (0, LANES - rows))[None], shifted, early)


def error_map(own, crossed, paired, truth, taps, lon, lat, pairs, owners):
    fields, _, sparse = own.shape
    _, fine_rows, dense = truth.shape
    depth = pl.cdiv(sparse + 4, LANES) * LANES
    vmem = pl.BlockSpec(memory_space=pltpu.VMEM)
    return pl.pallas_call(
        error_kernel,
        out_shape=[
            jax.ShapeDtypeStruct((2, owners // 2, pairs, fine_rows // owners, dense), jnp.float32),
            jax.ShapeDtypeStruct((fields * fine_rows, dense), jnp.float32),
        ],
        in_specs=[vmem] * 7,
        out_specs=[vmem] * 2,
        scratch_shapes=[
            pltpu.VMEM((2, fields * fine_rows, depth), jnp.bfloat16),
            pltpu.VMEM((pl.cdiv(dense, WIDE), 2 * LANES, WIDE), jnp.bfloat16),
        ],
        compiler_params=pltpu.CompilerParams(vmem_limit_bytes=24 * 1024 * 1024),
        cost_estimate=pl.CostEstimate(flops=1_000_000_000, bytes_accessed=4_000_000, transcendentals=0),
    )(own, crossed, paired, truth, taps, lon, lat)


def anomaly_map(fine, truth, normal, owners):
    pairs, fine_rows, dense = normal.shape
    vmem = pl.BlockSpec(memory_space=pltpu.VMEM)
    return pl.pallas_call(
        anomaly_kernel,
        out_shape=jax.ShapeDtypeStruct((2, owners // 2, pairs, fine_rows // owners, dense), jnp.float32),
        in_specs=[vmem] * 3,
        out_specs=vmem,
        compiler_params=pltpu.CompilerParams(vmem_limit_bytes=24 * 1024 * 1024),
        cost_estimate=pl.CostEstimate(flops=500_000_000, bytes_accessed=4_000_000, transcendentals=0),
    )(fine, truth, normal)


def first_core():
    return lax.rem(lax.axis_index("date"), 2) == 0


def lower_chip():
    return lax.axis_index("date") < lax.axis_size("date") // 2


def by_owner(ref, entries, lower):
    blocks = [ref[entry].astype(jnp.float32) for entry in entries]
    half = blocks[0].shape[0] // 2
    blocks = [jnp.where(lower, block[:half], block[half:]) for block in blocks]
    owned = half // 2
    return (
        jnp.concatenate([block[:owned] for block in blocks], axis=0),
        jnp.concatenate([block[owned:] for block in blocks], axis=0),
    )


def packed_tiles(entries, dense):
    full, tail = divmod(dense, LANES)
    return entries * full + (pl.cdiv(entries, LANES // tail) if tail else 0)


def pack_rows(blocks, out_ref):
    rows, dense = blocks[0].shape
    full, tail = divmod(dense, LANES)
    for at, block in enumerate(blocks):
        for tile in range(full):
            out_ref[at * full + tile] = block[:, tile * LANES : (tile + 1) * LANES].astype(out_ref.dtype)
    if tail:
        share = LANES // tail
        tails = [block[:, full * LANES :] for block in blocks]
        tails += [jnp.zeros((rows, tail), jnp.float32)] * (-len(tails) % share)
        filler = [jnp.zeros((rows, LANES - share * tail), jnp.float32)] if LANES % tail else []
        for at in range(0, len(tails), share):
            joined = jnp.concatenate(tails[at : at + share] + filler, axis=1)
            out_ref[len(blocks) * full + at // share] = joined.astype(out_ref.dtype)


def unpacked_rows(ref, at, entries, dense, low_x, width):
    full, tail = divmod(dense, LANES)
    parts = [
        ref[at * full + tile].astype(jnp.float32)
        for tile in range(low_x // LANES, min((low_x + width) // LANES, full))
    ]
    if low_x + width > full * LANES:
        share = LANES // tail
        start = at % share * tail
        parts.append(ref[entries * full + at // share].astype(jnp.float32)[:, start : start + tail])
    return jnp.concatenate(parts, axis=1)


def away_kernel(dates, truth_ref, _, straight_ref, crossed_ref):
    pairs = truth_ref.shape[0] // dates
    first = first_core()
    straight, crossed = [], []
    for pair in range(pairs):
        entries = [date * pairs + pair for date in range(dates)]
        one, two = by_owner(truth_ref, entries, jnp.logical_not(lower_chip()))
        straight.append(jnp.where(first, one, two))
        crossed.append(jnp.where(first, two, one))
    pack_rows(straight, straight_ref)
    pack_rows(crossed, crossed_ref)


def home_kernel(dates, truth_ref, normal_ref, mine_ref, sibling_ref, normals_ref):
    pairs = normal_ref.shape[0]
    first = first_core()
    lower = lower_chip()
    for pair in range(pairs):
        one, two = by_owner(truth_ref, [date * pairs + pair for date in range(dates)], lower)
        mine_ref[pair] = jnp.where(first, one, two).astype(mine_ref.dtype)
        sibling_ref[pair] = jnp.where(first, two, one).astype(sibling_ref.dtype)
        one, two = by_owner(normal_ref, [pair] * dates, lower)
        normals_ref[pair] = jnp.where(first, one, two)


def shift_rows_kernel(own_ref, peer_ref, both_ref, rows_ref):
    lower = lower_chip()
    fields, coarse_rows, _ = own_ref.shape
    for index in range(2 * fields):
        block = (own_ref if index < fields else peer_ref)[index % fields]
        both_ref[index] = block
        block = block.astype(jnp.float32)
        rows_ref[index] = jnp.where(lower, block[coarse_rows - 2 :], block[:2]).astype(jnp.bfloat16)


def latitude_step(pairs, coarse_ref, halo_ref, lat_ref, lhs_ref, stage_ref):
    fields = coarse_ref.shape[0] // 2
    dates = fields // pairs
    depth = lhs_ref.shape[2]
    rows = lhs_ref.shape[1] // (2 * pairs)
    owned = rows // dates
    band = lax.axis_index("band")
    lower = lower_chip()
    first = first_core()
    outside = jnp.logical_or(
        jnp.logical_and(lower, band == 0),
        jnp.logical_and(jnp.logical_not(lower), band == lax.axis_size("band") - 1),
    )
    weights = lat_ref[...].T
    weights = jnp.where(lower, weights[: 2 * owned], weights[2 * owned : 4 * owned])
    weights = jnp.where(first, weights[:owned], weights[owned:])
    weights = jnp.concatenate([weights] * dates, axis=0)
    lat = [jnp.broadcast_to(weights[:, tap : tap + 1], (rows, depth)) for tap in range(TAPS + 1)]
    date_of_row = lax.broadcasted_iota(jnp.int32, (rows, depth), 0) // owned
    for side in range(2):
        for pair in range(pairs):
            sources = []
            for date in range(dates):
                index = side * fields + date * pairs + pair
                inner = coarse_ref[index].astype(jnp.float32)
                edge = jnp.where(outside, 0.0, halo_ref[index].astype(jnp.float32))
                below = jnp.concatenate([edge, inner], axis=0)
                above = jnp.concatenate([inner, edge], axis=0)
                wrapped = wrapped_rows(jnp.where(lower, below, above), depth)
                sources.append(jnp.where(first, wrapped[: TAPS + 1], wrapped[1 : TAPS + 2]))
            total = 0.0
            for tap in range(TAPS + 1):
                mixed = jnp.broadcast_to(sources[0][tap : tap + 1], (rows, depth))
                for date in range(1, dates):
                    spread = jnp.broadcast_to(sources[date][tap : tap + 1], (rows, depth))
                    mixed = jnp.where(date_of_row == date, spread, mixed)
                total = total + lat[tap] * mixed
            upper = total.astype(jnp.bfloat16).astype(jnp.float32)
            at = (side * pairs + pair) * rows
            stage_ref[at : at + rows, :depth] = upper
            stage_ref[at : at + rows, depth:] = total - upper
    lhs_ref[0] = stage_ref[:, :depth].astype(jnp.bfloat16)
    lhs_ref[1] = stage_ref[:, depth:].astype(jnp.bfloat16)


def column_blocks(dense):
    for tile in range(pl.cdiv(dense, WIDE)):
        low_x = tile * WIDE
        width = min(WIDE, dense - low_x)
        yield tile, low_x, width, slice(low_x, low_x + width)


def added(sums, fine, actual, normal):
    error = fine - actual
    return sums[0] + error * error, sums[1] + (fine - normal) * (actual - normal)


def own_dates_kernel(
    coarse_ref,
    halo_ref,
    truth_ref,
    normals_ref,
    lat_ref,
    tap_ref,
    lon_ref,
    sums_ref,
    away_ref,
    table_ref,
    lhs_ref,
    stage_ref,
):
    pairs, rows, dense = truth_ref.shape
    fill_tables(tap_ref, lon_ref, table_ref)
    latitude_step(pairs, coarse_ref, halo_ref, lat_ref, lhs_ref, stage_ref)
    for tile, low_x, width, columns in column_blocks(dense):
        stage_ref[:, :width] = widened(lhs_ref, table_ref, tile, low_x, width)
        away_ref[:, columns] = stage_ref[pairs * rows :, :width]
        for pair in range(pairs):
            fine = stage_ref[pair * rows : (pair + 1) * rows, :width]
            actual = truth_ref[pair, :, columns].astype(jnp.float32)
            sums = added((0.0, 0.0), fine, actual, normals_ref[pair, :, columns])
            sums_ref[0, pair, :, columns], sums_ref[1, pair, :, columns] = sums


def sibling_dates_kernel(
    coarse_ref,
    halo_ref,
    truth_ref,
    normals_ref,
    lat_ref,
    table_ref,
    before_ref,
    straight_fine_ref,
    straight_ref,
    sums_ref,
    away_ref,
    lhs_ref,
    stage_ref,
):
    pairs, rows, dense = truth_ref.shape
    latitude_step(pairs, coarse_ref, halo_ref, lat_ref, lhs_ref, stage_ref)
    for tile, low_x, width, columns in column_blocks(dense):
        stage_ref[:, :width] = widened(lhs_ref, table_ref, tile, low_x, width)
        away_ref[:, columns] = stage_ref[pairs * rows :, :width]
        for pair in range(pairs):
            span = slice(pair * rows, (pair + 1) * rows)
            normal = normals_ref[pair, :, columns]
            sums = (before_ref[0, pair, :, columns], before_ref[1, pair, :, columns])
            actual = truth_ref[pair, :, columns].astype(jnp.float32)
            sums = added(sums, stage_ref[span, :width], actual, normal)
            actual = unpacked_rows(straight_ref, pair, pairs, dense, low_x, width)
            sums = added(sums, straight_fine_ref[span, columns], actual, normal)
            sums_ref[0, pair, :, columns], sums_ref[1, pair, :, columns] = sums


def mean_kernel(dates, count, before_ref, fine_ref, crossed_ref, normals_ref, *results):
    pairs, rows, dense = normals_ref.shape
    owned = rows // dates
    for _, low_x, width, columns in column_blocks(dense):
        for pair in range(pairs):
            sums = (before_ref[0, pair, :, columns], before_ref[1, pair, :, columns])
            actual = unpacked_rows(crossed_ref, pair, pairs, dense, low_x, width)
            fine = fine_ref[pair * rows : (pair + 1) * rows, columns]
            sums = added(sums, fine, actual, normals_ref[pair, :, columns])
            for total, out_ref in zip(sums, results):
                parts = [total[date * owned : (date + 1) * owned] for date in range(dates)]
                out_ref[pair, :, columns] = sum(parts[1:], parts[0]) / count


def kernel_call(kernel, out_shape, scratch, megabytes, flops, *operands):
    vmem = pl.BlockSpec(memory_space=pltpu.VMEM)
    return pl.pallas_call(
        kernel,
        out_shape=out_shape,
        in_specs=[vmem] * len(operands),
        out_specs=[vmem] * len(out_shape),
        scratch_shapes=scratch,
        compiler_params=pltpu.CompilerParams(vmem_limit_bytes=megabytes * 1024 * 1024),
        cost_estimate=pl.CostEstimate(flops=flops, bytes_accessed=0, transcendentals=0),
    )(*operands)


def two_chip_maps(model_prognosis, analysis_truth, expected_normal, taps, lon_weights, lat_weights):
    bands = lax.axis_size("band")
    groups = lax.axis_size("date")
    dates, leads, variables, coarse_rows, sparse = model_prognosis.shape
    fine_rows, dense = analysis_truth.shape[3:]
    owned = fine_rows // groups
    rows = dates * owned
    pairs = leads * variables
    fields = dates * pairs
    depth = pl.cdiv(sparse + 4, LANES) * LANES
    float32, bfloat16 = jnp.float32, jnp.bfloat16
    straight_way = [(i, (i + 2) % groups) for i in range(groups)]
    crossed_way = [(i, (i + 2) % groups ^ 1) for i in range(groups)]
    sibling_way = [(i, i ^ 1) for i in range(groups)]

    own = model_prognosis.reshape(fields, coarse_rows, sparse)
    truth = analysis_truth.reshape(fields, fine_rows, dense)
    normal = expected_normal.reshape(pairs, fine_rows, dense)
    peer = lax.ppermute(model_prognosis, "date", straight_way).reshape(own.shape)

    packed = jax.ShapeDtypeStruct((packed_tiles(pairs, dense), rows, LANES), bfloat16)
    straight, crossed = kernel_call(
        functools.partial(away_kernel, dates), [packed, packed], [], 8, 100_000_000, truth, taps
    )
    straight = lax.ppermute(straight, "date", straight_way)
    crossed = lax.ppermute(crossed, "date", crossed_way)
    plain = jax.ShapeDtypeStruct((pairs, rows, dense), bfloat16)
    mine, sibling, normals = kernel_call(
        functools.partial(home_kernel, dates),
        [plain, plain, jax.ShapeDtypeStruct((pairs, rows, dense), float32)],
        [],
        12,
        100_000_000,
        truth,
        normal,
    )
    sibling = lax.ppermute(sibling, "date", sibling_way)

    chain = []
    for group in range(groups):
        for band in range(bands):
            to = band + (1 if group < groups // 2 else -1)
            if 0 <= to < bands:
                chain.append((group * bands + band, group * bands + to))
    coarse, edges = kernel_call(
        shift_rows_kernel,
        [
            jax.ShapeDtypeStruct((2 * fields, coarse_rows, sparse), bfloat16),
            jax.ShapeDtypeStruct((2 * fields, 2, sparse), bfloat16),
        ],
        [],
        8,
        100_000_000,
        own,
        peer,
    )
    halo = lax.ppermute(edges, ("date", "band"), chain)
    sibling_coarse = lax.ppermute(coarse, "date", sibling_way)
    sibling_halo = lax.ppermute(halo, "date", sibling_way)

    sums = jax.ShapeDtypeStruct((2, pairs, rows, dense), float32)
    away = jax.ShapeDtypeStruct((pairs * rows, dense), float32)
    table = jax.ShapeDtypeStruct((pl.cdiv(dense, WIDE), 2 * LANES, WIDE), bfloat16)
    scratch = [
        pltpu.VMEM((2, 2 * pairs * rows, depth), bfloat16),
        pltpu.VMEM((2 * pairs * rows, 2 * depth), float32),
    ]
    own_sums, straight_fine, table = kernel_call(
        own_dates_kernel,
        [sums, away, table],
        scratch,
        20,
        0,
        coarse,
        halo,
        mine,
        normals,
        lat_weights,
        taps,
        lon_weights,
    )
    chip_sums, crossed_fine = kernel_call(
        sibling_dates_kernel,
        [sums, away],
        scratch,
        20,
        0,
        sibling_coarse,
        sibling_halo,
        sibling,
        normals,
        lat_weights,
        table,
        own_sums,
        straight_fine,
        straight,
    )
    out = jax.ShapeDtypeStruct((pairs, owned, dense), float32)
    results = kernel_call(
        functools.partial(mean_kernel, dates, dates * groups),
        [out, out],
        [],
        16,
        0,
        chip_sums,
        crossed_fine,
        crossed,
        normals,
    )
    return tuple(result.reshape(leads, variables, owned, dense) for result in results)


def shards(
    model_prognosis,
    analysis_truth,
    expected_normal,
    parallel_first_indices,
    parallel_blend_factors,
    meridian_first_indices,
    meridian_blend_factors,
):
    bands = lax.axis_size("band")
    groups = lax.axis_size("date")
    halves = groups // 2
    dates = model_prognosis.shape[0]
    group = lax.axis_index("date")
    core = lax.rem(group, 2)
    half = lax.div(group, 2)

    coarse_rows = model_prognosis.shape[3]
    lat_weights = lat_tap_weights(
        parallel_first_indices,
        parallel_blend_factors,
        lax.axis_index("band") * coarse_rows,
        analysis_truth.shape[3] // coarse_rows,
    )
    dense = meridian_first_indices.shape[0]
    late = meridian_first_indices == lax.iota(jnp.int32, dense) // 4
    lon_weights = jnp.where(
        lax.broadcasted_iota(jnp.int32, (8, dense), 0) < TAPS,
        jnp.pad(meridian_blend_factors, ((0, 8 - TAPS), (0, 0))).astype(jnp.float32),
        late.astype(jnp.float32)[None],
    )
    (taps,) = kernel_call(
        taps_kernel, [jax.ShapeDtypeStruct((WIDE // 4 + 8, WIDE), jnp.int32)], [], 8, 2_000_000_000
    )
    if halves == 2 and dates * analysis_truth.shape[3] == 8 * groups:
        return two_chip_maps(model_prognosis, analysis_truth, expected_normal, taps, lon_weights, lat_weights)

    own = model_prognosis.reshape((-1,) + model_prognosis.shape[3:])
    own, to_cross, to_pair = edge_rows(own)
    across = [(i, min(max(i + (1 if i % 2 else -1), 0), bands - 1)) for i in range(bands)]
    paired = lax.ppermute(to_pair, "band", [(i, i ^ 1) for i in range(bands)])
    crossed = lax.ppermute(to_cross, "band", across)
    truth = analysis_truth.reshape((-1,) + analysis_truth.shape[3:])
    normal = expected_normal.reshape((-1,) + expected_normal.shape[2:])
    error, fine = error_map(own, crossed, paired, truth, taps, lon_weights, lat_weights, normal.shape[0], groups)
    anomaly = anomaly_map(fine, truth, normal, groups)

    def packed(values):
        return (values * CARRY_SCALE).astype(jnp.float16)

    def unpacked(values):
        return values.astype(jnp.float32) / CARRY_SCALE

    def row_block(values, index):
        return lax.dynamic_index_in_dim(values, index, 0, keepdims=False)

    def mean_over_dates(maps):
        swapped = lax.ppermute(packed(row_block(maps, 1 - core)), "date", [(i, i ^ 1) for i in range(groups)])

        def chip_sum(index):
            mine = lax.dynamic_slice(maps, (core, index, 0, 0, 0), (1, 1) + maps.shape[2:])[0, 0]
            return mine + unpacked(row_block(swapped, index))

        pieces = []
        for step in range(1, halves):
            piece = packed(chip_sum(lax.rem(half + step, halves)))
            ring = [(i, (i + 2 * step) % groups) for i in range(groups)]
            pieces.append(lax.ppermute(piece, "date", ring))
        total = chip_sum(half)
        for piece in pieces:
            total = total + unpacked(piece)
        total = total / (dates * groups)
        return total.reshape(expected_normal.shape[:2] + total.shape[1:])

    return (mean_over_dates(error), mean_over_dates(anomaly))


def solution(mesh):
    in_specs = (
        P("date", None, None, "band", None),
        P("date", None, None, "band", None),
        P(None, None, "band", None),
        P("band"),
        P("band", None),
        P(),
        P(),
    )
    out_specs = (P(None, None, ("band", "date"), None), P(None, None, ("band", "date"), None))
    return jax.shard_map(shards, mesh=mesh, in_specs=in_specs, out_specs=out_specs, check_vma=False)
```

```python
import functools

import jax
import jax.numpy as jnp
from jax import lax
from jax.experimental import pallas as pl
from jax.experimental.pallas import tpu as pltpu
from jax.sharding import PartitionSpec as P

TAPS = 4
LANES = 128
WIDE = 256
CARRY_SCALE = 16.0


def edges_kernel(own_ref, kept_ref, cross_ref, pair_ref):
    even = lax.rem(lax.axis_index("band"), 2) == 0
    for index in range(own_ref.shape[0]):
        kept_ref[index] = own_ref[index]
        rows = own_ref[index].astype(jnp.float32)
        bottom, top = rows[:2], rows[rows.shape[0] - 2 :]
        pair_ref[index] = jnp.where(even, top, bottom).astype(jnp.bfloat16)
        cross_ref[index] = jnp.where(even, bottom, top).astype(jnp.bfloat16)


def taps_kernel(tap_ref):
    row = lax.broadcasted_iota(jnp.int32, tap_ref.shape, 0)
    tap_ref[...] = row - lax.broadcasted_iota(jnp.int32, tap_ref.shape, 1) // 4


def fill_tables(tap_ref, lon_ref, table_ref):
    dense = lon_ref.shape[1]
    for tile in range(pl.cdiv(dense, WIDE)):
        low_x = tile * WIDE
        width = min(WIDE, dense - low_x)
        base = low_x // 4 % LANES
        rows = width // 4 + 8
        depth_here = LANES if base + rows <= LANES else 2 * LANES
        columns = slice(low_x, low_x + width)
        offset = tap_ref[:rows, :width] - lon_ref[TAPS : TAPS + 1, columns].astype(jnp.int32)
        block = jnp.zeros((rows, width), jnp.float32)
        for tap in range(TAPS):
            block = jnp.where(offset == tap, lon_ref[tap : tap + 1, columns], block)
        parts = [block]
        if base:
            parts.insert(0, jnp.zeros((base, width), jnp.float32))
        if depth_here > base + rows:
            parts.append(jnp.zeros((depth_here - base - rows, width), jnp.float32))
        table_ref[tile, :depth_here, :width] = jnp.concatenate(parts, axis=0).astype(jnp.bfloat16)


def widened(lhs_ref, table_ref, tile, low_x, width):
    base = low_x // 4 % LANES
    begin = low_x // 4 - base
    depth = LANES if base + width // 4 + 8 <= LANES else 2 * LANES
    lhs = jnp.concatenate([lhs_ref[0, :, begin : begin + depth], lhs_ref[1, :, begin : begin + depth]], axis=1)
    table = table_ref[tile, :depth, :width]
    return jnp.dot(lhs, jnp.concatenate([table, table], axis=0), preferred_element_type=jnp.float32)


def wrapped_rows(rows, depth):
    sparse = rows.shape[1]
    filler = jnp.zeros((rows.shape[0], depth - sparse - 4), jnp.float32)
    return jnp.concatenate([rows[:, sparse - 1 :], rows, rows[:, :3], filler], axis=1)


def error_kernel(
    own_ref,
    cross_ref,
    pair_ref,
    truth_ref,
    tap_ref,
    lon_ref,
    lat_ref,
    out_ref,
    fine_ref,
    lhs_ref,
    table_ref,
):
    fields, coarse_rows, sparse = own_ref.shape
    _, fine_rows, dense = truth_ref.shape
    pairs = out_ref.shape[2]
    dates = fields // pairs
    ratio = fine_rows // coarse_rows
    span = 8 // ratio
    depth = lhs_ref.shape[2]
    tiles = pl.cdiv(dense, WIDE)
    band = lax.axis_index("band")
    even = lax.rem(band, 2) == 0
    lowest = band == 0
    highest = band == lax.axis_size("band") - 1

    fill_tables(tap_ref, lon_ref, table_ref)

    weights = lat_ref[...].T
    lat = [
        [
            jnp.broadcast_to(weights[8 * group : 8 * group + 8, tap : tap + 1], (8, LANES))
            for tap in range(TAPS + 1)
        ]
        for group in range(fine_rows // 8)
    ]
    lat = [[jnp.concatenate([w] * (depth // LANES), axis=1) for w in group] for group in lat]

    upper_half = lax.broadcasted_iota(jnp.int32, (8, depth), 0) < ratio
    for pair in range(pairs):
        for date in range(dates):
            index = date * pairs + pair
            paired = pair_ref[index].astype(jnp.float32)
            crossed = cross_ref[index].astype(jnp.float32)
            low = jnp.where(lowest, 0.0, jnp.where(even, crossed, paired))
            high = jnp.where(highest, 0.0, jnp.where(even, paired, crossed))
            rows8 = jnp.concatenate([low, own_ref[index].astype(jnp.float32), high], axis=0)
            wrapped = wrapped_rows(rows8, depth)
            spread = [jnp.broadcast_to(wrapped[i : i + 1], (8, depth)) for i in range(coarse_rows + 4)]
            mixed = [jnp.where(upper_half, spread[i], spread[i + 1]) for i in range(coarse_rows + 3)]
            both = []
            for group in range(fine_rows // 8):
                total = lat[group][0] * mixed[span * group]
                for tap in range(1, TAPS + 1):
                    total = total + lat[group][tap] * mixed[span * group + tap]
                both.append(total)
            both = jnp.concatenate(both, axis=0)
            upper = both.astype(jnp.bfloat16)
            rest = (both - upper.astype(jnp.float32)).astype(jnp.bfloat16)
            at = (pair * dates + date) * fine_rows
            lhs_ref[0, at : at + fine_rows, :] = upper
            lhs_ref[1, at : at + fine_rows, :] = rest

    for tile in range(tiles):
        low_x = tile * WIDE
        width = min(WIDE, dense - low_x)
        columns = slice(low_x, low_x + width)
        fine_ref[:, columns] = widened(lhs_ref, table_ref, tile, low_x, width)
        for pair in range(pairs):
            total = 0.0
            for date in range(dates):
                at = (pair * dates + date) * fine_rows
                actual = truth_ref[date * pairs + pair, :, columns].astype(jnp.float32)
                error = fine_ref[at : at + fine_rows, columns] - actual
                total = total + error * error
            store_by_owner(out_ref, pair, columns, total)


def store_by_owner(out_ref, pair, columns, values):
    _, halves, _, owned, _ = out_ref.shape
    for owner in range(2 * halves):
        out_ref[owner % 2, owner // 2, pair, :, columns] = values[owner * owned : (owner + 1) * owned]


def anomaly_kernel(fine_ref, truth_ref, normal_ref, out_ref):
    fields, fine_rows, dense = truth_ref.shape
    pairs = normal_ref.shape[0]
    dates = fields // pairs
    for low_x in range(0, dense, WIDE):
        columns = slice(low_x, min(low_x + WIDE, dense))
        for pair in range(pairs):
            normal = normal_ref[pair, :, columns].astype(jnp.float32)
            total = 0.0
            for date in range(dates):
                at = (pair * dates + date) * fine_rows
                actual = truth_ref[date * pairs + pair, :, columns].astype(jnp.float32)
                total = total + (fine_ref[at : at + fine_rows, columns] - normal) * (actual - normal)
            store_by_owner(out_ref, pair, columns, total)


def edge_rows(own):
    fields, _, sparse = own.shape
    vmem = pl.BlockSpec(memory_space=pltpu.VMEM)
    edges = jax.ShapeDtypeStruct((fields, 2, sparse), jnp.bfloat16)
    return pl.pallas_call(
        edges_kernel,
        out_shape=[jax.ShapeDtypeStruct(own.shape, own.dtype), edges, edges],
        in_specs=[vmem],
        out_specs=[vmem] * 3,
        compiler_params=pltpu.CompilerParams(vmem_limit_bytes=8 * 1024 * 1024),
        cost_estimate=pl.CostEstimate(flops=100_000_000, bytes_accessed=200_000, transcendentals=0),
    )(own)


def lat_tap_weights(starts, weights, first_coarse, ratio):
    rows = starts.shape[0]
    late = starts > first_coarse + lax.iota(jnp.int32, rows) // ratio - 2
    by_tap = weights.T
    early = jnp.pad(by_tap, ((0, 8 - TAPS), (0, LANES - rows)))
    shifted = jnp.pad(by_tap, ((1, 7 - TAPS), (0, LANES - rows)))
    return jnp.where(jnp.pad(late, (0, LANES - rows))[None], shifted, early)


def error_map(own, crossed, paired, truth, taps, lon, lat, pairs, owners):
    fields, _, sparse = own.shape
    _, fine_rows, dense = truth.shape
    depth = pl.cdiv(sparse + 4, LANES) * LANES
    vmem = pl.BlockSpec(memory_space=pltpu.VMEM)
    return pl.pallas_call(
        error_kernel,
        out_shape=[
            jax.ShapeDtypeStruct((2, owners // 2, pairs, fine_rows // owners, dense), jnp.float32),
            jax.ShapeDtypeStruct((fields * fine_rows, dense), jnp.float32),
        ],
        in_specs=[vmem] * 7,
        out_specs=[vmem] * 2,
        scratch_shapes=[
            pltpu.VMEM((2, fields * fine_rows, depth), jnp.bfloat16),
            pltpu.VMEM((pl.cdiv(dense, WIDE), 2 * LANES, WIDE), jnp.bfloat16),
        ],
        compiler_params=pltpu.CompilerParams(vmem_limit_bytes=24 * 1024 * 1024),
        cost_estimate=pl.CostEstimate(flops=1_000_000_000, bytes_accessed=4_000_000, transcendentals=0),
    )(own, crossed, paired, truth, taps, lon, lat)


def anomaly_map(fine, truth, normal, owners):
    pairs, fine_rows, dense = normal.shape
    vmem = pl.BlockSpec(memory_space=pltpu.VMEM)
    return pl.pallas_call(
        anomaly_kernel,
        out_shape=jax.ShapeDtypeStruct((2, owners // 2, pairs, fine_rows // owners, dense), jnp.float32),
        in_specs=[vmem] * 3,
        out_specs=vmem,
        compiler_params=pltpu.CompilerParams(vmem_limit_bytes=24 * 1024 * 1024),
        cost_estimate=pl.CostEstimate(flops=500_000_000, bytes_accessed=4_000_000, transcendentals=0),
    )(fine, truth, normal)


def first_core():
    return lax.rem(lax.axis_index("date"), 2) == 0


def lower_chip():
    return lax.axis_index("date") < lax.axis_size("date") // 2


def by_owner(ref, entries, lower):
    blocks = [ref[entry].astype(jnp.float32) for entry in entries]
    half = blocks[0].shape[0] // 2
    blocks = [jnp.where(lower, block[:half], block[half:]) for block in blocks]
    owned = half // 2
    return (
        jnp.concatenate([block[:owned] for block in blocks], axis=0),
        jnp.concatenate([block[owned:] for block in blocks], axis=0),
    )


def packed_tiles(entries, dense):
    full, tail = divmod(dense, LANES)
    return entries * full + (pl.cdiv(entries, LANES // tail) if tail else 0)


def pack_rows(blocks, out_ref):
    rows, dense = blocks[0].shape
    full, tail = divmod(dense, LANES)
    for at, block in enumerate(blocks):
        for tile in range(full):
            out_ref[at * full + tile] = block[:, tile * LANES : (tile + 1) * LANES].astype(out_ref.dtype)
    if tail:
        share = LANES // tail
        tails = [block[:, full * LANES :] for block in blocks]
        tails += [jnp.zeros((rows, tail), jnp.float32)] * (-len(tails) % share)
        filler = [jnp.zeros((rows, LANES - share * tail), jnp.float32)] if LANES % tail else []
        for at in range(0, len(tails), share):
            joined = jnp.concatenate(tails[at : at + share] + filler, axis=1)
            out_ref[len(blocks) * full + at // share] = joined.astype(out_ref.dtype)


def unpacked_rows(ref, at, entries, dense, low_x, width):
    full, tail = divmod(dense, LANES)
    parts = [
        ref[at * full + tile].astype(jnp.float32)
        for tile in range(low_x // LANES, min((low_x + width) // LANES, full))
    ]
    if low_x + width > full * LANES:
        share = LANES // tail
        start = at % share * tail
        parts.append(ref[entries * full + at // share].astype(jnp.float32)[:, start : start + tail])
    return jnp.concatenate(parts, axis=1)


def tile_entries(pairs, dates):
    return [[date * pairs + pair, date * pairs + pair + 1] for pair in range(0, pairs, 2) for date in range(dates)]


def straight_kernel(dates, truth_ref, own_ref, _, out_ref, kept_ref):
    first = first_core()
    blocks = []
    for entries in tile_entries(truth_ref.shape[0] // dates, dates):
        one, two = by_owner(truth_ref, entries, jnp.logical_not(lower_chip()))
        blocks.append(jnp.where(first, one, two))
    pack_rows(blocks, out_ref)
    for index in range(own_ref.shape[0]):
        kept_ref[index] = own_ref[index]


def home_kernel(dates, truth_ref, normal_ref, _, crossed_ref, mine_ref, sibling_ref, normals_ref):
    pairs = normal_ref.shape[0]
    first = first_core()
    lower = lower_chip()
    crossed = []
    for at, entries in enumerate(tile_entries(pairs, dates)):
        one, two = by_owner(truth_ref, entries, jnp.logical_not(lower))
        crossed.append(jnp.where(first, two, one))
        one, two = by_owner(truth_ref, entries, lower)
        mine_ref[at] = jnp.where(first, one, two).astype(mine_ref.dtype)
        sibling_ref[at] = jnp.where(first, two, one).astype(sibling_ref.dtype)
    pack_rows(crossed, crossed_ref)
    for pair in range(0, pairs, 2):
        one, two = by_owner(normal_ref, [pair, pair + 1], lower)
        normals_ref[pair // 2] = jnp.where(first, one, two)


def shift_rows_kernel(own_ref, peer_ref, both_ref, rows_ref):
    lower = lower_chip()
    fields, coarse_rows, _ = own_ref.shape
    for index in range(2 * fields):
        block = (own_ref if index < fields else peer_ref)[index % fields]
        both_ref[index] = block
        block = block.astype(jnp.float32)
        rows_ref[index] = jnp.where(lower, block[coarse_rows - 2 :], block[:2]).astype(jnp.bfloat16)


def latitude_step(dates, coarse_ref, halo_ref, lat_ref, lhs_ref):
    fields = coarse_ref.shape[0] // 2
    pairs = fields // dates
    depth = lhs_ref.shape[2]
    rows = 2 * lhs_ref.shape[1] // (2 * fields)
    owned = rows // 2
    band = lax.axis_index("band")
    lower = lower_chip()
    first = first_core()
    outside = jnp.logical_or(
        jnp.logical_and(lower, band == 0),
        jnp.logical_and(jnp.logical_not(lower), band == lax.axis_size("band") - 1),
    )
    weights = lat_ref[...].T
    weights = jnp.where(lower, weights[: 2 * owned], weights[2 * owned : 4 * owned])
    weights = jnp.where(first, weights[:owned], weights[owned:])
    weights = jnp.concatenate([weights, weights], axis=0)
    lat = [jnp.broadcast_to(weights[:, tap : tap + 1], (rows, depth)) for tap in range(TAPS + 1)]
    first_pair = lax.broadcasted_iota(jnp.int32, (rows, depth), 0) < owned
    pending = []
    at = 0
    for side in range(2):
        for entries in tile_entries(pairs, dates):
            sources = []
            for entry in entries:
                index = side * fields + entry
                inner = coarse_ref[index].astype(jnp.float32)
                edge = jnp.where(outside, 0.0, halo_ref[index].astype(jnp.float32))
                below = jnp.concatenate([edge, inner], axis=0)
                above = jnp.concatenate([inner, edge], axis=0)
                wrapped = wrapped_rows(jnp.where(lower, below, above), depth)
                sources.append(jnp.where(first, wrapped[: TAPS + 1], wrapped[1 : TAPS + 2]))
            total = 0.0
            for tap in range(TAPS + 1):
                one, two = [jnp.broadcast_to(source[tap : tap + 1], (rows, depth)) for source in sources]
                total = total + lat[tap] * jnp.where(first_pair, one, two)
            pending.append(total)
            at += rows
            if len(pending) * rows == 16:
                block = jnp.concatenate(pending, axis=0)
                upper = block.astype(jnp.bfloat16)
                lhs_ref[0, at - 16 : at] = upper
                lhs_ref[1, at - 16 : at] = (block - upper.astype(jnp.float32)).astype(jnp.bfloat16)
                pending = []


def column_blocks(dense):
    for tile in range(pl.cdiv(dense, WIDE)):
        low_x = tile * WIDE
        width = min(WIDE, dense - low_x)
        yield tile, low_x, width, slice(low_x, low_x + width)


def added(sums, fine, actual, normal):
    error = fine - actual
    return sums[0] + error * error, sums[1] + (fine - normal) * (actual - normal)


def own_dates_kernel(
    coarse_ref,
    halo_ref,
    truth_ref,
    normals_ref,
    lat_ref,
    table_ref,
    sums_ref,
    away_ref,
    lhs_ref,
    fine_ref,
):
    tiles, rows, dense = truth_ref.shape
    dates = tiles // normals_ref.shape[0]
    latitude_step(dates, coarse_ref, halo_ref, lat_ref, lhs_ref)
    for tile, low_x, width, columns in column_blocks(dense):
        fine_ref[:, :width] = widened(lhs_ref, table_ref, tile, low_x, width)
        away_ref[:, columns] = fine_ref[tiles * rows :, :width]
        for pair in range(normals_ref.shape[0]):
            normal = normals_ref[pair, :, columns]
            sums = (0.0, 0.0)
            for at in range(pair * dates, (pair + 1) * dates):
                actual = truth_ref[at, :, columns].astype(jnp.float32)
                sums = added(sums, fine_ref[at * rows : (at + 1) * rows, :width], actual, normal)
            sums_ref[0, pair, :, columns], sums_ref[1, pair, :, columns] = sums


def sibling_dates_kernel(
    coarse_ref,
    halo_ref,
    truth_ref,
    normals_ref,
    lat_ref,
    table_ref,
    before_ref,
    straight_fine_ref,
    straight_ref,
    sums_ref,
    away_ref,
    lhs_ref,
    fine_ref,
):
    tiles, rows, dense = truth_ref.shape
    dates = tiles // normals_ref.shape[0]
    latitude_step(dates, coarse_ref, halo_ref, lat_ref, lhs_ref)
    for tile, low_x, width, columns in column_blocks(dense):
        fine_ref[:, :width] = widened(lhs_ref, table_ref, tile, low_x, width)
        away_ref[:, columns] = fine_ref[tiles * rows :, :width]
        for pair in range(normals_ref.shape[0]):
            normal = normals_ref[pair, :, columns]
            sums = (before_ref[0, pair, :, columns], before_ref[1, pair, :, columns])
            for at in range(pair * dates, (pair + 1) * dates):
                span = slice(at * rows, (at + 1) * rows)
                actual = truth_ref[at, :, columns].astype(jnp.float32)
                sums = added(sums, fine_ref[span, :width], actual, normal)
                actual = unpacked_rows(straight_ref, at, tiles, dense, low_x, width)
                sums = added(sums, straight_fine_ref[span, columns], actual, normal)
            sums_ref[0, pair, :, columns], sums_ref[1, pair, :, columns] = sums


def mean_kernel(dates, count, before_ref, fine_ref, crossed_ref, normals_ref, *refs):
    *results, held_ref, sems = refs
    tiles, rows, dense = normals_ref.shape
    owned = rows // 2
    copies = []
    for pair in range(tiles):
        for _, low_x, width, columns in column_blocks(dense):
            normal = normals_ref[pair, :, columns]
            sums = (before_ref[0, pair, :, columns], before_ref[1, pair, :, columns])
            for at in range(pair * dates, (pair + 1) * dates):
                actual = unpacked_rows(crossed_ref, at, tiles * dates, dense, low_x, width)
                sums = added(sums, fine_ref[at * rows : (at + 1) * rows, columns], actual, normal)
            for kind, total in enumerate(sums):
                total = total * (1.0 / count)
                held_ref[kind, 2 * pair, :, columns] = total[:owned]
                held_ref[kind, 2 * pair + 1, :, columns] = total[owned:]
        done = pl.ds(2 * pair, 2)
        for kind, out_ref in enumerate(results):
            copy = pltpu.make_async_copy(held_ref.at[kind, done], out_ref.at[done], sems.at[len(copies)])
            copy.start()
            copies.append(copy)
    for copy in copies:
        copy.wait()


def kernel_call(kernel, out_shape, scratch, megabytes, flops, *operands, out_space=pltpu.VMEM):
    vmem = pl.BlockSpec(memory_space=pltpu.VMEM)
    return pl.pallas_call(
        kernel,
        out_shape=out_shape,
        in_specs=[vmem] * len(operands),
        out_specs=[pl.BlockSpec(memory_space=out_space)] * len(out_shape),
        scratch_shapes=scratch,
        compiler_params=pltpu.CompilerParams(vmem_limit_bytes=megabytes * 1024 * 1024),
        cost_estimate=pl.CostEstimate(flops=flops, bytes_accessed=0, transcendentals=0),
    )(*operands)


def two_chip_maps(model_prognosis, analysis_truth, expected_normal, taps, lon_weights, lat_weights):
    bands = lax.axis_size("band")
    groups = lax.axis_size("date")
    dates, leads, variables, coarse_rows, sparse = model_prognosis.shape
    fine_rows, dense = analysis_truth.shape[3:]
    owned = fine_rows // groups
    rows = 2 * owned
    pairs = leads * variables
    fields = dates * pairs
    tiles = fields // 2
    depth = pl.cdiv(sparse + 4, LANES) * LANES
    float32, bfloat16 = jnp.float32, jnp.bfloat16
    straight_way = [(i, (i + 2) % groups) for i in range(groups)]
    crossed_way = [(i, (i + 2) % groups ^ 1) for i in range(groups)]
    sibling_way = [(i, i ^ 1) for i in range(groups)]

    own = model_prognosis.reshape(fields, coarse_rows, sparse)
    truth = analysis_truth.reshape(fields, fine_rows, dense)
    normal = expected_normal.reshape(pairs, fine_rows, dense)
    peer = lax.ppermute(model_prognosis, "date", straight_way).reshape(own.shape)

    packed = jax.ShapeDtypeStruct((packed_tiles(tiles, dense), rows, LANES), bfloat16)
    straight, own = kernel_call(
        functools.partial(straight_kernel, dates),
        [packed, jax.ShapeDtypeStruct(own.shape, own.dtype)],
        [],
        8,
        100_000_000,
        truth,
        own,
        taps,
    )
    straight = lax.ppermute(straight, "date", straight_way)
    plain = jax.ShapeDtypeStruct((tiles, rows, dense), bfloat16)
    crossed, mine, sibling, normals = kernel_call(
        functools.partial(home_kernel, dates),
        [packed, plain, plain, jax.ShapeDtypeStruct((pairs // 2, rows, dense), float32)],
        [],
        12,
        100_000_000,
        truth,
        normal,
        own,
    )
    crossed = lax.ppermute(crossed, "date", crossed_way)
    sibling = lax.ppermute(sibling, "date", sibling_way)

    chain = []
    for group in range(groups):
        for band in range(bands):
            to = band + (1 if group < groups // 2 else -1)
            if 0 <= to < bands:
                chain.append((group * bands + band, group * bands + to))
    coarse, edges = kernel_call(
        shift_rows_kernel,
        [
            jax.ShapeDtypeStruct((2 * fields, coarse_rows, sparse), bfloat16),
            jax.ShapeDtypeStruct((2 * fields, 2, sparse), bfloat16),
        ],
        [],
        8,
        100_000_000,
        own,
        peer,
    )
    halo = lax.ppermute(edges, ("date", "band"), chain)
    sibling_coarse = lax.ppermute(coarse, "date", sibling_way)
    sibling_halo = lax.ppermute(halo, "date", sibling_way)

    sums = jax.ShapeDtypeStruct((2, pairs // 2, rows, dense), float32)
    away = jax.ShapeDtypeStruct((tiles * rows, dense), float32)
    table = jax.ShapeDtypeStruct((pl.cdiv(dense, WIDE), 2 * LANES, WIDE), bfloat16)
    scratch = [
        pltpu.VMEM((2, 2 * tiles * rows, depth), bfloat16),
        pltpu.VMEM((2 * tiles * rows, WIDE), float32),
    ]
    (table,) = kernel_call(fill_tables, [table], [], 8, 4_000_000_000, taps, lon_weights)
    own_sums, straight_fine = kernel_call(
        own_dates_kernel,
        [sums, away],
        scratch,
        20,
        0,
        coarse,
        halo,
        mine,
        normals,
        lat_weights,
        table,
    )
    chip_sums, crossed_fine = kernel_call(
        sibling_dates_kernel,
        [sums, away],
        scratch,
        20,
        0,
        sibling_coarse,
        sibling_halo,
        sibling,
        normals,
        lat_weights,
        table,
        own_sums,
        straight_fine,
        straight,
    )
    out = jax.ShapeDtypeStruct((pairs, owned, dense), float32)
    results = kernel_call(
        functools.partial(mean_kernel, dates, dates * groups),
        [out, out],
        [pltpu.VMEM((2,) + out.shape, float32), pltpu.SemaphoreType.DMA((pairs,))],
        16,
        0,
        chip_sums,
        crossed_fine,
        crossed,
        normals,
        out_space=pl.ANY,
    )
    return tuple(result.reshape(leads, variables, owned, dense) for result in results)


def shards(
    model_prognosis,
    analysis_truth,
    expected_normal,
    parallel_first_indices,
    parallel_blend_factors,
    meridian_first_indices,
    meridian_blend_factors,
):
    bands = lax.axis_size("band")
    groups = lax.axis_size("date")
    halves = groups // 2
    dates = model_prognosis.shape[0]
    group = lax.axis_index("date")
    core = lax.rem(group, 2)
    half = lax.div(group, 2)

    coarse_rows = model_prognosis.shape[3]
    lat_weights = lat_tap_weights(
        parallel_first_indices,
        parallel_blend_factors,
        lax.axis_index("band") * coarse_rows,
        analysis_truth.shape[3] // coarse_rows,
    )
    dense = meridian_first_indices.shape[0]
    late = meridian_first_indices == lax.iota(jnp.int32, dense) // 4
    lon_weights = jnp.where(
        lax.broadcasted_iota(jnp.int32, (8, dense), 0) < TAPS,
        jnp.pad(meridian_blend_factors, ((0, 8 - TAPS), (0, 0))).astype(jnp.float32),
        late.astype(jnp.float32)[None],
    )
    (taps,) = kernel_call(
        taps_kernel, [jax.ShapeDtypeStruct((WIDE // 4 + 8, WIDE), jnp.int32)], [], 8, 2_000_000_000
    )
    tall = 2 * analysis_truth.shape[3] == 8 * groups
    if halves == 2 and tall and expected_normal.shape[0] * expected_normal.shape[1] % 2 == 0:
        return two_chip_maps(model_prognosis, analysis_truth, expected_normal, taps, lon_weights, lat_weights)

    own = model_prognosis.reshape((-1,) + model_prognosis.shape[3:])
    own, to_cross, to_pair = edge_rows(own)
    across = [(i, min(max(i + (1 if i % 2 else -1), 0), bands - 1)) for i in range(bands)]
    paired = lax.ppermute(to_pair, "band", [(i, i ^ 1) for i in range(bands)])
    crossed = lax.ppermute(to_cross, "band", across)
    truth = analysis_truth.reshape((-1,) + analysis_truth.shape[3:])
    normal = expected_normal.reshape((-1,) + expected_normal.shape[2:])
    error, fine = error_map(own, crossed, paired, truth, taps, lon_weights, lat_weights, normal.shape[0], groups)
    anomaly = anomaly_map(fine, truth, normal, groups)

    def packed(values):
        return (values * CARRY_SCALE).astype(jnp.float16)

    def unpacked(values):
        return values.astype(jnp.float32) / CARRY_SCALE

    def row_block(values, index):
        return lax.dynamic_index_in_dim(values, index, 0, keepdims=False)

    def mean_over_dates(maps):
        swapped = lax.ppermute(packed(row_block(maps, 1 - core)), "date", [(i, i ^ 1) for i in range(groups)])

        def chip_sum(index):
            mine = lax.dynamic_slice(maps, (core, index, 0, 0, 0), (1, 1) + maps.shape[2:])[0, 0]
            return mine + unpacked(row_block(swapped, index))

        pieces = []
        for step in range(1, halves):
            piece = packed(chip_sum(lax.rem(half + step, halves)))
            ring = [(i, (i + 2 * step) % groups) for i in range(groups)]
            pieces.append(lax.ppermute(piece, "date", ring))
        total = chip_sum(half)
        for piece in pieces:
            total = total + unpacked(piece)
        total = total / (dates * groups)
        return total.reshape(expected_normal.shape[:2] + total.shape[1:])

    return (mean_over_dates(error), mean_over_dates(anomaly))


def solution(mesh):
    in_specs = (
        P("date", None, None, "band", None),
        P("date", None, None, "band", None),
        P(None, None, "band", None),
        P("band"),
        P("band", None),
        P(),
        P(),
    )
    out_specs = (P(None, None, ("band", "date"), None), P(None, None, ("band", "date"), None))
    return jax.shard_map(shards, mesh=mesh, in_specs=in_specs, out_specs=out_specs, check_vma=False)
```

```python
import functools

import jax
import jax.numpy as jnp
from jax import lax
from jax.experimental import pallas as pl
from jax.experimental.pallas import tpu as pltpu
from jax.sharding import PartitionSpec as P

TAPS = 4
LANES = 128
WIDE = 256
CARRY_SCALE = 16.0


def edges_kernel(own_ref, kept_ref, cross_ref, pair_ref):
    even = lax.rem(lax.axis_index("band"), 2) == 0
    for index in range(own_ref.shape[0]):
        kept_ref[index] = own_ref[index]
        rows = own_ref[index].astype(jnp.float32)
        bottom, top = rows[:2], rows[rows.shape[0] - 2 :]
        pair_ref[index] = jnp.where(even, top, bottom).astype(jnp.bfloat16)
        cross_ref[index] = jnp.where(even, bottom, top).astype(jnp.bfloat16)


def taps_kernel(tap_ref):
    row = lax.broadcasted_iota(jnp.int32, tap_ref.shape, 0)
    tap_ref[...] = row - lax.broadcasted_iota(jnp.int32, tap_ref.shape, 1) // 4


def fill_tables(tap_ref, lon_ref, table_ref):
    dense = lon_ref.shape[1]
    for tile in range(pl.cdiv(dense, WIDE)):
        low_x = tile * WIDE
        width = min(WIDE, dense - low_x)
        base = low_x // 4 % LANES
        rows = width // 4 + 8
        depth_here = LANES if base + rows <= LANES else 2 * LANES
        columns = slice(low_x, low_x + width)
        offset = tap_ref[:rows, :width] - lon_ref[TAPS : TAPS + 1, columns].astype(jnp.int32)
        block = jnp.zeros((rows, width), jnp.float32)
        for tap in range(TAPS):
            block = jnp.where(offset == tap, lon_ref[tap : tap + 1, columns], block)
        parts = [block]
        if base:
            parts.insert(0, jnp.zeros((base, width), jnp.float32))
        if depth_here > base + rows:
            parts.append(jnp.zeros((depth_here - base - rows, width), jnp.float32))
        table_ref[tile, :depth_here, :width] = jnp.concatenate(parts, axis=0).astype(jnp.bfloat16)


def widened(lhs_ref, table_ref, tile, low_x, width):
    base = low_x // 4 % LANES
    begin = low_x // 4 - base
    depth = LANES if base + width // 4 + 8 <= LANES else 2 * LANES
    lhs = jnp.concatenate([lhs_ref[0, :, begin : begin + depth], lhs_ref[1, :, begin : begin + depth]], axis=1)
    table = table_ref[tile, :depth, :width]
    return jnp.dot(lhs, jnp.concatenate([table, table], axis=0), preferred_element_type=jnp.float32)


def wrapped_rows(rows, depth):
    sparse = rows.shape[1]
    filler = jnp.zeros((rows.shape[0], depth - sparse - 4), jnp.float32)
    return jnp.concatenate([rows[:, sparse - 1 :], rows, rows[:, :3], filler], axis=1)


def error_kernel(
    own_ref,
    cross_ref,
    pair_ref,
    truth_ref,
    tap_ref,
    lon_ref,
    lat_ref,
    out_ref,
    fine_ref,
    lhs_ref,
    table_ref,
):
    fields, coarse_rows, sparse = own_ref.shape
    _, fine_rows, dense = truth_ref.shape
    pairs = out_ref.shape[2]
    dates = fields // pairs
    ratio = fine_rows // coarse_rows
    span = 8 // ratio
    depth = lhs_ref.shape[2]
    tiles = pl.cdiv(dense, WIDE)
    band = lax.axis_index("band")
    even = lax.rem(band, 2) == 0
    lowest = band == 0
    highest = band == lax.axis_size("band") - 1

    fill_tables(tap_ref, lon_ref, table_ref)

    weights = lat_ref[...].T
    lat = [
        [
            jnp.broadcast_to(weights[8 * group : 8 * group + 8, tap : tap + 1], (8, LANES))
            for tap in range(TAPS + 1)
        ]
        for group in range(fine_rows // 8)
    ]
    lat = [[jnp.concatenate([w] * (depth // LANES), axis=1) for w in group] for group in lat]

    upper_half = lax.broadcasted_iota(jnp.int32, (8, depth), 0) < ratio
    for pair in range(pairs):
        for date in range(dates):
            index = date * pairs + pair
            paired = pair_ref[index].astype(jnp.float32)
            crossed = cross_ref[index].astype(jnp.float32)
            low = jnp.where(lowest, 0.0, jnp.where(even, crossed, paired))
            high = jnp.where(highest, 0.0, jnp.where(even, paired, crossed))
            rows8 = jnp.concatenate([low, own_ref[index].astype(jnp.float32), high], axis=0)
            wrapped = wrapped_rows(rows8, depth)
            spread = [jnp.broadcast_to(wrapped[i : i + 1], (8, depth)) for i in range(coarse_rows + 4)]
            mixed = [jnp.where(upper_half, spread[i], spread[i + 1]) for i in range(coarse_rows + 3)]
            both = []
            for group in range(fine_rows // 8):
                total = lat[group][0] * mixed[span * group]
                for tap in range(1, TAPS + 1):
                    total = total + lat[group][tap] * mixed[span * group + tap]
                both.append(total)
            both = jnp.concatenate(both, axis=0)
            upper = both.astype(jnp.bfloat16)
            rest = (both - upper.astype(jnp.float32)).astype(jnp.bfloat16)
            at = (pair * dates + date) * fine_rows
            lhs_ref[0, at : at + fine_rows, :] = upper
            lhs_ref[1, at : at + fine_rows, :] = rest

    for tile in range(tiles):
        low_x = tile * WIDE
        width = min(WIDE, dense - low_x)
        columns = slice(low_x, low_x + width)
        fine_ref[:, columns] = widened(lhs_ref, table_ref, tile, low_x, width)
        for pair in range(pairs):
            total = 0.0
            for date in range(dates):
                at = (pair * dates + date) * fine_rows
                actual = truth_ref[date * pairs + pair, :, columns].astype(jnp.float32)
                error = fine_ref[at : at + fine_rows, columns] - actual
                total = total + error * error
            store_by_owner(out_ref, pair, columns, total)


def store_by_owner(out_ref, pair, columns, values):
    _, halves, _, owned, _ = out_ref.shape
    for owner in range(2 * halves):
        out_ref[owner % 2, owner // 2, pair, :, columns] = values[owner * owned : (owner + 1) * owned]


def anomaly_kernel(fine_ref, truth_ref, normal_ref, out_ref):
    fields, fine_rows, dense = truth_ref.shape
    pairs = normal_ref.shape[0]
    dates = fields // pairs
    for low_x in range(0, dense, WIDE):
        columns = slice(low_x, min(low_x + WIDE, dense))
        for pair in range(pairs):
            normal = normal_ref[pair, :, columns].astype(jnp.float32)
            total = 0.0
            for date in range(dates):
                at = (pair * dates + date) * fine_rows
                actual = truth_ref[date * pairs + pair, :, columns].astype(jnp.float32)
                total = total + (fine_ref[at : at + fine_rows, columns] - normal) * (actual - normal)
            store_by_owner(out_ref, pair, columns, total)


def edge_rows(own):
    fields, _, sparse = own.shape
    vmem = pl.BlockSpec(memory_space=pltpu.VMEM)
    edges = jax.ShapeDtypeStruct((fields, 2, sparse), jnp.bfloat16)
    return pl.pallas_call(
        edges_kernel,
        out_shape=[jax.ShapeDtypeStruct(own.shape, own.dtype), edges, edges],
        in_specs=[vmem],
        out_specs=[vmem] * 3,
        compiler_params=pltpu.CompilerParams(vmem_limit_bytes=8 * 1024 * 1024),
        cost_estimate=pl.CostEstimate(flops=100_000_000, bytes_accessed=200_000, transcendentals=0),
    )(own)


def lat_tap_weights(starts, weights, first_coarse, ratio):
    rows = starts.shape[0]
    late = starts > first_coarse + lax.iota(jnp.int32, rows) // ratio - 2
    by_tap = weights.T
    early = jnp.pad(by_tap, ((0, 8 - TAPS), (0, LANES - rows)))
    shifted = jnp.pad(by_tap, ((1, 7 - TAPS), (0, LANES - rows)))
    return jnp.where(jnp.pad(late, (0, LANES - rows))[None], shifted, early)


def error_map(own, crossed, paired, truth, taps, lon, lat, pairs, owners):
    fields, _, sparse = own.shape
    _, fine_rows, dense = truth.shape
    depth = pl.cdiv(sparse + 4, LANES) * LANES
    vmem = pl.BlockSpec(memory_space=pltpu.VMEM)
    return pl.pallas_call(
        error_kernel,
        out_shape=[
            jax.ShapeDtypeStruct((2, owners // 2, pairs, fine_rows // owners, dense), jnp.float32),
            jax.ShapeDtypeStruct((fields * fine_rows, dense), jnp.float32),
        ],
        in_specs=[vmem] * 7,
        out_specs=[vmem] * 2,
        scratch_shapes=[
            pltpu.VMEM((2, fields * fine_rows, depth), jnp.bfloat16),
            pltpu.VMEM((pl.cdiv(dense, WIDE), 2 * LANES, WIDE), jnp.bfloat16),
        ],
        compiler_params=pltpu.CompilerParams(vmem_limit_bytes=24 * 1024 * 1024),
        cost_estimate=pl.CostEstimate(flops=1_000_000_000, bytes_accessed=4_000_000, transcendentals=0),
    )(own, crossed, paired, truth, taps, lon, lat)


def anomaly_map(fine, truth, normal, owners):
    pairs, fine_rows, dense = normal.shape
    vmem = pl.BlockSpec(memory_space=pltpu.VMEM)
    return pl.pallas_call(
        anomaly_kernel,
        out_shape=jax.ShapeDtypeStruct((2, owners // 2, pairs, fine_rows // owners, dense), jnp.float32),
        in_specs=[vmem] * 3,
        out_specs=vmem,
        compiler_params=pltpu.CompilerParams(vmem_limit_bytes=24 * 1024 * 1024),
        cost_estimate=pl.CostEstimate(flops=500_000_000, bytes_accessed=4_000_000, transcendentals=0),
    )(fine, truth, normal)


def first_core():
    return lax.rem(lax.axis_index("date"), 2) == 0


def lower_chip():
    return lax.axis_index("date") < lax.axis_size("date") // 2


def by_owner(ref, entries, lower):
    blocks = [ref[entry].astype(jnp.float32) for entry in entries]
    half = blocks[0].shape[0] // 2
    blocks = [jnp.where(lower, block[:half], block[half:]) for block in blocks]
    owned = half // 2
    return (
        jnp.concatenate([block[:owned] for block in blocks], axis=0),
        jnp.concatenate([block[owned:] for block in blocks], axis=0),
    )


def packed_tiles(entries, dense):
    full, tail = divmod(dense, LANES)
    return entries * full + (pl.cdiv(entries, LANES // tail) if tail else 0)


def pack_rows(blocks, out_ref):
    rows, dense = blocks[0].shape
    full, tail = divmod(dense, LANES)
    for at, block in enumerate(blocks):
        for tile in range(full):
            out_ref[at * full + tile] = block[:, tile * LANES : (tile + 1) * LANES].astype(out_ref.dtype)
    if tail:
        share = LANES // tail
        tails = [block[:, full * LANES :] for block in blocks]
        tails += [jnp.zeros((rows, tail), jnp.float32)] * (-len(tails) % share)
        filler = [jnp.zeros((rows, LANES - share * tail), jnp.float32)] if LANES % tail else []
        for at in range(0, len(tails), share):
            joined = jnp.concatenate(tails[at : at + share] + filler, axis=1)
            out_ref[len(blocks) * full + at // share] = joined.astype(out_ref.dtype)


def unpacked_rows(ref, at, entries, dense, low_x, width):
    full, tail = divmod(dense, LANES)
    parts = [
        ref[at * full + tile].astype(jnp.float32)
        for tile in range(low_x // LANES, min((low_x + width) // LANES, full))
    ]
    if low_x + width > full * LANES:
        share = LANES // tail
        start = at % share * tail
        parts.append(ref[entries * full + at // share].astype(jnp.float32)[:, start : start + tail])
    return jnp.concatenate(parts, axis=1)


def tile_entries(pairs, dates):
    return [[date * pairs + pair, date * pairs + pair + 1] for pair in range(0, pairs, 2) for date in range(dates)]


def away_kernel(dates, truth_ref, own_ref, _, straight_ref, crossed_ref, kept_ref):
    first = first_core()
    straight, crossed = [], []
    for entries in tile_entries(truth_ref.shape[0] // dates, dates):
        one, two = by_owner(truth_ref, entries, jnp.logical_not(lower_chip()))
        straight.append(jnp.where(first, one, two))
        crossed.append(jnp.where(first, two, one))
    pack_rows(straight, straight_ref)
    pack_rows(crossed, crossed_ref)
    for index in range(own_ref.shape[0]):
        kept_ref[index] = own_ref[index]


def home_kernel(dates, truth_ref, normal_ref, mine_ref, sibling_ref, normals_ref):
    pairs = normal_ref.shape[0]
    first = first_core()
    lower = lower_chip()
    for at, entries in enumerate(tile_entries(pairs, dates)):
        one, two = by_owner(truth_ref, entries, lower)
        mine_ref[at] = jnp.where(first, one, two).astype(mine_ref.dtype)
        sibling_ref[at] = jnp.where(first, two, one).astype(sibling_ref.dtype)
    for pair in range(0, pairs, 2):
        one, two = by_owner(normal_ref, [pair, pair + 1], lower)
        normals_ref[pair // 2] = jnp.where(first, one, two)


def shift_rows_kernel(own_ref, peer_ref, both_ref, rows_ref):
    lower = lower_chip()
    fields, coarse_rows, _ = own_ref.shape
    for index in range(2 * fields):
        block = (own_ref if index < fields else peer_ref)[index % fields]
        both_ref[index] = block
        block = block.astype(jnp.float32)
        rows_ref[index] = jnp.where(lower, block[coarse_rows - 2 :], block[:2]).astype(jnp.bfloat16)


def latitude_step(dates, coarse_ref, halo_ref, lat_ref, lhs_ref):
    fields = coarse_ref.shape[0] // 2
    pairs = fields // dates
    depth = lhs_ref.shape[2]
    rows = 2 * lhs_ref.shape[1] // (2 * fields)
    owned = rows // 2
    band = lax.axis_index("band")
    lower = lower_chip()
    first = first_core()
    outside = jnp.logical_or(
        jnp.logical_and(lower, band == 0),
        jnp.logical_and(jnp.logical_not(lower), band == lax.axis_size("band") - 1),
    )
    weights = lat_ref[...].T
    weights = jnp.where(lower, weights[: 2 * owned], weights[2 * owned : 4 * owned])
    weights = jnp.where(first, weights[:owned], weights[owned:])
    weights = jnp.concatenate([weights, weights], axis=0)
    lat = [jnp.broadcast_to(weights[:, tap : tap + 1], (rows, depth)) for tap in range(TAPS + 1)]
    first_pair = lax.broadcasted_iota(jnp.int32, (rows, depth), 0) < owned
    pending = []
    at = 0
    for side in range(2):
        for entries in tile_entries(pairs, dates):
            sources = []
            for entry in entries:
                index = side * fields + entry
                inner = coarse_ref[index].astype(jnp.float32)
                edge = jnp.where(outside, 0.0, halo_ref[index].astype(jnp.float32))
                below = jnp.concatenate([edge, inner], axis=0)
                above = jnp.concatenate([inner, edge], axis=0)
                wrapped = wrapped_rows(jnp.where(lower, below, above), depth)
                sources.append(jnp.where(first, wrapped[: TAPS + 1], wrapped[1 : TAPS + 2]))
            total = 0.0
            for tap in range(TAPS + 1):
                one, two = [jnp.broadcast_to(source[tap : tap + 1], (rows, depth)) for source in sources]
                total = total + lat[tap] * jnp.where(first_pair, one, two)
            pending.append(total)
            at += rows
            if len(pending) * rows == 16:
                block = jnp.concatenate(pending, axis=0)
                upper = block.astype(jnp.bfloat16)
                lhs_ref[0, at - 16 : at] = upper
                lhs_ref[1, at - 16 : at] = (block - upper.astype(jnp.float32)).astype(jnp.bfloat16)
                pending = []


def column_blocks(dense):
    for tile in range(pl.cdiv(dense, WIDE)):
        low_x = tile * WIDE
        width = min(WIDE, dense - low_x)
        yield tile, low_x, width, slice(low_x, low_x + width)


def added(sums, fine, actual, normal):
    error = fine - actual
    return sums[0] + error * error, sums[1] + (fine - normal) * (actual - normal)


def own_dates_kernel(
    coarse_ref,
    halo_ref,
    truth_ref,
    normals_ref,
    lat_ref,
    table_ref,
    sums_ref,
    away_ref,
    lhs_ref,
    fine_ref,
):
    tiles, rows, dense = truth_ref.shape
    dates = tiles // normals_ref.shape[0]
    latitude_step(dates, coarse_ref, halo_ref, lat_ref, lhs_ref)
    for tile, low_x, width, columns in column_blocks(dense):
        fine_ref[:, :width] = widened(lhs_ref, table_ref, tile, low_x, width)
        away_ref[:, columns] = fine_ref[tiles * rows :, :width]
        for pair in range(normals_ref.shape[0]):
            normal = normals_ref[pair, :, columns]
            sums = (0.0, 0.0)
            for at in range(pair * dates, (pair + 1) * dates):
                actual = truth_ref[at, :, columns].astype(jnp.float32)
                sums = added(sums, fine_ref[at * rows : (at + 1) * rows, :width], actual, normal)
            sums_ref[0, pair, :, columns], sums_ref[1, pair, :, columns] = sums


def sibling_dates_kernel(
    coarse_ref,
    halo_ref,
    truth_ref,
    normals_ref,
    lat_ref,
    table_ref,
    before_ref,
    straight_fine_ref,
    straight_ref,
    sums_ref,
    away_ref,
    lhs_ref,
    fine_ref,
):
    tiles, rows, dense = truth_ref.shape
    dates = tiles // normals_ref.shape[0]
    latitude_step(dates, coarse_ref, halo_ref, lat_ref, lhs_ref)
    for tile, low_x, width, columns in column_blocks(dense):
        fine_ref[:, :width] = widened(lhs_ref, table_ref, tile, low_x, width)
        away_ref[:, columns] = fine_ref[tiles * rows :, :width]
        for pair in range(normals_ref.shape[0]):
            normal = normals_ref[pair, :, columns]
            sums = (before_ref[0, pair, :, columns], before_ref[1, pair, :, columns])
            for at in range(pair * dates, (pair + 1) * dates):
                span = slice(at * rows, (at + 1) * rows)
                actual = truth_ref[at, :, columns].astype(jnp.float32)
                sums = added(sums, fine_ref[span, :width], actual, normal)
                actual = unpacked_rows(straight_ref, at, tiles, dense, low_x, width)
                sums = added(sums, straight_fine_ref[span, columns], actual, normal)
            sums_ref[0, pair, :, columns], sums_ref[1, pair, :, columns] = sums


def mean_kernel(dates, count, before_ref, fine_ref, crossed_ref, normals_ref, *refs):
    *results, held_ref, sems = refs
    tiles, rows, dense = normals_ref.shape
    owned = rows // 2
    full = dense // LANES

    def add_columns(pair, columns, actuals):
        normal = normals_ref[pair, :, columns]
        sums = (before_ref[0, pair, :, columns], before_ref[1, pair, :, columns])
        for date, actual in enumerate(actuals):
            at = (pair * dates + date) * rows
            at = at if isinstance(at, int) else pl.multiple_of(at, rows)
            sums = added(sums, fine_ref[pl.ds(at, rows), columns], actual, normal)
        for kind, total in enumerate(sums):
            total = total * (1.0 / count)
            held_ref[kind, 2 * pair, :, columns] = total[:owned]
            held_ref[kind, 2 * pair + 1, :, columns] = total[owned:]

    def whole_tiles(pair, carry):
        for tile in range(full):
            actuals = [
                crossed_ref[(pair * dates + date) * full + tile].astype(jnp.float32) for date in range(dates)
            ]
            add_columns(pair, slice(tile * LANES, (tile + 1) * LANES), actuals)
        return carry

    lax.fori_loop(0, tiles, whole_tiles, 0)
    if dense % LANES:
        low_x = full * LANES
        for pair in range(tiles):
            actuals = [
                unpacked_rows(crossed_ref, pair * dates + date, tiles * dates, dense, low_x, dense - low_x)
                for date in range(dates)
            ]
            add_columns(pair, slice(low_x, dense), actuals)
    copies = [
        pltpu.make_async_copy(held_ref.at[kind], out_ref, sems.at[kind]) for kind, out_ref in enumerate(results)
    ]
    for copy in copies:
        copy.start()
    for copy in copies:
        copy.wait()


def kernel_call(kernel, out_shape, scratch, megabytes, flops, *operands, out_space=pltpu.VMEM):
    vmem = pl.BlockSpec(memory_space=pltpu.VMEM)
    return pl.pallas_call(
        kernel,
        out_shape=out_shape,
        in_specs=[vmem] * len(operands),
        out_specs=[pl.BlockSpec(memory_space=out_space)] * len(out_shape),
        scratch_shapes=scratch,
        compiler_params=pltpu.CompilerParams(vmem_limit_bytes=megabytes * 1024 * 1024),
        cost_estimate=pl.CostEstimate(flops=flops, bytes_accessed=0, transcendentals=0),
    )(*operands)


def two_chip_maps(model_prognosis, analysis_truth, expected_normal, taps, lon_weights, lat_weights):
    bands = lax.axis_size("band")
    groups = lax.axis_size("date")
    dates, leads, variables, coarse_rows, sparse = model_prognosis.shape
    fine_rows, dense = analysis_truth.shape[3:]
    owned = fine_rows // groups
    rows = 2 * owned
    pairs = leads * variables
    fields = dates * pairs
    tiles = fields // 2
    depth = pl.cdiv(sparse + 4, LANES) * LANES
    float32, bfloat16 = jnp.float32, jnp.bfloat16
    straight_way = [(i, (i + 2) % groups) for i in range(groups)]
    crossed_way = [(i, (i + 2) % groups ^ 1) for i in range(groups)]
    sibling_way = [(i, i ^ 1) for i in range(groups)]

    own = model_prognosis.reshape(fields, coarse_rows, sparse)
    truth = analysis_truth.reshape(fields, fine_rows, dense)
    normal = expected_normal.reshape(pairs, fine_rows, dense)
    peer = lax.ppermute(model_prognosis, "date", straight_way).reshape(own.shape)

    packed = jax.ShapeDtypeStruct((packed_tiles(tiles, dense), rows, LANES), bfloat16)
    straight, crossed, own = kernel_call(
        functools.partial(away_kernel, dates),
        [packed, packed, jax.ShapeDtypeStruct(own.shape, own.dtype)],
        [],
        8,
        100_000_000,
        truth,
        own,
        taps,
    )
    straight = lax.ppermute(straight, "date", straight_way)
    crossed = lax.ppermute(crossed, "date", crossed_way)
    plain = jax.ShapeDtypeStruct((tiles, rows, dense), bfloat16)
    mine, sibling, normals = kernel_call(
        functools.partial(home_kernel, dates),
        [plain, plain, jax.ShapeDtypeStruct((pairs // 2, rows, dense), float32)],
        [],
        12,
        100_000_000,
        truth,
        normal,
    )
    sibling = lax.ppermute(sibling, "date", sibling_way)

    chain = []
    for group in range(groups):
        for band in range(bands):
            to = band + (1 if group < groups // 2 else -1)
            if 0 <= to < bands:
                chain.append((group * bands + band, group * bands + to))
    coarse, edges = kernel_call(
        shift_rows_kernel,
        [
            jax.ShapeDtypeStruct((2 * fields, coarse_rows, sparse), bfloat16),
            jax.ShapeDtypeStruct((2 * fields, 2, sparse), bfloat16),
        ],
        [],
        8,
        100_000_000,
        own,
        peer,
    )
    halo = lax.ppermute(edges, ("date", "band"), chain)
    sibling_coarse = lax.ppermute(coarse, "date", sibling_way)
    sibling_halo = lax.ppermute(halo, "date", sibling_way)

    sums = jax.ShapeDtypeStruct((2, pairs // 2, rows, dense), float32)
    away = jax.ShapeDtypeStruct((tiles * rows, dense), float32)
    table = jax.ShapeDtypeStruct((pl.cdiv(dense, WIDE), 2 * LANES, WIDE), bfloat16)
    scratch = [
        pltpu.VMEM((2, 2 * tiles * rows, depth), bfloat16),
        pltpu.VMEM((2 * tiles * rows, WIDE), float32),
    ]
    (table,) = kernel_call(fill_tables, [table], [], 8, 4_000_000_000, taps, lon_weights)
    own_sums, straight_fine = kernel_call(
        own_dates_kernel,
        [sums, away],
        scratch,
        20,
        0,
        coarse,
        halo,
        mine,
        normals,
        lat_weights,
        table,
    )
    chip_sums, crossed_fine = kernel_call(
        sibling_dates_kernel,
        [sums, away],
        scratch,
        20,
        0,
        sibling_coarse,
        sibling_halo,
        sibling,
        normals,
        lat_weights,
        table,
        own_sums,
        straight_fine,
        straight,
    )
    out = jax.ShapeDtypeStruct((pairs, owned, dense), float32)
    results = kernel_call(
        functools.partial(mean_kernel, dates, dates * groups),
        [out, out],
        [pltpu.VMEM((2,) + out.shape, float32), pltpu.SemaphoreType.DMA((2,))],
        16,
        0,
        chip_sums,
        crossed_fine,
        crossed,
        normals,
        out_space=pl.ANY,
    )
    return tuple(result.reshape(leads, variables, owned, dense) for result in results)


def shards(
    model_prognosis,
    analysis_truth,
    expected_normal,
    parallel_first_indices,
    parallel_blend_factors,
    meridian_first_indices,
    meridian_blend_factors,
):
    bands = lax.axis_size("band")
    groups = lax.axis_size("date")
    halves = groups // 2
    dates = model_prognosis.shape[0]
    group = lax.axis_index("date")
    core = lax.rem(group, 2)
    half = lax.div(group, 2)

    coarse_rows = model_prognosis.shape[3]
    lat_weights = lat_tap_weights(
        parallel_first_indices,
        parallel_blend_factors,
        lax.axis_index("band") * coarse_rows,
        analysis_truth.shape[3] // coarse_rows,
    )
    dense = meridian_first_indices.shape[0]
    late = meridian_first_indices == lax.iota(jnp.int32, dense) // 4
    lon_weights = jnp.where(
        lax.broadcasted_iota(jnp.int32, (8, dense), 0) < TAPS,
        jnp.pad(meridian_blend_factors, ((0, 8 - TAPS), (0, 0))).astype(jnp.float32),
        late.astype(jnp.float32)[None],
    )
    (taps,) = kernel_call(
        taps_kernel, [jax.ShapeDtypeStruct((WIDE // 4 + 8, WIDE), jnp.int32)], [], 8, 2_000_000_000
    )
    tall = 2 * analysis_truth.shape[3] == 8 * groups
    if halves == 2 and tall and expected_normal.shape[0] * expected_normal.shape[1] % 2 == 0:
        return two_chip_maps(model_prognosis, analysis_truth, expected_normal, taps, lon_weights, lat_weights)

    own = model_prognosis.reshape((-1,) + model_prognosis.shape[3:])
    own, to_cross, to_pair = edge_rows(own)
    across = [(i, min(max(i + (1 if i % 2 else -1), 0), bands - 1)) for i in range(bands)]
    paired = lax.ppermute(to_pair, "band", [(i, i ^ 1) for i in range(bands)])
    crossed = lax.ppermute(to_cross, "band", across)
    truth = analysis_truth.reshape((-1,) + analysis_truth.shape[3:])
    normal = expected_normal.reshape((-1,) + expected_normal.shape[2:])
    error, fine = error_map(own, crossed, paired, truth, taps, lon_weights, lat_weights, normal.shape[0], groups)
    anomaly = anomaly_map(fine, truth, normal, groups)

    def packed(values):
        return (values * CARRY_SCALE).astype(jnp.float16)

    def unpacked(values):
        return values.astype(jnp.float32) / CARRY_SCALE

    def row_block(values, index):
        return lax.dynamic_index_in_dim(values, index, 0, keepdims=False)

    def mean_over_dates(maps):
        swapped = lax.ppermute(packed(row_block(maps, 1 - core)), "date", [(i, i ^ 1) for i in range(groups)])

        def chip_sum(index):
            mine = lax.dynamic_slice(maps, (core, index, 0, 0, 0), (1, 1) + maps.shape[2:])[0, 0]
            return mine + unpacked(row_block(swapped, index))

        pieces = []
        for step in range(1, halves):
            piece = packed(chip_sum(lax.rem(half + step, halves)))
            ring = [(i, (i + 2 * step) % groups) for i in range(groups)]
            pieces.append(lax.ppermute(piece, "date", ring))
        total = chip_sum(half)
        for piece in pieces:
            total = total + unpacked(piece)
        total = total / (dates * groups)
        return total.reshape(expected_normal.shape[:2] + total.shape[1:])

    return (mean_over_dates(error), mean_over_dates(anomaly))


def solution(mesh):
    in_specs = (
        P("date", None, None, "band", None),
        P("date", None, None, "band", None),
        P(None, None, "band", None),
        P("band"),
        P("band", None),
        P(),
        P(),
    )
    out_specs = (P(None, None, ("band", "date"), None), P(None, None, ("band", "date"), None))
    return jax.shard_map(shards, mesh=mesh, in_specs=in_specs, out_specs=out_specs, check_vma=False)
```

```python
import functools

import jax
import jax.numpy as jnp
from jax import lax
from jax.experimental import pallas as pl
from jax.experimental.pallas import tpu as pltpu
from jax.sharding import PartitionSpec as P

TAPS = 4
LANES = 128
WIDE = 256
CARRY_SCALE = 16.0


def edges_kernel(own_ref, kept_ref, cross_ref, pair_ref):
    even = lax.rem(lax.axis_index("band"), 2) == 0
    for index in range(own_ref.shape[0]):
        kept_ref[index] = own_ref[index]
        rows = own_ref[index].astype(jnp.float32)
        bottom, top = rows[:2], rows[rows.shape[0] - 2 :]
        pair_ref[index] = jnp.where(even, top, bottom).astype(jnp.bfloat16)
        cross_ref[index] = jnp.where(even, bottom, top).astype(jnp.bfloat16)


def taps_kernel(tap_ref):
    row = lax.broadcasted_iota(jnp.int32, tap_ref.shape, 0)
    tap_ref[...] = row - lax.broadcasted_iota(jnp.int32, tap_ref.shape, 1) // 4


def fill_tables(tap_ref, lon_ref, table_ref):
    dense = lon_ref.shape[1]
    for tile in range(pl.cdiv(dense, WIDE)):
        low_x = tile * WIDE
        width = min(WIDE, dense - low_x)
        base = low_x // 4 % LANES
        rows = width // 4 + 8
        depth_here = LANES if base + rows <= LANES else 2 * LANES
        columns = slice(low_x, low_x + width)
        offset = tap_ref[:rows, :width] - lon_ref[TAPS : TAPS + 1, columns].astype(jnp.int32)
        block = jnp.zeros((rows, width), jnp.float32)
        for tap in range(TAPS):
            block = jnp.where(offset == tap, lon_ref[tap : tap + 1, columns], block)
        parts = [block]
        if base:
            parts.insert(0, jnp.zeros((base, width), jnp.float32))
        if depth_here > base + rows:
            parts.append(jnp.zeros((depth_here - base - rows, width), jnp.float32))
        table_ref[tile, :depth_here, :width] = jnp.concatenate(parts, axis=0).astype(jnp.bfloat16)


def widened(lhs_ref, table_ref, tile, low_x, width):
    base = low_x // 4 % LANES
    begin = low_x // 4 - base
    depth = LANES if base + width // 4 + 8 <= LANES else 2 * LANES
    lhs = jnp.concatenate([lhs_ref[0, :, begin : begin + depth], lhs_ref[1, :, begin : begin + depth]], axis=1)
    table = table_ref[tile, :depth, :width]
    return jnp.dot(lhs, jnp.concatenate([table, table], axis=0), preferred_element_type=jnp.float32)


def wrapped_rows(rows, depth):
    sparse = rows.shape[1]
    filler = jnp.zeros((rows.shape[0], depth - sparse - 4), jnp.float32)
    return jnp.concatenate([rows[:, sparse - 1 :], rows, rows[:, :3], filler], axis=1)


def error_kernel(
    own_ref,
    cross_ref,
    pair_ref,
    truth_ref,
    tap_ref,
    lon_ref,
    lat_ref,
    out_ref,
    fine_ref,
    lhs_ref,
    table_ref,
):
    fields, coarse_rows, sparse = own_ref.shape
    _, fine_rows, dense = truth_ref.shape
    pairs = out_ref.shape[2]
    dates = fields // pairs
    ratio = fine_rows // coarse_rows
    span = 8 // ratio
    depth = lhs_ref.shape[2]
    tiles = pl.cdiv(dense, WIDE)
    band = lax.axis_index("band")
    even = lax.rem(band, 2) == 0
    lowest = band == 0
    highest = band == lax.axis_size("band") - 1

    fill_tables(tap_ref, lon_ref, table_ref)

    weights = lat_ref[...].T
    lat = [
        [
            jnp.broadcast_to(weights[8 * group : 8 * group + 8, tap : tap + 1], (8, LANES))
            for tap in range(TAPS + 1)
        ]
        for group in range(fine_rows // 8)
    ]
    lat = [[jnp.concatenate([w] * (depth // LANES), axis=1) for w in group] for group in lat]

    upper_half = lax.broadcasted_iota(jnp.int32, (8, depth), 0) < ratio
    for pair in range(pairs):
        for date in range(dates):
            index = date * pairs + pair
            paired = pair_ref[index].astype(jnp.float32)
            crossed = cross_ref[index].astype(jnp.float32)
            low = jnp.where(lowest, 0.0, jnp.where(even, crossed, paired))
            high = jnp.where(highest, 0.0, jnp.where(even, paired, crossed))
            rows8 = jnp.concatenate([low, own_ref[index].astype(jnp.float32), high], axis=0)
            wrapped = wrapped_rows(rows8, depth)
            spread = [jnp.broadcast_to(wrapped[i : i + 1], (8, depth)) for i in range(coarse_rows + 4)]
            mixed = [jnp.where(upper_half, spread[i], spread[i + 1]) for i in range(coarse_rows + 3)]
            both = []
            for group in range(fine_rows // 8):
                total = lat[group][0] * mixed[span * group]
                for tap in range(1, TAPS + 1):
                    total = total + lat[group][tap] * mixed[span * group + tap]
                both.append(total)
            both = jnp.concatenate(both, axis=0)
            upper = both.astype(jnp.bfloat16)
            rest = (both - upper.astype(jnp.float32)).astype(jnp.bfloat16)
            at = (pair * dates + date) * fine_rows
            lhs_ref[0, at : at + fine_rows, :] = upper
            lhs_ref[1, at : at + fine_rows, :] = rest

    for tile in range(tiles):
        low_x = tile * WIDE
        width = min(WIDE, dense - low_x)
        columns = slice(low_x, low_x + width)
        fine_ref[:, columns] = widened(lhs_ref, table_ref, tile, low_x, width)
        for pair in range(pairs):
            total = 0.0
            for date in range(dates):
                at = (pair * dates + date) * fine_rows
                actual = truth_ref[date * pairs + pair, :, columns].astype(jnp.float32)
                error = fine_ref[at : at + fine_rows, columns] - actual
                total = total + error * error
            store_by_owner(out_ref, pair, columns, total)


def store_by_owner(out_ref, pair, columns, values):
    _, halves, _, owned, _ = out_ref.shape
    for owner in range(2 * halves):
        out_ref[owner % 2, owner // 2, pair, :, columns] = values[owner * owned : (owner + 1) * owned]


def anomaly_kernel(fine_ref, truth_ref, normal_ref, out_ref):
    fields, fine_rows, dense = truth_ref.shape
    pairs = normal_ref.shape[0]
    dates = fields // pairs
    for low_x in range(0, dense, WIDE):
        columns = slice(low_x, min(low_x + WIDE, dense))
        for pair in range(pairs):
            normal = normal_ref[pair, :, columns].astype(jnp.float32)
            total = 0.0
            for date in range(dates):
                at = (pair * dates + date) * fine_rows
                actual = truth_ref[date * pairs + pair, :, columns].astype(jnp.float32)
                total = total + (fine_ref[at : at + fine_rows, columns] - normal) * (actual - normal)
            store_by_owner(out_ref, pair, columns, total)


def edge_rows(own):
    fields, _, sparse = own.shape
    vmem = pl.BlockSpec(memory_space=pltpu.VMEM)
    edges = jax.ShapeDtypeStruct((fields, 2, sparse), jnp.bfloat16)
    return pl.pallas_call(
        edges_kernel,
        out_shape=[jax.ShapeDtypeStruct(own.shape, own.dtype), edges, edges],
        in_specs=[vmem],
        out_specs=[vmem] * 3,
        compiler_params=pltpu.CompilerParams(vmem_limit_bytes=8 * 1024 * 1024),
        cost_estimate=pl.CostEstimate(flops=100_000_000, bytes_accessed=200_000, transcendentals=0),
    )(own)


def lat_tap_weights(starts, weights, first_coarse, ratio):
    rows = starts.shape[0]
    late = starts > first_coarse + lax.iota(jnp.int32, rows) // ratio - 2
    by_tap = weights.T
    early = jnp.pad(by_tap, ((0, 8 - TAPS), (0, LANES - rows)))
    shifted = jnp.pad(by_tap, ((1, 7 - TAPS), (0, LANES - rows)))
    return jnp.where(jnp.pad(late, (0, LANES - rows))[None], shifted, early)


def error_map(own, crossed, paired, truth, taps, lon, lat, pairs, owners):
    fields, _, sparse = own.shape
    _, fine_rows, dense = truth.shape
    depth = pl.cdiv(sparse + 4, LANES) * LANES
    vmem = pl.BlockSpec(memory_space=pltpu.VMEM)
    return pl.pallas_call(
        error_kernel,
        out_shape=[
            jax.ShapeDtypeStruct((2, owners // 2, pairs, fine_rows // owners, dense), jnp.float32),
            jax.ShapeDtypeStruct((fields * fine_rows, dense), jnp.float32),
        ],
        in_specs=[vmem] * 7,
        out_specs=[vmem] * 2,
        scratch_shapes=[
            pltpu.VMEM((2, fields * fine_rows, depth), jnp.bfloat16),
            pltpu.VMEM((pl.cdiv(dense, WIDE), 2 * LANES, WIDE), jnp.bfloat16),
        ],
        compiler_params=pltpu.CompilerParams(vmem_limit_bytes=24 * 1024 * 1024),
        cost_estimate=pl.CostEstimate(flops=1_000_000_000, bytes_accessed=4_000_000, transcendentals=0),
    )(own, crossed, paired, truth, taps, lon, lat)


def anomaly_map(fine, truth, normal, owners):
    pairs, fine_rows, dense = normal.shape
    vmem = pl.BlockSpec(memory_space=pltpu.VMEM)
    return pl.pallas_call(
        anomaly_kernel,
        out_shape=jax.ShapeDtypeStruct((2, owners // 2, pairs, fine_rows // owners, dense), jnp.float32),
        in_specs=[vmem] * 3,
        out_specs=vmem,
        compiler_params=pltpu.CompilerParams(vmem_limit_bytes=24 * 1024 * 1024),
        cost_estimate=pl.CostEstimate(flops=500_000_000, bytes_accessed=4_000_000, transcendentals=0),
    )(fine, truth, normal)


def first_core():
    return lax.rem(lax.axis_index("date"), 2) == 0


def lower_chip():
    return lax.axis_index("date") < lax.axis_size("date") // 2


def by_owner(ref, entries, lower):
    blocks = [ref[entry].astype(jnp.float32) for entry in entries]
    half = blocks[0].shape[0] // 2
    blocks = [jnp.where(lower, block[:half], block[half:]) for block in blocks]
    owned = half // 2
    return (
        jnp.concatenate([block[:owned] for block in blocks], axis=0),
        jnp.concatenate([block[owned:] for block in blocks], axis=0),
    )


def packed_tiles(entries, dense):
    full, tail = divmod(dense, LANES)
    return entries * full + (pl.cdiv(entries, LANES // tail) if tail else 0)


def pack_rows(blocks, out_ref):
    rows, dense = blocks[0].shape
    full, tail = divmod(dense, LANES)
    for at, block in enumerate(blocks):
        for tile in range(full):
            out_ref[at * full + tile] = block[:, tile * LANES : (tile + 1) * LANES].astype(out_ref.dtype)
    if tail:
        share = LANES // tail
        tails = [block[:, full * LANES :] for block in blocks]
        tails += [jnp.zeros((rows, tail), jnp.float32)] * (-len(tails) % share)
        filler = [jnp.zeros((rows, LANES - share * tail), jnp.float32)] if LANES % tail else []
        for at in range(0, len(tails), share):
            joined = jnp.concatenate(tails[at : at + share] + filler, axis=1)
            out_ref[len(blocks) * full + at // share] = joined.astype(out_ref.dtype)


def unpacked_rows(ref, at, entries, dense, low_x, width):
    full, tail = divmod(dense, LANES)
    parts = [
        ref[at * full + tile].astype(jnp.float32)
        for tile in range(low_x // LANES, min((low_x + width) // LANES, full))
    ]
    if low_x + width > full * LANES:
        share = LANES // tail
        start = at % share * tail
        parts.append(ref[entries * full + at // share].astype(jnp.float32)[:, start : start + tail])
    return jnp.concatenate(parts, axis=1)


def tile_entries(pairs, dates):
    return [[date * pairs + pair, date * pairs + pair + 1] for pair in range(0, pairs, 2) for date in range(dates)]


def away_kernel(dates, truth_ref, own_ref, _, straight_ref, crossed_ref, kept_ref):
    first = first_core()
    straight, crossed = [], []
    for entries in tile_entries(truth_ref.shape[0] // dates, dates):
        one, two = by_owner(truth_ref, entries, jnp.logical_not(lower_chip()))
        straight.append(jnp.where(first, one, two))
        crossed.append(jnp.where(first, two, one))
    pack_rows(straight, straight_ref)
    pack_rows(crossed, crossed_ref)
    for index in range(own_ref.shape[0]):
        kept_ref[index] = own_ref[index]


def home_kernel(dates, truth_ref, normal_ref, mine_ref, sibling_ref, normals_ref):
    pairs = normal_ref.shape[0]
    first = first_core()
    lower = lower_chip()
    for at, entries in enumerate(tile_entries(pairs, dates)):
        one, two = by_owner(truth_ref, entries, lower)
        mine_ref[at] = jnp.where(first, one, two).astype(mine_ref.dtype)
        sibling_ref[at] = jnp.where(first, two, one).astype(sibling_ref.dtype)
    for pair in range(0, pairs, 2):
        one, two = by_owner(normal_ref, [pair, pair + 1], lower)
        normals_ref[pair // 2] = jnp.where(first, one, two)


def shift_rows_kernel(own_ref, peer_ref, both_ref, rows_ref):
    lower = lower_chip()
    fields, coarse_rows, _ = own_ref.shape
    for index in range(2 * fields):
        block = (own_ref if index < fields else peer_ref)[index % fields]
        both_ref[index] = block
        block = block.astype(jnp.float32)
        rows_ref[index] = jnp.where(lower, block[coarse_rows - 2 :], block[:2]).astype(jnp.bfloat16)


def pick_halo_kernel(paired_ref, crossed_ref, halo_ref):
    odd = lax.rem(lax.axis_index("band"), 2) == 1
    from_pair = jnp.logical_not(jnp.logical_xor(odd, lower_chip()))
    for index in range(halo_ref.shape[0]):
        paired = paired_ref[index].astype(jnp.float32)
        crossed = crossed_ref[index].astype(jnp.float32)
        halo_ref[index] = jnp.where(from_pair, paired, crossed).astype(halo_ref.dtype)


def latitude_step(dates, coarse_ref, halo_ref, lat_ref, lhs_ref):
    fields = coarse_ref.shape[0] // 2
    pairs = fields // dates
    depth = lhs_ref.shape[2]
    rows = 2 * lhs_ref.shape[1] // (2 * fields)
    owned = rows // 2
    band = lax.axis_index("band")
    lower = lower_chip()
    first = first_core()
    outside = jnp.logical_or(
        jnp.logical_and(lower, band == 0),
        jnp.logical_and(jnp.logical_not(lower), band == lax.axis_size("band") - 1),
    )
    weights = lat_ref[...].T
    weights = jnp.where(lower, weights[: 2 * owned], weights[2 * owned : 4 * owned])
    weights = jnp.where(first, weights[:owned], weights[owned:])
    weights = jnp.concatenate([weights, weights], axis=0)
    lat = [jnp.broadcast_to(weights[:, tap : tap + 1], (rows, depth)) for tap in range(TAPS + 1)]
    first_pair = lax.broadcasted_iota(jnp.int32, (rows, depth), 0) < owned
    pending = []
    at = 0
    for side in range(2):
        for entries in tile_entries(pairs, dates):
            sources = []
            for entry in entries:
                index = side * fields + entry
                inner = coarse_ref[index].astype(jnp.float32)
                edge = jnp.where(outside, 0.0, halo_ref[index].astype(jnp.float32))
                below = jnp.concatenate([edge, inner], axis=0)
                above = jnp.concatenate([inner, edge], axis=0)
                wrapped = wrapped_rows(jnp.where(lower, below, above), depth)
                sources.append(jnp.where(first, wrapped[: TAPS + 1], wrapped[1 : TAPS + 2]))
            total = 0.0
            for tap in range(TAPS + 1):
                one, two = [jnp.broadcast_to(source[tap : tap + 1], (rows, depth)) for source in sources]
                total = total + lat[tap] * jnp.where(first_pair, one, two)
            pending.append(total)
            at += rows
            if len(pending) * rows == 16:
                block = jnp.concatenate(pending, axis=0)
                upper = block.astype(jnp.bfloat16)
                lhs_ref[0, at - 16 : at] = upper
                lhs_ref[1, at - 16 : at] = (block - upper.astype(jnp.float32)).astype(jnp.bfloat16)
                pending = []


def column_blocks(dense):
    for tile in range(pl.cdiv(dense, WIDE)):
        low_x = tile * WIDE
        width = min(WIDE, dense - low_x)
        yield tile, low_x, width, slice(low_x, low_x + width)


def added(sums, fine, actual, normal):
    error = fine - actual
    return sums[0] + error * error, sums[1] + (fine - normal) * (actual - normal)


def own_dates_kernel(
    coarse_ref,
    halo_ref,
    truth_ref,
    normals_ref,
    lat_ref,
    table_ref,
    sums_ref,
    away_ref,
    lhs_ref,
    fine_ref,
):
    tiles, rows, dense = truth_ref.shape
    dates = tiles // normals_ref.shape[0]
    latitude_step(dates, coarse_ref, halo_ref, lat_ref, lhs_ref)
    for tile, low_x, width, columns in column_blocks(dense):
        fine_ref[:, :width] = widened(lhs_ref, table_ref, tile, low_x, width)
        away_ref[:, columns] = fine_ref[tiles * rows :, :width]
        for pair in range(normals_ref.shape[0]):
            normal = normals_ref[pair, :, columns]
            sums = (0.0, 0.0)
            for at in range(pair * dates, (pair + 1) * dates):
                actual = truth_ref[at, :, columns].astype(jnp.float32)
                sums = added(sums, fine_ref[at * rows : (at + 1) * rows, :width], actual, normal)
            sums_ref[0, pair, :, columns], sums_ref[1, pair, :, columns] = sums


def sibling_dates_kernel(
    coarse_ref,
    halo_ref,
    truth_ref,
    normals_ref,
    lat_ref,
    table_ref,
    before_ref,
    straight_fine_ref,
    straight_ref,
    sums_ref,
    away_ref,
    lhs_ref,
    fine_ref,
):
    tiles, rows, dense = truth_ref.shape
    dates = tiles // normals_ref.shape[0]
    latitude_step(dates, coarse_ref, halo_ref, lat_ref, lhs_ref)
    for tile, low_x, width, columns in column_blocks(dense):
        fine_ref[:, :width] = widened(lhs_ref, table_ref, tile, low_x, width)
        away_ref[:, columns] = fine_ref[tiles * rows :, :width]
        for pair in range(normals_ref.shape[0]):
            normal = normals_ref[pair, :, columns]
            sums = (before_ref[0, pair, :, columns], before_ref[1, pair, :, columns])
            for at in range(pair * dates, (pair + 1) * dates):
                span = slice(at * rows, (at + 1) * rows)
                actual = truth_ref[at, :, columns].astype(jnp.float32)
                sums = added(sums, fine_ref[span, :width], actual, normal)
                actual = unpacked_rows(straight_ref, at, tiles, dense, low_x, width)
                sums = added(sums, straight_fine_ref[span, columns], actual, normal)
            sums_ref[0, pair, :, columns], sums_ref[1, pair, :, columns] = sums


def mean_kernel(dates, count, before_ref, fine_ref, crossed_ref, normals_ref, *refs):
    *results, held_ref, sems = refs
    tiles, rows, dense = normals_ref.shape
    owned = rows // 2
    copies = []
    for pair in range(tiles):
        for _, low_x, width, columns in column_blocks(dense):
            normal = normals_ref[pair, :, columns]
            sums = (before_ref[0, pair, :, columns], before_ref[1, pair, :, columns])
            for at in range(pair * dates, (pair + 1) * dates):
                actual = unpacked_rows(crossed_ref, at, tiles * dates, dense, low_x, width)
                sums = added(sums, fine_ref[at * rows : (at + 1) * rows, columns], actual, normal)
            for kind, total in enumerate(sums):
                total = total * (1.0 / count)
                held_ref[kind, 2 * pair, :, columns] = total[:owned]
                held_ref[kind, 2 * pair + 1, :, columns] = total[owned:]
        done = pl.ds(2 * pair, 2)
        for kind, out_ref in enumerate(results):
            copy = pltpu.make_async_copy(held_ref.at[kind, done], out_ref.at[done], sems.at[len(copies)])
            copy.start()
            copies.append(copy)
    for copy in copies:
        copy.wait()


def kernel_call(kernel, out_shape, scratch, megabytes, flops, *operands, out_space=pltpu.VMEM):
    vmem = pl.BlockSpec(memory_space=pltpu.VMEM)
    return pl.pallas_call(
        kernel,
        out_shape=out_shape,
        in_specs=[vmem] * len(operands),
        out_specs=[pl.BlockSpec(memory_space=out_space)] * len(out_shape),
        scratch_shapes=scratch,
        compiler_params=pltpu.CompilerParams(vmem_limit_bytes=megabytes * 1024 * 1024),
        cost_estimate=pl.CostEstimate(flops=flops, bytes_accessed=0, transcendentals=0),
    )(*operands)


def two_chip_maps(model_prognosis, analysis_truth, expected_normal, taps, lon_weights, lat_weights):
    bands = lax.axis_size("band")
    groups = lax.axis_size("date")
    dates, leads, variables, coarse_rows, sparse = model_prognosis.shape
    fine_rows, dense = analysis_truth.shape[3:]
    owned = fine_rows // groups
    rows = 2 * owned
    pairs = leads * variables
    fields = dates * pairs
    tiles = fields // 2
    depth = pl.cdiv(sparse + 4, LANES) * LANES
    float32, bfloat16 = jnp.float32, jnp.bfloat16
    straight_way = [(i, (i + 2) % groups) for i in range(groups)]
    crossed_way = [(i, (i + 2) % groups ^ 1) for i in range(groups)]
    sibling_way = [(i, i ^ 1) for i in range(groups)]

    own = model_prognosis.reshape(fields, coarse_rows, sparse)
    truth = analysis_truth.reshape(fields, fine_rows, dense)
    normal = expected_normal.reshape(pairs, fine_rows, dense)
    peer = lax.ppermute(model_prognosis, "date", straight_way).reshape(own.shape)

    packed = jax.ShapeDtypeStruct((packed_tiles(tiles, dense), rows, LANES), bfloat16)
    straight, crossed, own = kernel_call(
        functools.partial(away_kernel, dates),
        [packed, packed, jax.ShapeDtypeStruct(own.shape, own.dtype)],
        [],
        8,
        100_000_000,
        truth,
        own,
        taps,
    )
    straight = lax.ppermute(straight, "date", straight_way)
    crossed = lax.ppermute(crossed, "date", crossed_way)
    plain = jax.ShapeDtypeStruct((tiles, rows, dense), bfloat16)
    mine, sibling, normals = kernel_call(
        functools.partial(home_kernel, dates),
        [plain, plain, jax.ShapeDtypeStruct((pairs // 2, rows, dense), float32)],
        [],
        12,
        100_000_000,
        truth,
        normal,
    )
    sibling = lax.ppermute(sibling, "date", sibling_way)

    coarse, edges = kernel_call(
        shift_rows_kernel,
        [
            jax.ShapeDtypeStruct((2 * fields, coarse_rows, sparse), bfloat16),
            jax.ShapeDtypeStruct((2 * fields, 2, sparse), bfloat16),
        ],
        [],
        8,
        100_000_000,
        own,
        peer,
    )
    across = [(i, min(max(i + (1 if i % 2 else -1), 0), bands - 1)) for i in range(bands)]
    crossed_rows = lax.ppermute(edges, "band", across)
    paired_rows = lax.ppermute(edges, "band", [(i, i ^ 1) for i in range(bands)])
    (halo,) = kernel_call(
        pick_halo_kernel, [jax.ShapeDtypeStruct(edges.shape, bfloat16)], [], 8, 0, paired_rows, crossed_rows
    )
    sibling_coarse = lax.ppermute(coarse, "date", sibling_way)
    sibling_halo = lax.ppermute(halo, "date", sibling_way)

    sums = jax.ShapeDtypeStruct((2, pairs // 2, rows, dense), float32)
    away = jax.ShapeDtypeStruct((tiles * rows, dense), float32)
    table = jax.ShapeDtypeStruct((pl.cdiv(dense, WIDE), 2 * LANES, WIDE), bfloat16)
    scratch = [
        pltpu.VMEM((2, 2 * tiles * rows, depth), bfloat16),
        pltpu.VMEM((2 * tiles * rows, WIDE), float32),
    ]
    (table,) = kernel_call(fill_tables, [table], [], 8, 4_000_000_000, taps, lon_weights)
    own_sums, straight_fine = kernel_call(
        own_dates_kernel,
        [sums, away],
        scratch,
        20,
        0,
        coarse,
        halo,
        mine,
        normals,
        lat_weights,
        table,
    )
    chip_sums, crossed_fine = kernel_call(
        sibling_dates_kernel,
        [sums, away],
        scratch,
        20,
        0,
        sibling_coarse,
        sibling_halo,
        sibling,
        normals,
        lat_weights,
        table,
        own_sums,
        straight_fine,
        straight,
    )
    out = jax.ShapeDtypeStruct((pairs, owned, dense), float32)
    results = kernel_call(
        functools.partial(mean_kernel, dates, dates * groups),
        [out, out],
        [pltpu.VMEM((2,) + out.shape, float32), pltpu.SemaphoreType.DMA((pairs,))],
        16,
        0,
        chip_sums,
        crossed_fine,
        crossed,
        normals,
        out_space=pl.ANY,
    )
    return tuple(result.reshape(leads, variables, owned, dense) for result in results)


def shards(
    model_prognosis,
    analysis_truth,
    expected_normal,
    parallel_first_indices,
    parallel_blend_factors,
    meridian_first_indices,
    meridian_blend_factors,
):
    bands = lax.axis_size("band")
    groups = lax.axis_size("date")
    halves = groups // 2
    dates = model_prognosis.shape[0]
    group = lax.axis_index("date")
    core = lax.rem(group, 2)
    half = lax.div(group, 2)

    coarse_rows = model_prognosis.shape[3]
    lat_weights = lat_tap_weights(
        parallel_first_indices,
        parallel_blend_factors,
        lax.axis_index("band") * coarse_rows,
        analysis_truth.shape[3] // coarse_rows,
    )
    dense = meridian_first_indices.shape[0]
    late = meridian_first_indices == lax.iota(jnp.int32, dense) // 4
    lon_weights = jnp.where(
        lax.broadcasted_iota(jnp.int32, (8, dense), 0) < TAPS,
        jnp.pad(meridian_blend_factors, ((0, 8 - TAPS), (0, 0))).astype(jnp.float32),
        late.astype(jnp.float32)[None],
    )
    (taps,) = kernel_call(
        taps_kernel, [jax.ShapeDtypeStruct((WIDE // 4 + 8, WIDE), jnp.int32)], [], 8, 2_000_000_000
    )
    tall = 2 * analysis_truth.shape[3] == 8 * groups
    if halves == 2 and tall and expected_normal.shape[0] * expected_normal.shape[1] % 2 == 0:
        return two_chip_maps(model_prognosis, analysis_truth, expected_normal, taps, lon_weights, lat_weights)

    own = model_prognosis.reshape((-1,) + model_prognosis.shape[3:])
    own, to_cross, to_pair = edge_rows(own)
    across = [(i, min(max(i + (1 if i % 2 else -1), 0), bands - 1)) for i in range(bands)]
    paired = lax.ppermute(to_pair, "band", [(i, i ^ 1) for i in range(bands)])
    crossed = lax.ppermute(to_cross, "band", across)
    truth = analysis_truth.reshape((-1,) + analysis_truth.shape[3:])
    normal = expected_normal.reshape((-1,) + expected_normal.shape[2:])
    error, fine = error_map(own, crossed, paired, truth, taps, lon_weights, lat_weights, normal.shape[0], groups)
    anomaly = anomaly_map(fine, truth, normal, groups)

    def packed(values):
        return (values * CARRY_SCALE).astype(jnp.float16)

    def unpacked(values):
        return values.astype(jnp.float32) / CARRY_SCALE

    def row_block(values, index):
        return lax.dynamic_index_in_dim(values, index, 0, keepdims=False)

    def mean_over_dates(maps):
        swapped = lax.ppermute(packed(row_block(maps, 1 - core)), "date", [(i, i ^ 1) for i in range(groups)])

        def chip_sum(index):
            mine = lax.dynamic_slice(maps, (core, index, 0, 0, 0), (1, 1) + maps.shape[2:])[0, 0]
            return mine + unpacked(row_block(swapped, index))

        pieces = []
        for step in range(1, halves):
            piece = packed(chip_sum(lax.rem(half + step, halves)))
            ring = [(i, (i + 2 * step) % groups) for i in range(groups)]
            pieces.append(lax.ppermute(piece, "date", ring))
        total = chip_sum(half)
        for piece in pieces:
            total = total + unpacked(piece)
        total = total / (dates * groups)
        return total.reshape(expected_normal.shape[:2] + total.shape[1:])

    return (mean_over_dates(error), mean_over_dates(anomaly))


def solution(mesh):
    in_specs = (
        P("date", None, None, "band", None),
        P("date", None, None, "band", None),
        P(None, None, "band", None),
        P("band"),
        P("band", None),
        P(),
        P(),
    )
    out_specs = (P(None, None, ("band", "date"), None), P(None, None, ("band", "date"), None))
    return jax.shard_map(shards, mesh=mesh, in_specs=in_specs, out_specs=out_specs, check_vma=False)
```

```python
import functools

import jax
import jax.numpy as jnp
from jax import lax
from jax.experimental import pallas as pl
from jax.experimental.pallas import tpu as pltpu
from jax.sharding import PartitionSpec as P

TAPS = 4
LANES = 128
WIDE = 256
CARRY_SCALE = 16.0


def edges_kernel(own_ref, kept_ref, cross_ref, pair_ref):
    even = lax.rem(lax.axis_index("band"), 2) == 0
    for index in range(own_ref.shape[0]):
        kept_ref[index] = own_ref[index]
        rows = own_ref[index].astype(jnp.float32)
        bottom, top = rows[:2], rows[rows.shape[0] - 2 :]
        pair_ref[index] = jnp.where(even, top, bottom).astype(jnp.bfloat16)
        cross_ref[index] = jnp.where(even, bottom, top).astype(jnp.bfloat16)


def taps_kernel(tap_ref):
    row = lax.broadcasted_iota(jnp.int32, tap_ref.shape, 0)
    tap_ref[...] = row - lax.broadcasted_iota(jnp.int32, tap_ref.shape, 1) // 4


def fill_tables(tap_ref, lon_ref, table_ref):
    dense = lon_ref.shape[1]
    for tile in range(pl.cdiv(dense, WIDE)):
        low_x = tile * WIDE
        width = min(WIDE, dense - low_x)
        base = low_x // 4 % LANES
        rows = width // 4 + 8
        depth_here = LANES if base + rows <= LANES else 2 * LANES
        columns = slice(low_x, low_x + width)
        offset = tap_ref[:rows, :width] - lon_ref[TAPS : TAPS + 1, columns].astype(jnp.int32)
        block = jnp.zeros((rows, width), jnp.float32)
        for tap in range(TAPS):
            block = jnp.where(offset == tap, lon_ref[tap : tap + 1, columns], block)
        parts = [block]
        if base:
            parts.insert(0, jnp.zeros((base, width), jnp.float32))
        if depth_here > base + rows:
            parts.append(jnp.zeros((depth_here - base - rows, width), jnp.float32))
        table_ref[tile, :depth_here, :width] = jnp.concatenate(parts, axis=0).astype(jnp.bfloat16)


def widened(lhs_ref, table_ref, tile, low_x, width):
    base = low_x // 4 % LANES
    begin = low_x // 4 - base
    depth = LANES if base + width // 4 + 8 <= LANES else 2 * LANES
    lhs = jnp.concatenate([lhs_ref[0, :, begin : begin + depth], lhs_ref[1, :, begin : begin + depth]], axis=1)
    table = table_ref[tile, :depth, :width]
    return jnp.dot(lhs, jnp.concatenate([table, table], axis=0), preferred_element_type=jnp.float32)


def wrapped_rows(rows, depth):
    sparse = rows.shape[1]
    filler = jnp.zeros((rows.shape[0], depth - sparse - 4), jnp.float32)
    return jnp.concatenate([rows[:, sparse - 1 :], rows, rows[:, :3], filler], axis=1)


def error_kernel(
    own_ref,
    cross_ref,
    pair_ref,
    truth_ref,
    tap_ref,
    lon_ref,
    lat_ref,
    out_ref,
    fine_ref,
    lhs_ref,
    table_ref,
):
    fields, coarse_rows, sparse = own_ref.shape
    _, fine_rows, dense = truth_ref.shape
    pairs = out_ref.shape[2]
    dates = fields // pairs
    ratio = fine_rows // coarse_rows
    span = 8 // ratio
    depth = lhs_ref.shape[2]
    tiles = pl.cdiv(dense, WIDE)
    band = lax.axis_index("band")
    even = lax.rem(band, 2) == 0
    lowest = band == 0
    highest = band == lax.axis_size("band") - 1

    fill_tables(tap_ref, lon_ref, table_ref)

    weights = lat_ref[...].T
    lat = [
        [
            jnp.broadcast_to(weights[8 * group : 8 * group + 8, tap : tap + 1], (8, LANES))
            for tap in range(TAPS + 1)
        ]
        for group in range(fine_rows // 8)
    ]
    lat = [[jnp.concatenate([w] * (depth // LANES), axis=1) for w in group] for group in lat]

    upper_half = lax.broadcasted_iota(jnp.int32, (8, depth), 0) < ratio
    for pair in range(pairs):
        for date in range(dates):
            index = date * pairs + pair
            paired = pair_ref[index].astype(jnp.float32)
            crossed = cross_ref[index].astype(jnp.float32)
            low = jnp.where(lowest, 0.0, jnp.where(even, crossed, paired))
            high = jnp.where(highest, 0.0, jnp.where(even, paired, crossed))
            rows8 = jnp.concatenate([low, own_ref[index].astype(jnp.float32), high], axis=0)
            wrapped = wrapped_rows(rows8, depth)
            spread = [jnp.broadcast_to(wrapped[i : i + 1], (8, depth)) for i in range(coarse_rows + 4)]
            mixed = [jnp.where(upper_half, spread[i], spread[i + 1]) for i in range(coarse_rows + 3)]
            both = []
            for group in range(fine_rows // 8):
                total = lat[group][0] * mixed[span * group]
                for tap in range(1, TAPS + 1):
                    total = total + lat[group][tap] * mixed[span * group + tap]
                both.append(total)
            both = jnp.concatenate(both, axis=0)
            upper = both.astype(jnp.bfloat16)
            rest = (both - upper.astype(jnp.float32)).astype(jnp.bfloat16)
            at = (pair * dates + date) * fine_rows
            lhs_ref[0, at : at + fine_rows, :] = upper
            lhs_ref[1, at : at + fine_rows, :] = rest

    for tile in range(tiles):
        low_x = tile * WIDE
        width = min(WIDE, dense - low_x)
        columns = slice(low_x, low_x + width)
        fine_ref[:, columns] = widened(lhs_ref, table_ref, tile, low_x, width)
        for pair in range(pairs):
            total = 0.0
            for date in range(dates):
                at = (pair * dates + date) * fine_rows
                actual = truth_ref[date * pairs + pair, :, columns].astype(jnp.float32)
                error = fine_ref[at : at + fine_rows, columns] - actual
                total = total + error * error
            store_by_owner(out_ref, pair, columns, total)


def store_by_owner(out_ref, pair, columns, values):
    _, halves, _, owned, _ = out_ref.shape
    for owner in range(2 * halves):
        out_ref[owner % 2, owner // 2, pair, :, columns] = values[owner * owned : (owner + 1) * owned]


def anomaly_kernel(fine_ref, truth_ref, normal_ref, out_ref):
    fields, fine_rows, dense = truth_ref.shape
    pairs = normal_ref.shape[0]
    dates = fields // pairs
    for low_x in range(0, dense, WIDE):
        columns = slice(low_x, min(low_x + WIDE, dense))
        for pair in range(pairs):
            normal = normal_ref[pair, :, columns].astype(jnp.float32)
            total = 0.0
            for date in range(dates):
                at = (pair * dates + date) * fine_rows
                actual = truth_ref[date * pairs + pair, :, columns].astype(jnp.float32)
                total = total + (fine_ref[at : at + fine_rows, columns] - normal) * (actual - normal)
            store_by_owner(out_ref, pair, columns, total)


def edge_rows(own):
    fields, _, sparse = own.shape
    vmem = pl.BlockSpec(memory_space=pltpu.VMEM)
    edges = jax.ShapeDtypeStruct((fields, 2, sparse), jnp.bfloat16)
    return pl.pallas_call(
        edges_kernel,
        out_shape=[jax.ShapeDtypeStruct(own.shape, own.dtype), edges, edges],
        in_specs=[vmem],
        out_specs=[vmem] * 3,
        compiler_params=pltpu.CompilerParams(vmem_limit_bytes=8 * 1024 * 1024),
        cost_estimate=pl.CostEstimate(flops=100_000_000, bytes_accessed=200_000, transcendentals=0),
    )(own)


def lat_tap_weights(starts, weights, first_coarse, ratio):
    rows = starts.shape[0]
    late = starts > first_coarse + lax.iota(jnp.int32, rows) // ratio - 2
    by_tap = weights.T
    early = jnp.pad(by_tap, ((0, 8 - TAPS), (0, LANES - rows)))
    shifted = jnp.pad(by_tap, ((1, 7 - TAPS), (0, LANES - rows)))
    return jnp.where(jnp.pad(late, (0, LANES - rows))[None], shifted, early)


def error_map(own, crossed, paired, truth, taps, lon, lat, pairs, owners):
    fields, _, sparse = own.shape
    _, fine_rows, dense = truth.shape
    depth = pl.cdiv(sparse + 4, LANES) * LANES
    vmem = pl.BlockSpec(memory_space=pltpu.VMEM)
    return pl.pallas_call(
        error_kernel,
        out_shape=[
            jax.ShapeDtypeStruct((2, owners // 2, pairs, fine_rows // owners, dense), jnp.float32),
            jax.ShapeDtypeStruct((fields * fine_rows, dense), jnp.float32),
        ],
        in_specs=[vmem] * 7,
        out_specs=[vmem] * 2,
        scratch_shapes=[
            pltpu.VMEM((2, fields * fine_rows, depth), jnp.bfloat16),
            pltpu.VMEM((pl.cdiv(dense, WIDE), 2 * LANES, WIDE), jnp.bfloat16),
        ],
        compiler_params=pltpu.CompilerParams(vmem_limit_bytes=24 * 1024 * 1024),
        cost_estimate=pl.CostEstimate(flops=1_000_000_000, bytes_accessed=4_000_000, transcendentals=0),
    )(own, crossed, paired, truth, taps, lon, lat)


def anomaly_map(fine, truth, normal, owners):
    pairs, fine_rows, dense = normal.shape
    vmem = pl.BlockSpec(memory_space=pltpu.VMEM)
    return pl.pallas_call(
        anomaly_kernel,
        out_shape=jax.ShapeDtypeStruct((2, owners // 2, pairs, fine_rows // owners, dense), jnp.float32),
        in_specs=[vmem] * 3,
        out_specs=vmem,
        compiler_params=pltpu.CompilerParams(vmem_limit_bytes=24 * 1024 * 1024),
        cost_estimate=pl.CostEstimate(flops=500_000_000, bytes_accessed=4_000_000, transcendentals=0),
    )(fine, truth, normal)


def first_core():
    return lax.rem(lax.axis_index("date"), 2) == 0


def lower_chip():
    return lax.axis_index("date") < lax.axis_size("date") // 2


def by_owner(ref, entries, lower):
    blocks = [ref[entry] for entry in entries]
    half = blocks[0].shape[0] // 2
    blocks = [jnp.where(lower, block[:half], block[half:]).astype(jnp.float32) for block in blocks]
    owned = half // 2
    return (
        jnp.concatenate([block[:owned] for block in blocks], axis=0),
        jnp.concatenate([block[owned:] for block in blocks], axis=0),
    )


def packed_tiles(entries, dense):
    full, tail = divmod(dense, LANES)
    return entries * full + (pl.cdiv(entries, LANES // tail) if tail else 0)


def pack_rows(blocks, out_ref):
    rows, dense = blocks[0].shape
    full, tail = divmod(dense, LANES)
    for at, block in enumerate(blocks):
        for tile in range(full):
            out_ref[at * full + tile] = block[:, tile * LANES : (tile + 1) * LANES].astype(out_ref.dtype)
    if tail:
        share = LANES // tail
        tails = [block[:, full * LANES :] for block in blocks]
        tails += [jnp.zeros((rows, tail), jnp.float32)] * (-len(tails) % share)
        filler = [jnp.zeros((rows, LANES - share * tail), jnp.float32)] if LANES % tail else []
        for at in range(0, len(tails), share):
            joined = jnp.concatenate(tails[at : at + share] + filler, axis=1)
            out_ref[len(blocks) * full + at // share] = joined.astype(out_ref.dtype)


def unpacked_rows(ref, at, entries, dense, low_x, width):
    full, tail = divmod(dense, LANES)
    parts = [
        ref[at * full + tile].astype(jnp.float32)
        for tile in range(low_x // LANES, min((low_x + width) // LANES, full))
    ]
    if low_x + width > full * LANES:
        share = LANES // tail
        start = at % share * tail
        parts.append(ref[entries * full + at // share].astype(jnp.float32)[:, start : start + tail])
    return jnp.concatenate(parts, axis=1)


def tile_entries(pairs, dates):
    return [[date * pairs + pair, date * pairs + pair + 1] for pair in range(0, pairs, 2) for date in range(dates)]


def away_kernel(dates, truth_ref, own_ref, _, straight_ref, crossed_ref, kept_ref):
    first = first_core()
    straight, crossed = [], []
    for entries in tile_entries(truth_ref.shape[0] // dates, dates):
        one, two = by_owner(truth_ref, entries, jnp.logical_not(lower_chip()))
        straight.append(jnp.where(first, one, two))
        crossed.append(jnp.where(first, two, one))
    pack_rows(straight, straight_ref)
    pack_rows(crossed, crossed_ref)
    for index in range(own_ref.shape[0]):
        kept_ref[index] = own_ref[index]


def home_kernel(dates, truth_ref, normal_ref, mine_ref, sibling_ref, normals_ref):
    pairs = normal_ref.shape[0]
    first = first_core()
    lower = lower_chip()
    for at, entries in enumerate(tile_entries(pairs, dates)):
        one, two = by_owner(truth_ref, entries, lower)
        mine_ref[at] = jnp.where(first, one, two).astype(mine_ref.dtype)
        sibling_ref[at] = jnp.where(first, two, one).astype(sibling_ref.dtype)
    for pair in range(0, pairs, 2):
        one, two = by_owner(normal_ref, [pair, pair + 1], lower)
        normals_ref[pair // 2] = jnp.where(first, one, two)


def shift_rows_kernel(own_ref, peer_ref, both_ref, rows_ref):
    lower = lower_chip()
    fields, coarse_rows, _ = own_ref.shape
    for index in range(2 * fields):
        block = (own_ref if index < fields else peer_ref)[index % fields]
        both_ref[index] = block
        block = block.astype(jnp.float32)
        rows_ref[index] = jnp.where(lower, block[coarse_rows - 2 :], block[:2]).astype(jnp.bfloat16)


def latitude_step(dates, coarse_ref, halo_ref, lat_ref, lhs_ref):
    fields = coarse_ref.shape[0] // 2
    pairs = fields // dates
    depth = lhs_ref.shape[2]
    rows = 2 * lhs_ref.shape[1] // (2 * fields)
    owned = rows // 2
    band = lax.axis_index("band")
    lower = lower_chip()
    first = first_core()
    outside = jnp.logical_or(
        jnp.logical_and(lower, band == 0),
        jnp.logical_and(jnp.logical_not(lower), band == lax.axis_size("band") - 1),
    )
    weights = lat_ref[...].T
    weights = jnp.where(lower, weights[: 2 * owned], weights[2 * owned : 4 * owned])
    weights = jnp.where(first, weights[:owned], weights[owned:])
    weights = jnp.concatenate([weights, weights], axis=0)
    lat = [jnp.broadcast_to(weights[:, tap : tap + 1], (rows, depth)) for tap in range(TAPS + 1)]
    first_pair = lax.broadcasted_iota(jnp.int32, (rows, depth), 0) < owned
    pending = []
    at = 0
    for side in range(2):
        for entries in tile_entries(pairs, dates):
            sources = []
            for entry in entries:
                index = side * fields + entry
                inner = coarse_ref[index].astype(jnp.float32)
                edge = jnp.where(outside, 0.0, halo_ref[index].astype(jnp.float32))
                below = jnp.concatenate([edge, inner], axis=0)
                above = jnp.concatenate([inner, edge], axis=0)
                wrapped = wrapped_rows(jnp.where(lower, below, above), depth)
                sources.append(jnp.where(first, wrapped[: TAPS + 1], wrapped[1 : TAPS + 2]))
            total = 0.0
            for tap in range(TAPS + 1):
                one, two = [jnp.broadcast_to(source[tap : tap + 1], (rows, depth)) for source in sources]
                total = total + lat[tap] * jnp.where(first_pair, one, two)
            pending.append(total)
            at += rows
            if len(pending) * rows == 16:
                block = jnp.concatenate(pending, axis=0)
                upper = block.astype(jnp.bfloat16)
                lhs_ref[0, at - 16 : at] = upper
                lhs_ref[1, at - 16 : at] = (block - upper.astype(jnp.float32)).astype(jnp.bfloat16)
                pending = []


def column_blocks(dense):
    for tile in range(pl.cdiv(dense, WIDE)):
        low_x = tile * WIDE
        width = min(WIDE, dense - low_x)
        yield tile, low_x, width, slice(low_x, low_x + width)


def added(sums, fine, actual, normal):
    error = fine - actual
    return sums[0] + error * error, sums[1] + (fine - normal) * (actual - normal)


def own_dates_kernel(
    coarse_ref,
    halo_ref,
    truth_ref,
    normals_ref,
    lat_ref,
    table_ref,
    sums_ref,
    away_ref,
    lhs_ref,
    fine_ref,
):
    tiles, rows, dense = truth_ref.shape
    dates = tiles // normals_ref.shape[0]
    latitude_step(dates, coarse_ref, halo_ref, lat_ref, lhs_ref)
    for tile, low_x, width, columns in column_blocks(dense):
        fine_ref[:, :width] = widened(lhs_ref, table_ref, tile, low_x, width)
        away_ref[:, columns] = fine_ref[tiles * rows :, :width]
        for pair in range(normals_ref.shape[0]):
            normal = normals_ref[pair, :, columns]
            sums = (0.0, 0.0)
            for at in range(pair * dates, (pair + 1) * dates):
                actual = truth_ref[at, :, columns].astype(jnp.float32)
                sums = added(sums, fine_ref[at * rows : (at + 1) * rows, :width], actual, normal)
            sums_ref[0, pair, :, columns], sums_ref[1, pair, :, columns] = sums


def sibling_dates_kernel(
    coarse_ref,
    halo_ref,
    truth_ref,
    normals_ref,
    lat_ref,
    table_ref,
    before_ref,
    straight_fine_ref,
    straight_ref,
    sums_ref,
    away_ref,
    lhs_ref,
    fine_ref,
):
    tiles, rows, dense = truth_ref.shape
    dates = tiles // normals_ref.shape[0]
    latitude_step(dates, coarse_ref, halo_ref, lat_ref, lhs_ref)
    for tile, low_x, width, columns in column_blocks(dense):
        fine_ref[:, :width] = widened(lhs_ref, table_ref, tile, low_x, width)
        away_ref[:, columns] = fine_ref[tiles * rows :, :width]
        for pair in range(normals_ref.shape[0]):
            normal = normals_ref[pair, :, columns]
            sums = (before_ref[0, pair, :, columns], before_ref[1, pair, :, columns])
            for at in range(pair * dates, (pair + 1) * dates):
                span = slice(at * rows, (at + 1) * rows)
                actual = truth_ref[at, :, columns].astype(jnp.float32)
                sums = added(sums, fine_ref[span, :width], actual, normal)
                actual = unpacked_rows(straight_ref, at, tiles, dense, low_x, width)
                sums = added(sums, straight_fine_ref[span, columns], actual, normal)
            sums_ref[0, pair, :, columns], sums_ref[1, pair, :, columns] = sums


def mean_kernel(dates, count, before_ref, fine_ref, crossed_ref, normals_ref, *refs):
    *results, held_ref, sems = refs
    tiles, rows, dense = normals_ref.shape
    owned = rows // 2
    copies = []
    for pair in range(tiles):
        for _, low_x, width, columns in column_blocks(dense):
            normal = normals_ref[pair, :, columns]
            sums = (before_ref[0, pair, :, columns], before_ref[1, pair, :, columns])
            for at in range(pair * dates, (pair + 1) * dates):
                actual = unpacked_rows(crossed_ref, at, tiles * dates, dense, low_x, width)
                sums = added(sums, fine_ref[at * rows : (at + 1) * rows, columns], actual, normal)
            for kind, total in enumerate(sums):
                total = total * (1.0 / count)
                held_ref[kind, 2 * pair, :, columns] = total[:owned]
                held_ref[kind, 2 * pair + 1, :, columns] = total[owned:]
        done = pl.ds(2 * pair, 2)
        for kind, out_ref in enumerate(results):
            copy = pltpu.make_async_copy(held_ref.at[kind, done], out_ref.at[done], sems.at[len(copies)])
            copy.start()
            copies.append(copy)
    for copy in copies:
        copy.wait()


def kernel_call(kernel, out_shape, scratch, megabytes, flops, *operands, out_space=pltpu.VMEM):
    vmem = pl.BlockSpec(memory_space=pltpu.VMEM)
    return pl.pallas_call(
        kernel,
        out_shape=out_shape,
        in_specs=[vmem] * len(operands),
        out_specs=[pl.BlockSpec(memory_space=out_space)] * len(out_shape),
        scratch_shapes=scratch,
        compiler_params=pltpu.CompilerParams(vmem_limit_bytes=megabytes * 1024 * 1024),
        cost_estimate=pl.CostEstimate(flops=flops, bytes_accessed=0, transcendentals=0),
    )(*operands)


def two_chip_maps(model_prognosis, analysis_truth, expected_normal, taps, lon_weights, lat_weights):
    bands = lax.axis_size("band")
    groups = lax.axis_size("date")
    dates, leads, variables, coarse_rows, sparse = model_prognosis.shape
    fine_rows, dense = analysis_truth.shape[3:]
    owned = fine_rows // groups
    rows = 2 * owned
    pairs = leads * variables
    fields = dates * pairs
    tiles = fields // 2
    depth = pl.cdiv(sparse + 4, LANES) * LANES
    float32, bfloat16 = jnp.float32, jnp.bfloat16
    straight_way = [(i, (i + 2) % groups) for i in range(groups)]
    crossed_way = [(i, (i + 2) % groups ^ 1) for i in range(groups)]
    sibling_way = [(i, i ^ 1) for i in range(groups)]

    own = model_prognosis.reshape(fields, coarse_rows, sparse)
    truth = analysis_truth.reshape(fields, fine_rows, dense)
    normal = expected_normal.reshape(pairs, fine_rows, dense)
    peer = lax.ppermute(model_prognosis, "date", straight_way).reshape(own.shape)

    packed = jax.ShapeDtypeStruct((packed_tiles(tiles, dense), rows, LANES), bfloat16)
    straight, crossed, own = kernel_call(
        functools.partial(away_kernel, dates),
        [packed, packed, jax.ShapeDtypeStruct(own.shape, own.dtype)],
        [],
        8,
        100_000_000,
        truth,
        own,
        taps,
    )
    straight = lax.ppermute(straight, "date", straight_way)
    crossed = lax.ppermute(crossed, "date", crossed_way)
    plain = jax.ShapeDtypeStruct((tiles, rows, dense), bfloat16)
    mine, sibling, normals = kernel_call(
        functools.partial(home_kernel, dates),
        [plain, plain, jax.ShapeDtypeStruct((pairs // 2, rows, dense), float32)],
        [],
        12,
        100_000_000,
        truth,
        normal,
    )
    sibling = lax.ppermute(sibling, "date", sibling_way)

    chain = []
    for group in range(groups):
        for band in range(bands):
            to = band + (1 if group < groups // 2 else -1)
            if 0 <= to < bands:
                chain.append((group * bands + band, group * bands + to))
    coarse, edges = kernel_call(
        shift_rows_kernel,
        [
            jax.ShapeDtypeStruct((2 * fields, coarse_rows, sparse), bfloat16),
            jax.ShapeDtypeStruct((2 * fields, 2, sparse), bfloat16),
        ],
        [],
        8,
        100_000_000,
        own,
        peer,
    )
    halo = lax.ppermute(edges, ("date", "band"), chain)
    sibling_coarse = lax.ppermute(coarse, "date", sibling_way)
    sibling_halo = lax.ppermute(halo, "date", sibling_way)

    sums = jax.ShapeDtypeStruct((2, pairs // 2, rows, dense), float32)
    away = jax.ShapeDtypeStruct((tiles * rows, dense), float32)
    table = jax.ShapeDtypeStruct((pl.cdiv(dense, WIDE), 2 * LANES, WIDE), bfloat16)
    scratch = [
        pltpu.VMEM((2, 2 * tiles * rows, depth), bfloat16),
        pltpu.VMEM((2 * tiles * rows, WIDE), float32),
    ]
    (table,) = kernel_call(fill_tables, [table], [], 8, 4_000_000_000, taps, lon_weights)
    own_sums, straight_fine = kernel_call(
        own_dates_kernel,
        [sums, away],
        scratch,
        20,
        0,
        coarse,
        halo,
        mine,
        normals,
        lat_weights,
        table,
    )
    chip_sums, crossed_fine = kernel_call(
        sibling_dates_kernel,
        [sums, away],
        scratch,
        20,
        0,
        sibling_coarse,
        sibling_halo,
        sibling,
        normals,
        lat_weights,
        table,
        own_sums,
        straight_fine,
        straight,
    )
    out = jax.ShapeDtypeStruct((pairs, owned, dense), float32)
    results = kernel_call(
        functools.partial(mean_kernel, dates, dates * groups),
        [out, out],
        [pltpu.VMEM((2,) + out.shape, float32), pltpu.SemaphoreType.DMA((pairs,))],
        16,
        0,
        chip_sums,
        crossed_fine,
        crossed,
        normals,
        out_space=pl.ANY,
    )
    return tuple(result.reshape(leads, variables, owned, dense) for result in results)


def shards(
    model_prognosis,
    analysis_truth,
    expected_normal,
    parallel_first_indices,
    parallel_blend_factors,
    meridian_first_indices,
    meridian_blend_factors,
):
    bands = lax.axis_size("band")
    groups = lax.axis_size("date")
    halves = groups // 2
    dates = model_prognosis.shape[0]
    group = lax.axis_index("date")
    core = lax.rem(group, 2)
    half = lax.div(group, 2)

    coarse_rows = model_prognosis.shape[3]
    lat_weights = lat_tap_weights(
        parallel_first_indices,
        parallel_blend_factors,
        lax.axis_index("band") * coarse_rows,
        analysis_truth.shape[3] // coarse_rows,
    )
    dense = meridian_first_indices.shape[0]
    late = meridian_first_indices == lax.iota(jnp.int32, dense) // 4
    lon_weights = jnp.where(
        lax.broadcasted_iota(jnp.int32, (8, dense), 0) < TAPS,
        jnp.pad(meridian_blend_factors, ((0, 8 - TAPS), (0, 0))).astype(jnp.float32),
        late.astype(jnp.float32)[None],
    )
    (taps,) = kernel_call(
        taps_kernel, [jax.ShapeDtypeStruct((WIDE // 4 + 8, WIDE), jnp.int32)], [], 8, 2_000_000_000
    )
    tall = 2 * analysis_truth.shape[3] == 8 * groups
    if halves == 2 and tall and expected_normal.shape[0] * expected_normal.shape[1] % 2 == 0:
        return two_chip_maps(model_prognosis, analysis_truth, expected_normal, taps, lon_weights, lat_weights)

    own = model_prognosis.reshape((-1,) + model_prognosis.shape[3:])
    own, to_cross, to_pair = edge_rows(own)
    across = [(i, min(max(i + (1 if i % 2 else -1), 0), bands - 1)) for i in range(bands)]
    paired = lax.ppermute(to_pair, "band", [(i, i ^ 1) for i in range(bands)])
    crossed = lax.ppermute(to_cross, "band", across)
    truth = analysis_truth.reshape((-1,) + analysis_truth.shape[3:])
    normal = expected_normal.reshape((-1,) + expected_normal.shape[2:])
    error, fine = error_map(own, crossed, paired, truth, taps, lon_weights, lat_weights, normal.shape[0], groups)
    anomaly = anomaly_map(fine, truth, normal, groups)

    def packed(values):
        return (values * CARRY_SCALE).astype(jnp.float16)

    def unpacked(values):
        return values.astype(jnp.float32) / CARRY_SCALE

    def row_block(values, index):
        return lax.dynamic_index_in_dim(values, index, 0, keepdims=False)

    def mean_over_dates(maps):
        swapped = lax.ppermute(packed(row_block(maps, 1 - core)), "date", [(i, i ^ 1) for i in range(groups)])

        def chip_sum(index):
            mine = lax.dynamic_slice(maps, (core, index, 0, 0, 0), (1, 1) + maps.shape[2:])[0, 0]
            return mine + unpacked(row_block(swapped, index))

        pieces = []
        for step in range(1, halves):
            piece = packed(chip_sum(lax.rem(half + step, halves)))
            ring = [(i, (i + 2 * step) % groups) for i in range(groups)]
            pieces.append(lax.ppermute(piece, "date", ring))
        total = chip_sum(half)
        for piece in pieces:
            total = total + unpacked(piece)
        total = total / (dates * groups)
        return total.reshape(expected_normal.shape[:2] + total.shape[1:])

    return (mean_over_dates(error), mean_over_dates(anomaly))


def solution(mesh):
    in_specs = (
        P("date", None, None, "band", None),
        P("date", None, None, "band", None),
        P(None, None, "band", None),
        P("band"),
        P("band", None),
        P(),
        P(),
    )
    out_specs = (P(None, None, ("band", "date"), None), P(None, None, ("band", "date"), None))
    return jax.shard_map(shards, mesh=mesh, in_specs=in_specs, out_specs=out_specs, check_vma=False)
```

```python
import functools

import jax
import jax.numpy as jnp
from jax import lax
from jax.experimental import pallas as pl
from jax.experimental.pallas import tpu as pltpu
from jax.sharding import PartitionSpec as P

TAPS = 4
LANES = 128
WIDE = 256
CARRY_SCALE = 16.0


def edges_kernel(own_ref, kept_ref, cross_ref, pair_ref):
    even = lax.rem(lax.axis_index("band"), 2) == 0
    for index in range(own_ref.shape[0]):
        kept_ref[index] = own_ref[index]
        rows = own_ref[index].astype(jnp.float32)
        bottom, top = rows[:2], rows[rows.shape[0] - 2 :]
        pair_ref[index] = jnp.where(even, top, bottom).astype(jnp.bfloat16)
        cross_ref[index] = jnp.where(even, bottom, top).astype(jnp.bfloat16)


def taps_kernel(tap_ref):
    row = lax.broadcasted_iota(jnp.int32, tap_ref.shape, 0)
    tap_ref[...] = row - lax.broadcasted_iota(jnp.int32, tap_ref.shape, 1) // 4


def fill_tables(tap_ref, lon_ref, table_ref):
    dense = lon_ref.shape[1]
    for tile in range(pl.cdiv(dense, WIDE)):
        low_x = tile * WIDE
        width = min(WIDE, dense - low_x)
        base = low_x // 4 % LANES
        rows = width // 4 + 8
        depth_here = LANES if base + rows <= LANES else 2 * LANES
        columns = slice(low_x, low_x + width)
        offset = tap_ref[:rows, :width] - lon_ref[TAPS : TAPS + 1, columns].astype(jnp.int32)
        block = jnp.zeros((rows, width), jnp.float32)
        for tap in range(TAPS):
            block = jnp.where(offset == tap, lon_ref[tap : tap + 1, columns], block)
        parts = [block]
        if base:
            parts.insert(0, jnp.zeros((base, width), jnp.float32))
        if depth_here > base + rows:
            parts.append(jnp.zeros((depth_here - base - rows, width), jnp.float32))
        table_ref[tile, :depth_here, :width] = jnp.concatenate(parts, axis=0).astype(jnp.bfloat16)


def widened(lhs_ref, table_ref, tile, low_x, width):
    base = low_x // 4 % LANES
    begin = low_x // 4 - base
    depth = LANES if base + width // 4 + 8 <= LANES else 2 * LANES
    lhs = jnp.concatenate([lhs_ref[0, :, begin : begin + depth], lhs_ref[1, :, begin : begin + depth]], axis=1)
    table = table_ref[tile, :depth, :width]
    return jnp.dot(lhs, jnp.concatenate([table, table], axis=0), preferred_element_type=jnp.float32)


def wrapped_rows(rows, depth):
    sparse = rows.shape[1]
    filler = jnp.zeros((rows.shape[0], depth - sparse - 4), jnp.float32)
    return jnp.concatenate([rows[:, sparse - 1 :], rows, rows[:, :3], filler], axis=1)


def error_kernel(
    own_ref,
    cross_ref,
    pair_ref,
    truth_ref,
    tap_ref,
    lon_ref,
    lat_ref,
    out_ref,
    fine_ref,
    lhs_ref,
    table_ref,
):
    fields, coarse_rows, sparse = own_ref.shape
    _, fine_rows, dense = truth_ref.shape
    pairs = out_ref.shape[2]
    dates = fields // pairs
    ratio = fine_rows // coarse_rows
    span = 8 // ratio
    depth = lhs_ref.shape[2]
    tiles = pl.cdiv(dense, WIDE)
    band = lax.axis_index("band")
    even = lax.rem(band, 2) == 0
    lowest = band == 0
    highest = band == lax.axis_size("band") - 1

    fill_tables(tap_ref, lon_ref, table_ref)

    weights = lat_ref[...].T
    lat = [
        [
            jnp.broadcast_to(weights[8 * group : 8 * group + 8, tap : tap + 1], (8, LANES))
            for tap in range(TAPS + 1)
        ]
        for group in range(fine_rows // 8)
    ]
    lat = [[jnp.concatenate([w] * (depth // LANES), axis=1) for w in group] for group in lat]

    upper_half = lax.broadcasted_iota(jnp.int32, (8, depth), 0) < ratio
    for pair in range(pairs):
        for date in range(dates):
            index = date * pairs + pair
            paired = pair_ref[index].astype(jnp.float32)
            crossed = cross_ref[index].astype(jnp.float32)
            low = jnp.where(lowest, 0.0, jnp.where(even, crossed, paired))
            high = jnp.where(highest, 0.0, jnp.where(even, paired, crossed))
            rows8 = jnp.concatenate([low, own_ref[index].astype(jnp.float32), high], axis=0)
            wrapped = wrapped_rows(rows8, depth)
            spread = [jnp.broadcast_to(wrapped[i : i + 1], (8, depth)) for i in range(coarse_rows + 4)]
            mixed = [jnp.where(upper_half, spread[i], spread[i + 1]) for i in range(coarse_rows + 3)]
            both = []
            for group in range(fine_rows // 8):
                total = lat[group][0] * mixed[span * group]
                for tap in range(1, TAPS + 1):
                    total = total + lat[group][tap] * mixed[span * group + tap]
                both.append(total)
            both = jnp.concatenate(both, axis=0)
            upper = both.astype(jnp.bfloat16)
            rest = (both - upper.astype(jnp.float32)).astype(jnp.bfloat16)
            at = (pair * dates + date) * fine_rows
            lhs_ref[0, at : at + fine_rows, :] = upper
            lhs_ref[1, at : at + fine_rows, :] = rest

    for tile in range(tiles):
        low_x = tile * WIDE
        width = min(WIDE, dense - low_x)
        columns = slice(low_x, low_x + width)
        fine_ref[:, columns] = widened(lhs_ref, table_ref, tile, low_x, width)
        for pair in range(pairs):
            total = 0.0
            for date in range(dates):
                at = (pair * dates + date) * fine_rows
                actual = truth_ref[date * pairs + pair, :, columns].astype(jnp.float32)
                error = fine_ref[at : at + fine_rows, columns] - actual
                total = total + error * error
            store_by_owner(out_ref, pair, columns, total)


def store_by_owner(out_ref, pair, columns, values):
    _, halves, _, owned, _ = out_ref.shape
    for owner in range(2 * halves):
        out_ref[owner % 2, owner // 2, pair, :, columns] = values[owner * owned : (owner + 1) * owned]


def anomaly_kernel(fine_ref, truth_ref, normal_ref, out_ref):
    fields, fine_rows, dense = truth_ref.shape
    pairs = normal_ref.shape[0]
    dates = fields // pairs
    for low_x in range(0, dense, WIDE):
        columns = slice(low_x, min(low_x + WIDE, dense))
        for pair in range(pairs):
            normal = normal_ref[pair, :, columns].astype(jnp.float32)
            total = 0.0
            for date in range(dates):
                at = (pair * dates + date) * fine_rows
                actual = truth_ref[date * pairs + pair, :, columns].astype(jnp.float32)
                total = total + (fine_ref[at : at + fine_rows, columns] - normal) * (actual - normal)
            store_by_owner(out_ref, pair, columns, total)


def edge_rows(own):
    fields, _, sparse = own.shape
    vmem = pl.BlockSpec(memory_space=pltpu.VMEM)
    edges = jax.ShapeDtypeStruct((fields, 2, sparse), jnp.bfloat16)
    return pl.pallas_call(
        edges_kernel,
        out_shape=[jax.ShapeDtypeStruct(own.shape, own.dtype), edges, edges],
        in_specs=[vmem],
        out_specs=[vmem] * 3,
        compiler_params=pltpu.CompilerParams(vmem_limit_bytes=8 * 1024 * 1024),
        cost_estimate=pl.CostEstimate(flops=100_000_000, bytes_accessed=200_000, transcendentals=0),
    )(own)


def lat_tap_weights(starts, weights, first_coarse, ratio):
    rows = starts.shape[0]
    late = starts > first_coarse + lax.iota(jnp.int32, rows) // ratio - 2
    by_tap = weights.T
    early = jnp.pad(by_tap, ((0, 8 - TAPS), (0, LANES - rows)))
    shifted = jnp.pad(by_tap, ((1, 7 - TAPS), (0, LANES - rows)))
    return jnp.where(jnp.pad(late, (0, LANES - rows))[None], shifted, early)


def error_map(own, crossed, paired, truth, taps, lon, lat, pairs, owners):
    fields, _, sparse = own.shape
    _, fine_rows, dense = truth.shape
    depth = pl.cdiv(sparse + 4, LANES) * LANES
    vmem = pl.BlockSpec(memory_space=pltpu.VMEM)
    return pl.pallas_call(
        error_kernel,
        out_shape=[
            jax.ShapeDtypeStruct((2, owners // 2, pairs, fine_rows // owners, dense), jnp.float32),
            jax.ShapeDtypeStruct((fields * fine_rows, dense), jnp.float32),
        ],
        in_specs=[vmem] * 7,
        out_specs=[vmem] * 2,
        scratch_shapes=[
            pltpu.VMEM((2, fields * fine_rows, depth), jnp.bfloat16),
            pltpu.VMEM((pl.cdiv(dense, WIDE), 2 * LANES, WIDE), jnp.bfloat16),
        ],
        compiler_params=pltpu.CompilerParams(vmem_limit_bytes=24 * 1024 * 1024),
        cost_estimate=pl.CostEstimate(flops=1_000_000_000, bytes_accessed=4_000_000, transcendentals=0),
    )(own, crossed, paired, truth, taps, lon, lat)


def anomaly_map(fine, truth, normal, owners):
    pairs, fine_rows, dense = normal.shape
    vmem = pl.BlockSpec(memory_space=pltpu.VMEM)
    return pl.pallas_call(
        anomaly_kernel,
        out_shape=jax.ShapeDtypeStruct((2, owners // 2, pairs, fine_rows // owners, dense), jnp.float32),
        in_specs=[vmem] * 3,
        out_specs=vmem,
        compiler_params=pltpu.CompilerParams(vmem_limit_bytes=24 * 1024 * 1024),
        cost_estimate=pl.CostEstimate(flops=500_000_000, bytes_accessed=4_000_000, transcendentals=0),
    )(fine, truth, normal)


def first_core():
    return lax.rem(lax.axis_index("date"), 2) == 0


def lower_chip():
    return lax.axis_index("date") < lax.axis_size("date") // 2


def by_owner(ref, entries, lower):
    blocks = [ref[entry] for entry in entries]
    half = blocks[0].shape[0] // 2
    blocks = [jnp.where(lower, block[:half], block[half:]) for block in blocks]
    owned = half // 2
    return (
        jnp.concatenate([block[:owned] for block in blocks], axis=0),
        jnp.concatenate([block[owned:] for block in blocks], axis=0),
    )


def packed_tiles(entries, dense):
    full, tail = divmod(dense, LANES)
    return entries * full + (pl.cdiv(entries, LANES // tail) if tail else 0)


def pack_rows(blocks, out_ref):
    rows, dense = blocks[0].shape
    full, tail = divmod(dense, LANES)
    for at, block in enumerate(blocks):
        for tile in range(full):
            out_ref[at * full + tile] = block[:, tile * LANES : (tile + 1) * LANES].astype(out_ref.dtype)
    if tail:
        share = LANES // tail
        tails = [block[:, full * LANES :] for block in blocks]
        tails += [jnp.zeros((rows, tail), blocks[0].dtype)] * (-len(tails) % share)
        filler = [jnp.zeros((rows, LANES - share * tail), blocks[0].dtype)] if LANES % tail else []
        for at in range(0, len(tails), share):
            joined = jnp.concatenate(tails[at : at + share] + filler, axis=1)
            out_ref[len(blocks) * full + at // share] = joined.astype(out_ref.dtype)


def unpacked_rows(ref, at, entries, dense, low_x, width):
    full, tail = divmod(dense, LANES)
    parts = [
        ref[at * full + tile].astype(jnp.float32)
        for tile in range(low_x // LANES, min((low_x + width) // LANES, full))
    ]
    if low_x + width > full * LANES:
        share = LANES // tail
        start = at % share * tail
        parts.append(ref[entries * full + at // share].astype(jnp.float32)[:, start : start + tail])
    return jnp.concatenate(parts, axis=1)


def tile_entries(pairs, dates):
    return [[date * pairs + pair, date * pairs + pair + 1] for pair in range(0, pairs, 2) for date in range(dates)]


def straight_kernel(dates, truth_ref, own_ref, _, out_ref, kept_ref):
    first = first_core()
    blocks = []
    for entries in tile_entries(truth_ref.shape[0] // dates, dates):
        one, two = by_owner(truth_ref, entries, jnp.logical_not(lower_chip()))
        blocks.append(jnp.where(first, one, two))
    pack_rows(blocks, out_ref)
    for index in range(own_ref.shape[0]):
        kept_ref[index] = own_ref[index]


def home_kernel(dates, truth_ref, normal_ref, _, crossed_ref, mine_ref, sibling_ref, normals_ref):
    pairs = normal_ref.shape[0]
    first = first_core()
    lower = lower_chip()
    crossed = []
    for at, entries in enumerate(tile_entries(pairs, dates)):
        one, two = by_owner(truth_ref, entries, jnp.logical_not(lower))
        crossed.append(jnp.where(first, two, one))
        one, two = by_owner(truth_ref, entries, lower)
        mine_ref[at] = jnp.where(first, one, two).astype(mine_ref.dtype)
        sibling_ref[at] = jnp.where(first, two, one).astype(sibling_ref.dtype)
    pack_rows(crossed, crossed_ref)
    for pair in range(0, pairs, 2):
        one, two = by_owner(normal_ref, [pair, pair + 1], lower)
        normals_ref[pair // 2] = jnp.where(first, one, two).astype(jnp.float32)


def shift_rows_kernel(own_ref, peer_ref, both_ref, rows_ref):
    lower = lower_chip()
    fields, coarse_rows, _ = own_ref.shape
    for index in range(2 * fields):
        block = (own_ref if index < fields else peer_ref)[index % fields]
        both_ref[index] = block
        block = block.astype(jnp.float32)
        rows_ref[index] = jnp.where(lower, block[coarse_rows - 2 :], block[:2]).astype(jnp.bfloat16)


def latitude_step(dates, coarse_ref, halo_ref, lat_ref, lhs_ref):
    fields = coarse_ref.shape[0] // 2
    pairs = fields // dates
    depth = lhs_ref.shape[2]
    rows = 2 * lhs_ref.shape[1] // (2 * fields)
    owned = rows // 2
    band = lax.axis_index("band")
    lower = lower_chip()
    first = first_core()
    outside = jnp.logical_or(
        jnp.logical_and(lower, band == 0),
        jnp.logical_and(jnp.logical_not(lower), band == lax.axis_size("band") - 1),
    )
    weights = lat_ref[...].T
    weights = jnp.where(lower, weights[: 2 * owned], weights[2 * owned : 4 * owned])
    weights = jnp.where(first, weights[:owned], weights[owned:])
    weights = jnp.concatenate([weights, weights], axis=0)
    lat = [jnp.broadcast_to(weights[:, tap : tap + 1], (rows, depth)) for tap in range(TAPS + 1)]
    first_pair = lax.broadcasted_iota(jnp.int32, (rows, depth), 0) < owned
    pending = []
    at = 0
    for side in range(2):
        for entries in tile_entries(pairs, dates):
            sources = []
            for entry in entries:
                index = side * fields + entry
                inner = coarse_ref[index].astype(jnp.float32)
                edge = jnp.where(outside, 0.0, halo_ref[index].astype(jnp.float32))
                below = jnp.concatenate([edge, inner], axis=0)
                above = jnp.concatenate([inner, edge], axis=0)
                wrapped = wrapped_rows(jnp.where(lower, below, above), depth)
                sources.append(jnp.where(first, wrapped[: TAPS + 1], wrapped[1 : TAPS + 2]))
            total = 0.0
            for tap in range(TAPS + 1):
                one, two = [jnp.broadcast_to(source[tap : tap + 1], (rows, depth)) for source in sources]
                total = total + lat[tap] * jnp.where(first_pair, one, two)
            pending.append(total)
            at += rows
            if len(pending) * rows == 16:
                block = jnp.concatenate(pending, axis=0)
                upper = block.astype(jnp.bfloat16)
                lhs_ref[0, at - 16 : at] = upper
                lhs_ref[1, at - 16 : at] = (block - upper.astype(jnp.float32)).astype(jnp.bfloat16)
                pending = []


def column_blocks(dense):
    for tile in range(pl.cdiv(dense, WIDE)):
        low_x = tile * WIDE
        width = min(WIDE, dense - low_x)
        yield tile, low_x, width, slice(low_x, low_x + width)


def added(sums, fine, actual, normal):
    error = fine - actual
    return sums[0] + error * error, sums[1] + (fine - normal) * (actual - normal)


def own_dates_kernel(
    coarse_ref,
    halo_ref,
    truth_ref,
    normals_ref,
    lat_ref,
    table_ref,
    sums_ref,
    away_ref,
    lhs_ref,
    fine_ref,
):
    tiles, rows, dense = truth_ref.shape
    dates = tiles // normals_ref.shape[0]
    latitude_step(dates, coarse_ref, halo_ref, lat_ref, lhs_ref)
    for tile, low_x, width, columns in column_blocks(dense):
        fine_ref[:, :width] = widened(lhs_ref, table_ref, tile, low_x, width)
        away_ref[:, columns] = fine_ref[tiles * rows :, :width]
        for pair in range(normals_ref.shape[0]):
            normal = normals_ref[pair, :, columns]
            sums = (0.0, 0.0)
            for at in range(pair * dates, (pair + 1) * dates):
                actual = truth_ref[at, :, columns].astype(jnp.float32)
                sums = added(sums, fine_ref[at * rows : (at + 1) * rows, :width], actual, normal)
            sums_ref[0, pair, :, columns], sums_ref[1, pair, :, columns] = sums


def sibling_dates_kernel(
    coarse_ref,
    halo_ref,
    truth_ref,
    normals_ref,
    lat_ref,
    table_ref,
    before_ref,
    straight_fine_ref,
    straight_ref,
    sums_ref,
    away_ref,
    lhs_ref,
    fine_ref,
):
    tiles, rows, dense = truth_ref.shape
    dates = tiles // normals_ref.shape[0]
    latitude_step(dates, coarse_ref, halo_ref, lat_ref, lhs_ref)
    for tile, low_x, width, columns in column_blocks(dense):
        fine_ref[:, :width] = widened(lhs_ref, table_ref, tile, low_x, width)
        away_ref[:, columns] = fine_ref[tiles * rows :, :width]
        for pair in range(normals_ref.shape[0]):
            normal = normals_ref[pair, :, columns]
            sums = (before_ref[0, pair, :, columns], before_ref[1, pair, :, columns])
            for at in range(pair * dates, (pair + 1) * dates):
                span = slice(at * rows, (at + 1) * rows)
                actual = truth_ref[at, :, columns].astype(jnp.float32)
                sums = added(sums, fine_ref[span, :width], actual, normal)
                actual = unpacked_rows(straight_ref, at, tiles, dense, low_x, width)
                sums = added(sums, straight_fine_ref[span, columns], actual, normal)
            sums_ref[0, pair, :, columns], sums_ref[1, pair, :, columns] = sums


def mean_kernel(dates, count, before_ref, fine_ref, crossed_ref, normals_ref, *refs):
    *results, held_ref, sems = refs
    tiles, rows, dense = normals_ref.shape
    owned = rows // 2
    copies = []
    for pair in range(tiles):
        for _, low_x, width, columns in column_blocks(dense):
            normal = normals_ref[pair, :, columns]
            sums = (before_ref[0, pair, :, columns], before_ref[1, pair, :, columns])
            for at in range(pair * dates, (pair + 1) * dates):
                actual = unpacked_rows(crossed_ref, at, tiles * dates, dense, low_x, width)
                sums = added(sums, fine_ref[at * rows : (at + 1) * rows, columns], actual, normal)
            for kind, total in enumerate(sums):
                total = total * (1.0 / count)
                held_ref[kind, 2 * pair, :, columns] = total[:owned]
                held_ref[kind, 2 * pair + 1, :, columns] = total[owned:]
        done = pl.ds(2 * pair, 2)
        for kind, out_ref in enumerate(results):
            copy = pltpu.make_async_copy(held_ref.at[kind, done], out_ref.at[done], sems.at[len(copies)])
            copy.start()
            copies.append(copy)
    for copy in copies:
        copy.wait()


def kernel_call(kernel, out_shape, scratch, megabytes, flops, *operands, out_space=pltpu.VMEM):
    vmem = pl.BlockSpec(memory_space=pltpu.VMEM)
    return pl.pallas_call(
        kernel,
        out_shape=out_shape,
        in_specs=[vmem] * len(operands),
        out_specs=[pl.BlockSpec(memory_space=out_space)] * len(out_shape),
        scratch_shapes=scratch,
        compiler_params=pltpu.CompilerParams(vmem_limit_bytes=megabytes * 1024 * 1024),
        cost_estimate=pl.CostEstimate(flops=flops, bytes_accessed=0, transcendentals=0),
    )(*operands)


def two_chip_maps(model_prognosis, analysis_truth, expected_normal, taps, lon_weights, lat_weights):
    bands = lax.axis_size("band")
    groups = lax.axis_size("date")
    dates, leads, variables, coarse_rows, sparse = model_prognosis.shape
    fine_rows, dense = analysis_truth.shape[3:]
    owned = fine_rows // groups
    rows = 2 * owned
    pairs = leads * variables
    fields = dates * pairs
    tiles = fields // 2
    depth = pl.cdiv(sparse + 4, LANES) * LANES
    float32, bfloat16 = jnp.float32, jnp.bfloat16
    straight_way = [(i, (i + 2) % groups) for i in range(groups)]
    crossed_way = [(i, (i + 2) % groups ^ 1) for i in range(groups)]
    sibling_way = [(i, i ^ 1) for i in range(groups)]

    own = model_prognosis.reshape(fields, coarse_rows, sparse)
    truth = analysis_truth.reshape(fields, fine_rows, dense)
    normal = expected_normal.reshape(pairs, fine_rows, dense)
    peer = lax.ppermute(model_prognosis, "date", straight_way).reshape(own.shape)

    packed = jax.ShapeDtypeStruct((packed_tiles(tiles, dense), rows, LANES), bfloat16)
    straight, own = kernel_call(
        functools.partial(straight_kernel, dates),
        [packed, jax.ShapeDtypeStruct(own.shape, own.dtype)],
        [],
        8,
        100_000_000,
        truth,
        own,
        taps,
    )
    straight = lax.ppermute(straight, "date", straight_way)
    plain = jax.ShapeDtypeStruct((tiles, rows, dense), bfloat16)
    crossed, mine, sibling, normals = kernel_call(
        functools.partial(home_kernel, dates),
        [packed, plain, plain, jax.ShapeDtypeStruct((pairs // 2, rows, dense), float32)],
        [],
        12,
        100_000_000,
        truth,
        normal,
        own,
    )
    crossed = lax.ppermute(crossed, "date", crossed_way)
    sibling = lax.ppermute(sibling, "date", sibling_way)

    chain = []
    for group in range(groups):
        for band in range(bands):
            to = band + (1 if group < groups // 2 else -1)
            if 0 <= to < bands:
                chain.append((group * bands + band, group * bands + to))
    coarse, edges = kernel_call(
        shift_rows_kernel,
        [
            jax.ShapeDtypeStruct((2 * fields, coarse_rows, sparse), bfloat16),
            jax.ShapeDtypeStruct((2 * fields, 2, sparse), bfloat16),
        ],
        [],
        8,
        100_000_000,
        own,
        peer,
    )
    halo = lax.ppermute(edges, ("date", "band"), chain)
    sibling_coarse = lax.ppermute(coarse, "date", sibling_way)
    sibling_halo = lax.ppermute(halo, "date", sibling_way)

    sums = jax.ShapeDtypeStruct((2, pairs // 2, rows, dense), float32)
    away = jax.ShapeDtypeStruct((tiles * rows, dense), float32)
    table = jax.ShapeDtypeStruct((pl.cdiv(dense, WIDE), 2 * LANES, WIDE), bfloat16)
    scratch = [
        pltpu.VMEM((2, 2 * tiles * rows, depth), bfloat16),
        pltpu.VMEM((2 * tiles * rows, WIDE), float32),
    ]
    (table,) = kernel_call(fill_tables, [table], [], 8, 4_000_000_000, taps, lon_weights)
    own_sums, straight_fine = kernel_call(
        own_dates_kernel,
        [sums, away],
        scratch,
        20,
        0,
        coarse,
        halo,
        mine,
        normals,
        lat_weights,
        table,
    )
    chip_sums, crossed_fine = kernel_call(
        sibling_dates_kernel,
        [sums, away],
        scratch,
        20,
        0,
        sibling_coarse,
        sibling_halo,
        sibling,
        normals,
        lat_weights,
        table,
        own_sums,
        straight_fine,
        straight,
    )
    out = jax.ShapeDtypeStruct((pairs, owned, dense), float32)
    results = kernel_call(
        functools.partial(mean_kernel, dates, dates * groups),
        [out, out],
        [pltpu.VMEM((2,) + out.shape, float32), pltpu.SemaphoreType.DMA((pairs,))],
        16,
        0,
        chip_sums,
        crossed_fine,
        crossed,
        normals,
        out_space=pl.ANY,
    )
    return tuple(result.reshape(leads, variables, owned, dense) for result in results)


def shards(
    model_prognosis,
    analysis_truth,
    expected_normal,
    parallel_first_indices,
    parallel_blend_factors,
    meridian_first_indices,
    meridian_blend_factors,
):
    bands = lax.axis_size("band")
    groups = lax.axis_size("date")
    halves = groups // 2
    dates = model_prognosis.shape[0]
    group = lax.axis_index("date")
    core = lax.rem(group, 2)
    half = lax.div(group, 2)

    coarse_rows = model_prognosis.shape[3]
    lat_weights = lat_tap_weights(
        parallel_first_indices,
        parallel_blend_factors,
        lax.axis_index("band") * coarse_rows,
        analysis_truth.shape[3] // coarse_rows,
    )
    dense = meridian_first_indices.shape[0]
    late = meridian_first_indices == lax.iota(jnp.int32, dense) // 4
    lon_weights = jnp.where(
        lax.broadcasted_iota(jnp.int32, (8, dense), 0) < TAPS,
        jnp.pad(meridian_blend_factors, ((0, 8 - TAPS), (0, 0))).astype(jnp.float32),
        late.astype(jnp.float32)[None],
    )
    (taps,) = kernel_call(
        taps_kernel, [jax.ShapeDtypeStruct((WIDE // 4 + 8, WIDE), jnp.int32)], [], 8, 2_000_000_000
    )
    tall = 2 * analysis_truth.shape[3] == 8 * groups
    if halves == 2 and tall and expected_normal.shape[0] * expected_normal.shape[1] % 2 == 0:
        return two_chip_maps(model_prognosis, analysis_truth, expected_normal, taps, lon_weights, lat_weights)

    own = model_prognosis.reshape((-1,) + model_prognosis.shape[3:])
    own, to_cross, to_pair = edge_rows(own)
    across = [(i, min(max(i + (1 if i % 2 else -1), 0), bands - 1)) for i in range(bands)]
    paired = lax.ppermute(to_pair, "band", [(i, i ^ 1) for i in range(bands)])
    crossed = lax.ppermute(to_cross, "band", across)
    truth = analysis_truth.reshape((-1,) + analysis_truth.shape[3:])
    normal = expected_normal.reshape((-1,) + expected_normal.shape[2:])
    error, fine = error_map(own, crossed, paired, truth, taps, lon_weights, lat_weights, normal.shape[0], groups)
    anomaly = anomaly_map(fine, truth, normal, groups)

    def packed(values):
        return (values * CARRY_SCALE).astype(jnp.float16)

    def unpacked(values):
        return values.astype(jnp.float32) / CARRY_SCALE

    def row_block(values, index):
        return lax.dynamic_index_in_dim(values, index, 0, keepdims=False)

    def mean_over_dates(maps):
        swapped = lax.ppermute(packed(row_block(maps, 1 - core)), "date", [(i, i ^ 1) for i in range(groups)])

        def chip_sum(index):
            mine = lax.dynamic_slice(maps, (core, index, 0, 0, 0), (1, 1) + maps.shape[2:])[0, 0]
            return mine + unpacked(row_block(swapped, index))

        pieces = []
        for step in range(1, halves):
            piece = packed(chip_sum(lax.rem(half + step, halves)))
            ring = [(i, (i + 2 * step) % groups) for i in range(groups)]
            pieces.append(lax.ppermute(piece, "date", ring))
        total = chip_sum(half)
        for piece in pieces:
            total = total + unpacked(piece)
        total = total / (dates * groups)
        return total.reshape(expected_normal.shape[:2] + total.shape[1:])

    return (mean_over_dates(error), mean_over_dates(anomaly))


def solution(mesh):
    in_specs = (
        P("date", None, None, "band", None),
        P("date", None, None, "band", None),
        P(None, None, "band", None),
        P("band"),
        P("band", None),
        P(),
        P(),
    )
    out_specs = (P(None, None, ("band", "date"), None), P(None, None, ("band", "date"), None))
    return jax.shard_map(shards, mesh=mesh, in_specs=in_specs, out_specs=out_specs, check_vma=False)
```

```python
import functools

import jax
import jax.numpy as jnp
from jax import lax
from jax.experimental import pallas as pl
from jax.experimental.pallas import tpu as pltpu
from jax.sharding import PartitionSpec as P

TAPS = 4
LANES = 128
WIDE = 256
CARRY_SCALE = 16.0


def edges_kernel(own_ref, kept_ref, cross_ref, pair_ref):
    even = lax.rem(lax.axis_index("band"), 2) == 0
    for index in range(own_ref.shape[0]):
        kept_ref[index] = own_ref[index]
        rows = own_ref[index].astype(jnp.float32)
        bottom, top = rows[:2], rows[rows.shape[0] - 2 :]
        pair_ref[index] = jnp.where(even, top, bottom).astype(jnp.bfloat16)
        cross_ref[index] = jnp.where(even, bottom, top).astype(jnp.bfloat16)


def taps_kernel(tap_ref):
    row = lax.broadcasted_iota(jnp.int32, tap_ref.shape, 0)
    tap_ref[...] = row - lax.broadcasted_iota(jnp.int32, tap_ref.shape, 1) // 4


def fill_tables(tap_ref, lon_ref, table_ref):
    dense = lon_ref.shape[1]
    for tile in range(pl.cdiv(dense, WIDE)):
        low_x = tile * WIDE
        width = min(WIDE, dense - low_x)
        base = low_x // 4 % LANES
        rows = width // 4 + 8
        depth_here = LANES if base + rows <= LANES else 2 * LANES
        columns = slice(low_x, low_x + width)
        offset = tap_ref[:rows, :width] - lon_ref[TAPS : TAPS + 1, columns].astype(jnp.int32)
        block = jnp.zeros((rows, width), jnp.float32)
        for tap in range(TAPS):
            block = jnp.where(offset == tap, lon_ref[tap : tap + 1, columns], block)
        parts = [block]
        if base:
            parts.insert(0, jnp.zeros((base, width), jnp.float32))
        if depth_here > base + rows:
            parts.append(jnp.zeros((depth_here - base - rows, width), jnp.float32))
        table_ref[tile, :depth_here, :width] = jnp.concatenate(parts, axis=0).astype(jnp.bfloat16)


def widened(lhs_ref, table_ref, tile, low_x, width):
    base = low_x // 4 % LANES
    begin = low_x // 4 - base
    depth = LANES if base + width // 4 + 8 <= LANES else 2 * LANES
    lhs = jnp.concatenate([lhs_ref[0, :, begin : begin + depth], lhs_ref[1, :, begin : begin + depth]], axis=1)
    table = table_ref[tile, :depth, :width]
    return jnp.dot(lhs, jnp.concatenate([table, table], axis=0), preferred_element_type=jnp.float32)


def wrapped_rows(rows, depth):
    sparse = rows.shape[1]
    filler = jnp.zeros((rows.shape[0], depth - sparse - 4), jnp.float32)
    return jnp.concatenate([rows[:, sparse - 1 :], rows, rows[:, :3], filler], axis=1)


def error_kernel(
    own_ref,
    cross_ref,
    pair_ref,
    truth_ref,
    tap_ref,
    lon_ref,
    lat_ref,
    out_ref,
    fine_ref,
    lhs_ref,
    table_ref,
):
    fields, coarse_rows, sparse = own_ref.shape
    _, fine_rows, dense = truth_ref.shape
    pairs = out_ref.shape[2]
    dates = fields // pairs
    ratio = fine_rows // coarse_rows
    span = 8 // ratio
    depth = lhs_ref.shape[2]
    tiles = pl.cdiv(dense, WIDE)
    band = lax.axis_index("band")
    even = lax.rem(band, 2) == 0
    lowest = band == 0
    highest = band == lax.axis_size("band") - 1

    fill_tables(tap_ref, lon_ref, table_ref)

    weights = lat_ref[...].T
    lat = [
        [
            jnp.broadcast_to(weights[8 * group : 8 * group + 8, tap : tap + 1], (8, LANES))
            for tap in range(TAPS + 1)
        ]
        for group in range(fine_rows // 8)
    ]
    lat = [[jnp.concatenate([w] * (depth // LANES), axis=1) for w in group] for group in lat]

    upper_half = lax.broadcasted_iota(jnp.int32, (8, depth), 0) < ratio
    for pair in range(pairs):
        for date in range(dates):
            index = date * pairs + pair
            paired = pair_ref[index].astype(jnp.float32)
            crossed = cross_ref[index].astype(jnp.float32)
            low = jnp.where(lowest, 0.0, jnp.where(even, crossed, paired))
            high = jnp.where(highest, 0.0, jnp.where(even, paired, crossed))
            rows8 = jnp.concatenate([low, own_ref[index].astype(jnp.float32), high], axis=0)
            wrapped = wrapped_rows(rows8, depth)
            spread = [jnp.broadcast_to(wrapped[i : i + 1], (8, depth)) for i in range(coarse_rows + 4)]
            mixed = [jnp.where(upper_half, spread[i], spread[i + 1]) for i in range(coarse_rows + 3)]
            both = []
            for group in range(fine_rows // 8):
                total = lat[group][0] * mixed[span * group]
                for tap in range(1, TAPS + 1):
                    total = total + lat[group][tap] * mixed[span * group + tap]
                both.append(total)
            both = jnp.concatenate(both, axis=0)
            upper = both.astype(jnp.bfloat16)
            rest = (both - upper.astype(jnp.float32)).astype(jnp.bfloat16)
            at = (pair * dates + date) * fine_rows
            lhs_ref[0, at : at + fine_rows, :] = upper
            lhs_ref[1, at : at + fine_rows, :] = rest

    for tile in range(tiles):
        low_x = tile * WIDE
        width = min(WIDE, dense - low_x)
        columns = slice(low_x, low_x + width)
        fine_ref[:, columns] = widened(lhs_ref, table_ref, tile, low_x, width)
        for pair in range(pairs):
            total = 0.0
            for date in range(dates):
                at = (pair * dates + date) * fine_rows
                actual = truth_ref[date * pairs + pair, :, columns].astype(jnp.float32)
                error = fine_ref[at : at + fine_rows, columns] - actual
                total = total + error * error
            store_by_owner(out_ref, pair, columns, total)


def store_by_owner(out_ref, pair, columns, values):
    _, halves, _, owned, _ = out_ref.shape
    for owner in range(2 * halves):
        out_ref[owner % 2, owner // 2, pair, :, columns] = values[owner * owned : (owner + 1) * owned]


def anomaly_kernel(fine_ref, truth_ref, normal_ref, out_ref):
    fields, fine_rows, dense = truth_ref.shape
    pairs = normal_ref.shape[0]
    dates = fields // pairs
    for low_x in range(0, dense, WIDE):
        columns = slice(low_x, min(low_x + WIDE, dense))
        for pair in range(pairs):
            normal = normal_ref[pair, :, columns].astype(jnp.float32)
            total = 0.0
            for date in range(dates):
                at = (pair * dates + date) * fine_rows
                actual = truth_ref[date * pairs + pair, :, columns].astype(jnp.float32)
                total = total + (fine_ref[at : at + fine_rows, columns] - normal) * (actual - normal)
            store_by_owner(out_ref, pair, columns, total)


def edge_rows(own):
    fields, _, sparse = own.shape
    vmem = pl.BlockSpec(memory_space=pltpu.VMEM)
    edges = jax.ShapeDtypeStruct((fields, 2, sparse), jnp.bfloat16)
    return pl.pallas_call(
        edges_kernel,
        out_shape=[jax.ShapeDtypeStruct(own.shape, own.dtype), edges, edges],
        in_specs=[vmem],
        out_specs=[vmem] * 3,
        compiler_params=pltpu.CompilerParams(vmem_limit_bytes=8 * 1024 * 1024),
        cost_estimate=pl.CostEstimate(flops=100_000_000, bytes_accessed=200_000, transcendentals=0),
    )(own)


def lat_tap_weights(starts, weights, first_coarse, ratio):
    rows = starts.shape[0]
    late = starts > first_coarse + lax.iota(jnp.int32, rows) // ratio - 2
    by_tap = weights.T
    early = jnp.pad(by_tap, ((0, 8 - TAPS), (0, LANES - rows)))
    shifted = jnp.pad(by_tap, ((1, 7 - TAPS), (0, LANES - rows)))
    return jnp.where(jnp.pad(late, (0, LANES - rows))[None], shifted, early)


def error_map(own, crossed, paired, truth, taps, lon, lat, pairs, owners):
    fields, _, sparse = own.shape
    _, fine_rows, dense = truth.shape
    depth = pl.cdiv(sparse + 4, LANES) * LANES
    vmem = pl.BlockSpec(memory_space=pltpu.VMEM)
    return pl.pallas_call(
        error_kernel,
        out_shape=[
            jax.ShapeDtypeStruct((2, owners // 2, pairs, fine_rows // owners, dense), jnp.float32),
            jax.ShapeDtypeStruct((fields * fine_rows, dense), jnp.float32),
        ],
        in_specs=[vmem] * 7,
        out_specs=[vmem] * 2,
        scratch_shapes=[
            pltpu.VMEM((2, fields * fine_rows, depth), jnp.bfloat16),
            pltpu.VMEM((pl.cdiv(dense, WIDE), 2 * LANES, WIDE), jnp.bfloat16),
        ],
        compiler_params=pltpu.CompilerParams(vmem_limit_bytes=24 * 1024 * 1024),
        cost_estimate=pl.CostEstimate(flops=1_000_000_000, bytes_accessed=4_000_000, transcendentals=0),
    )(own, crossed, paired, truth, taps, lon, lat)


def anomaly_map(fine, truth, normal, owners):
    pairs, fine_rows, dense = normal.shape
    vmem = pl.BlockSpec(memory_space=pltpu.VMEM)
    return pl.pallas_call(
        anomaly_kernel,
        out_shape=jax.ShapeDtypeStruct((2, owners // 2, pairs, fine_rows // owners, dense), jnp.float32),
        in_specs=[vmem] * 3,
        out_specs=vmem,
        compiler_params=pltpu.CompilerParams(vmem_limit_bytes=24 * 1024 * 1024),
        cost_estimate=pl.CostEstimate(flops=500_000_000, bytes_accessed=4_000_000, transcendentals=0),
    )(fine, truth, normal)


def first_core():
    return lax.rem(lax.axis_index("date"), 2) == 0


def lower_chip():
    return lax.axis_index("date") < lax.axis_size("date") // 2


def by_owner(ref, entries, lower):
    blocks = [ref[entry] for entry in entries]
    half = blocks[0].shape[0] // 2
    blocks = [jnp.where(lower, block[:half], block[half:]) for block in blocks]
    owned = half // 2
    return (
        jnp.concatenate([block[:owned] for block in blocks], axis=0),
        jnp.concatenate([block[owned:] for block in blocks], axis=0),
    )


def packed_tiles(entries, dense):
    full, tail = divmod(dense, LANES)
    return entries * full + (pl.cdiv(entries, LANES // tail) if tail else 0)


def pack_rows(blocks, out_ref):
    rows, dense = blocks[0].shape
    full, tail = divmod(dense, LANES)
    for at, block in enumerate(blocks):
        for tile in range(full):
            out_ref[at * full + tile] = block[:, tile * LANES : (tile + 1) * LANES].astype(out_ref.dtype)
    if tail:
        share = LANES // tail
        tails = [block[:, full * LANES :] for block in blocks]
        tails += [jnp.zeros((rows, tail), blocks[0].dtype)] * (-len(tails) % share)
        filler = [jnp.zeros((rows, LANES - share * tail), blocks[0].dtype)] if LANES % tail else []
        for at in range(0, len(tails), share):
            joined = jnp.concatenate(tails[at : at + share] + filler, axis=1)
            out_ref[len(blocks) * full + at // share] = joined.astype(out_ref.dtype)


def unpacked_rows(ref, at, entries, dense, low_x, width):
    full, tail = divmod(dense, LANES)
    parts = [
        ref[at * full + tile].astype(jnp.float32)
        for tile in range(low_x // LANES, min((low_x + width) // LANES, full))
    ]
    if low_x + width > full * LANES:
        share = LANES // tail
        start = at % share * tail
        parts.append(ref[entries * full + at // share].astype(jnp.float32)[:, start : start + tail])
    return jnp.concatenate(parts, axis=1)


def tile_entries(pairs, dates):
    return [[date * pairs + pair, date * pairs + pair + 1] for pair in range(0, pairs, 2) for date in range(dates)]


def straight_kernel(dates, truth_ref, own_ref, _, out_ref, kept_ref):
    first = first_core()
    blocks = []
    for entries in tile_entries(truth_ref.shape[0] // dates, dates):
        one, two = by_owner(truth_ref, entries, jnp.logical_not(lower_chip()))
        blocks.append(jnp.where(first, one, two))
    pack_rows(blocks, out_ref)
    for index in range(own_ref.shape[0]):
        kept_ref[index] = own_ref[index]


def home_kernel(dates, truth_ref, normal_ref, _, crossed_ref, mine_ref, sibling_ref, normals_ref):
    pairs = normal_ref.shape[0]
    first = first_core()
    lower = lower_chip()
    crossed = []
    for at, entries in enumerate(tile_entries(pairs, dates)):
        one, two = by_owner(truth_ref, entries, jnp.logical_not(lower))
        crossed.append(jnp.where(first, two, one))
        one, two = by_owner(truth_ref, entries, lower)
        mine_ref[at] = jnp.where(first, one, two).astype(mine_ref.dtype)
        sibling_ref[at] = jnp.where(first, two, one).astype(sibling_ref.dtype)
    pack_rows(crossed, crossed_ref)
    for pair in range(0, pairs, 2):
        one, two = by_owner(normal_ref, [pair, pair + 1], lower)
        normals_ref[pair // 2] = jnp.where(first, one, two).astype(jnp.float32)


def shift_rows_kernel(own_ref, peer_ref, both_ref, rows_ref):
    lower = lower_chip()
    fields, coarse_rows, _ = own_ref.shape
    depth = both_ref.shape[2]
    for index in range(2 * fields):
        block = (own_ref if index < fields else peer_ref)[index % fields].astype(jnp.float32)
        block = wrapped_rows(block, depth)
        both_ref[index] = block.astype(both_ref.dtype)
        rows_ref[index] = jnp.where(lower, block[coarse_rows - 2 :], block[:2]).astype(jnp.bfloat16)


def latitude_step(dates, coarse_ref, halo_ref, lat_ref, lhs_ref):
    fields = coarse_ref.shape[0] // 2
    pairs = fields // dates
    depth = lhs_ref.shape[2]
    rows = 2 * lhs_ref.shape[1] // (2 * fields)
    owned = rows // 2
    band = lax.axis_index("band")
    lower = lower_chip()
    first = first_core()
    outside = jnp.logical_or(
        jnp.logical_and(lower, band == 0),
        jnp.logical_and(jnp.logical_not(lower), band == lax.axis_size("band") - 1),
    )
    weights = lat_ref[...].T
    weights = jnp.where(lower, weights[: 2 * owned], weights[2 * owned : 4 * owned])
    weights = jnp.where(first, weights[:owned], weights[owned:])
    weights = jnp.concatenate([weights, weights], axis=0)
    lat = [jnp.broadcast_to(weights[:, tap : tap + 1], (rows, depth)) for tap in range(TAPS + 1)]
    first_pair = lax.broadcasted_iota(jnp.int32, (rows, depth), 0) < owned
    pending = []
    at = 0
    for side in range(2):
        for entries in tile_entries(pairs, dates):
            sources = []
            for entry in entries:
                index = side * fields + entry
                inner = coarse_ref[index].astype(jnp.float32)
                edge = jnp.where(outside, 0.0, halo_ref[index].astype(jnp.float32))
                below = jnp.concatenate([edge, inner], axis=0)
                above = jnp.concatenate([inner, edge], axis=0)
                wrapped = jnp.where(lower, below, above)
                sources.append(jnp.where(first, wrapped[: TAPS + 1], wrapped[1 : TAPS + 2]))
            total = 0.0
            for tap in range(TAPS + 1):
                one, two = [jnp.broadcast_to(source[tap : tap + 1], (rows, depth)) for source in sources]
                total = total + lat[tap] * jnp.where(first_pair, one, two)
            pending.append(total)
            at += rows
            if len(pending) * rows == 16:
                block = jnp.concatenate(pending, axis=0)
                upper = block.astype(jnp.bfloat16)
                lhs_ref[0, at - 16 : at] = upper
                lhs_ref[1, at - 16 : at] = (block - upper.astype(jnp.float32)).astype(jnp.bfloat16)
                pending = []


def column_blocks(dense):
    for tile in range(pl.cdiv(dense, WIDE)):
        low_x = tile * WIDE
        width = min(WIDE, dense - low_x)
        yield tile, low_x, width, slice(low_x, low_x + width)


def added(sums, fine, actual, normal):
    error = fine - actual
    return sums[0] + error * error, sums[1] + (fine - normal) * (actual - normal)


def own_dates_kernel(
    coarse_ref,
    halo_ref,
    truth_ref,
    normals_ref,
    lat_ref,
    table_ref,
    sums_ref,
    away_ref,
    lhs_ref,
    fine_ref,
):
    tiles, rows, dense = truth_ref.shape
    dates = tiles // normals_ref.shape[0]
    latitude_step(dates, coarse_ref, halo_ref, lat_ref, lhs_ref)
    for tile, low_x, width, columns in column_blocks(dense):
        fine_ref[:, :width] = widened(lhs_ref, table_ref, tile, low_x, width)
        away_ref[:, columns] = fine_ref[tiles * rows :, :width]
        for pair in range(normals_ref.shape[0]):
            normal = normals_ref[pair, :, columns]
            sums = (0.0, 0.0)
            for at in range(pair * dates, (pair + 1) * dates):
                actual = truth_ref[at, :, columns].astype(jnp.float32)
                sums = added(sums, fine_ref[at * rows : (at + 1) * rows, :width], actual, normal)
            sums_ref[0, pair, :, columns], sums_ref[1, pair, :, columns] = sums


def sibling_dates_kernel(
    coarse_ref,
    halo_ref,
    truth_ref,
    normals_ref,
    lat_ref,
    table_ref,
    before_ref,
    straight_fine_ref,
    straight_ref,
    sums_ref,
    away_ref,
    lhs_ref,
    fine_ref,
):
    tiles, rows, dense = truth_ref.shape
    dates = tiles // normals_ref.shape[0]
    latitude_step(dates, coarse_ref, halo_ref, lat_ref, lhs_ref)
    for tile, low_x, width, columns in column_blocks(dense):
        fine_ref[:, :width] = widened(lhs_ref, table_ref, tile, low_x, width)
        away_ref[:, columns] = fine_ref[tiles * rows :, :width]
        for pair in range(normals_ref.shape[0]):
            normal = normals_ref[pair, :, columns]
            sums = (before_ref[0, pair, :, columns], before_ref[1, pair, :, columns])
            for at in range(pair * dates, (pair + 1) * dates):
                span = slice(at * rows, (at + 1) * rows)
                actual = truth_ref[at, :, columns].astype(jnp.float32)
                sums = added(sums, fine_ref[span, :width], actual, normal)
                actual = unpacked_rows(straight_ref, at, tiles, dense, low_x, width)
                sums = added(sums, straight_fine_ref[span, columns], actual, normal)
            sums_ref[0, pair, :, columns], sums_ref[1, pair, :, columns] = sums


def mean_kernel(dates, count, before_ref, fine_ref, crossed_ref, normals_ref, *refs):
    *results, held_ref, sems = refs
    tiles, rows, dense = normals_ref.shape
    owned = rows // 2
    copies = []
    for pair in range(tiles):
        for _, low_x, width, columns in column_blocks(dense):
            normal = normals_ref[pair, :, columns]
            sums = (before_ref[0, pair, :, columns], before_ref[1, pair, :, columns])
            for at in range(pair * dates, (pair + 1) * dates):
                actual = unpacked_rows(crossed_ref, at, tiles * dates, dense, low_x, width)
                sums = added(sums, fine_ref[at * rows : (at + 1) * rows, columns], actual, normal)
            for kind, total in enumerate(sums):
                total = total * (1.0 / count)
                held_ref[kind, 2 * pair, :, columns] = total[:owned]
                held_ref[kind, 2 * pair + 1, :, columns] = total[owned:]
        done = pl.ds(2 * pair, 2)
        for kind, out_ref in enumerate(results):
            copy = pltpu.make_async_copy(held_ref.at[kind, done], out_ref.at[done], sems.at[len(copies)])
            copy.start()
            copies.append(copy)
    for copy in copies:
        copy.wait()


def kernel_call(kernel, out_shape, scratch, megabytes, flops, *operands, out_space=pltpu.VMEM):
    vmem = pl.BlockSpec(memory_space=pltpu.VMEM)
    return pl.pallas_call(
        kernel,
        out_shape=out_shape,
        in_specs=[vmem] * len(operands),
        out_specs=[pl.BlockSpec(memory_space=out_space)] * len(out_shape),
        scratch_shapes=scratch,
        compiler_params=pltpu.CompilerParams(vmem_limit_bytes=megabytes * 1024 * 1024),
        cost_estimate=pl.CostEstimate(flops=flops, bytes_accessed=0, transcendentals=0),
    )(*operands)


def two_chip_maps(model_prognosis, analysis_truth, expected_normal, taps, lon_weights, lat_weights):
    bands = lax.axis_size("band")
    groups = lax.axis_size("date")
    dates, leads, variables, coarse_rows, sparse = model_prognosis.shape
    fine_rows, dense = analysis_truth.shape[3:]
    owned = fine_rows // groups
    rows = 2 * owned
    pairs = leads * variables
    fields = dates * pairs
    tiles = fields // 2
    depth = pl.cdiv(sparse + 4, LANES) * LANES
    float32, bfloat16 = jnp.float32, jnp.bfloat16
    straight_way = [(i, (i + 2) % groups) for i in range(groups)]
    crossed_way = [(i, (i + 2) % groups ^ 1) for i in range(groups)]
    sibling_way = [(i, i ^ 1) for i in range(groups)]

    own = model_prognosis.reshape(fields, coarse_rows, sparse)
    truth = analysis_truth.reshape(fields, fine_rows, dense)
    normal = expected_normal.reshape(pairs, fine_rows, dense)
    peer = lax.ppermute(model_prognosis, "date", straight_way).reshape(own.shape)

    packed = jax.ShapeDtypeStruct((packed_tiles(tiles, dense), rows, LANES), bfloat16)
    straight, own = kernel_call(
        functools.partial(straight_kernel, dates),
        [packed, jax.ShapeDtypeStruct(own.shape, own.dtype)],
        [],
        8,
        100_000_000,
        truth,
        own,
        taps,
    )
    straight = lax.ppermute(straight, "date", straight_way)
    plain = jax.ShapeDtypeStruct((tiles, rows, dense), bfloat16)
    crossed, mine, sibling, normals = kernel_call(
        functools.partial(home_kernel, dates),
        [packed, plain, plain, jax.ShapeDtypeStruct((pairs // 2, rows, dense), float32)],
        [],
        12,
        100_000_000,
        truth,
        normal,
        own,
    )
    crossed = lax.ppermute(crossed, "date", crossed_way)
    sibling = lax.ppermute(sibling, "date", sibling_way)

    chain = []
    for group in range(groups):
        for band in range(bands):
            to = band + (1 if group < groups // 2 else -1)
            if 0 <= to < bands:
                chain.append((group * bands + band, group * bands + to))
    coarse, edges = kernel_call(
        shift_rows_kernel,
        [
            jax.ShapeDtypeStruct((2 * fields, coarse_rows, depth), bfloat16),
            jax.ShapeDtypeStruct((2 * fields, 2, depth), bfloat16),
        ],
        [],
        8,
        100_000_000,
        own,
        peer,
    )
    halo = lax.ppermute(edges, ("date", "band"), chain)
    sibling_coarse = lax.ppermute(coarse, "date", sibling_way)
    sibling_halo = lax.ppermute(halo, "date", sibling_way)

    sums = jax.ShapeDtypeStruct((2, pairs // 2, rows, dense), float32)
    away = jax.ShapeDtypeStruct((tiles * rows, dense), float32)
    table = jax.ShapeDtypeStruct((pl.cdiv(dense, WIDE), 2 * LANES, WIDE), bfloat16)
    scratch = [
        pltpu.VMEM((2, 2 * tiles * rows, depth), bfloat16),
        pltpu.VMEM((2 * tiles * rows, WIDE), float32),
    ]
    (table,) = kernel_call(fill_tables, [table], [], 8, 4_000_000_000, taps, lon_weights)
    own_sums, straight_fine = kernel_call(
        own_dates_kernel,
        [sums, away],
        scratch,
        20,
        0,
        coarse,
        halo,
        mine,
        normals,
        lat_weights,
        table,
    )
    chip_sums, crossed_fine = kernel_call(
        sibling_dates_kernel,
        [sums, away],
        scratch,
        20,
        0,
        sibling_coarse,
        sibling_halo,
        sibling,
        normals,
        lat_weights,
        table,
        own_sums,
        straight_fine,
        straight,
    )
    out = jax.ShapeDtypeStruct((pairs, owned, dense), float32)
    results = kernel_call(
        functools.partial(mean_kernel, dates, dates * groups),
        [out, out],
        [pltpu.VMEM((2,) + out.shape, float32), pltpu.SemaphoreType.DMA((pairs,))],
        16,
        0,
        chip_sums,
        crossed_fine,
        crossed,
        normals,
        out_space=pl.ANY,
    )
    return tuple(result.reshape(leads, variables, owned, dense) for result in results)


def shards(
    model_prognosis,
    analysis_truth,
    expected_normal,
    parallel_first_indices,
    parallel_blend_factors,
    meridian_first_indices,
    meridian_blend_factors,
):
    bands = lax.axis_size("band")
    groups = lax.axis_size("date")
    halves = groups // 2
    dates = model_prognosis.shape[0]
    group = lax.axis_index("date")
    core = lax.rem(group, 2)
    half = lax.div(group, 2)

    coarse_rows = model_prognosis.shape[3]
    lat_weights = lat_tap_weights(
        parallel_first_indices,
        parallel_blend_factors,
        lax.axis_index("band") * coarse_rows,
        analysis_truth.shape[3] // coarse_rows,
    )
    dense = meridian_first_indices.shape[0]
    late = meridian_first_indices == lax.iota(jnp.int32, dense) // 4
    lon_weights = jnp.where(
        lax.broadcasted_iota(jnp.int32, (8, dense), 0) < TAPS,
        jnp.pad(meridian_blend_factors, ((0, 8 - TAPS), (0, 0))).astype(jnp.float32),
        late.astype(jnp.float32)[None],
    )
    (taps,) = kernel_call(
        taps_kernel, [jax.ShapeDtypeStruct((WIDE // 4 + 8, WIDE), jnp.int32)], [], 8, 2_000_000_000
    )
    tall = 2 * analysis_truth.shape[3] == 8 * groups
    if halves == 2 and tall and expected_normal.shape[0] * expected_normal.shape[1] % 2 == 0:
        return two_chip_maps(model_prognosis, analysis_truth, expected_normal, taps, lon_weights, lat_weights)

    own = model_prognosis.reshape((-1,) + model_prognosis.shape[3:])
    own, to_cross, to_pair = edge_rows(own)
    across = [(i, min(max(i + (1 if i % 2 else -1), 0), bands - 1)) for i in range(bands)]
    paired = lax.ppermute(to_pair, "band", [(i, i ^ 1) for i in range(bands)])
    crossed = lax.ppermute(to_cross, "band", across)
    truth = analysis_truth.reshape((-1,) + analysis_truth.shape[3:])
    normal = expected_normal.reshape((-1,) + expected_normal.shape[2:])
    error, fine = error_map(own, crossed, paired, truth, taps, lon_weights, lat_weights, normal.shape[0], groups)
    anomaly = anomaly_map(fine, truth, normal, groups)

    def packed(values):
        return (values * CARRY_SCALE).astype(jnp.float16)

    def unpacked(values):
        return values.astype(jnp.float32) / CARRY_SCALE

    def row_block(values, index):
        return lax.dynamic_index_in_dim(values, index, 0, keepdims=False)

    def mean_over_dates(maps):
        swapped = lax.ppermute(packed(row_block(maps, 1 - core)), "date", [(i, i ^ 1) for i in range(groups)])

        def chip_sum(index):
            mine = lax.dynamic_slice(maps, (core, index, 0, 0, 0), (1, 1) + maps.shape[2:])[0, 0]
            return mine + unpacked(row_block(swapped, index))

        pieces = []
        for step in range(1, halves):
            piece = packed(chip_sum(lax.rem(half + step, halves)))
            ring = [(i, (i + 2 * step) % groups) for i in range(groups)]
            pieces.append(lax.ppermute(piece, "date", ring))
        total = chip_sum(half)
        for piece in pieces:
            total = total + unpacked(piece)
        total = total / (dates * groups)
        return total.reshape(expected_normal.shape[:2] + total.shape[1:])

    return (mean_over_dates(error), mean_over_dates(anomaly))


def solution(mesh):
    in_specs = (
        P("date", None, None, "band", None),
        P("date", None, None, "band", None),
        P(None, None, "band", None),
        P("band"),
        P("band", None),
        P(),
        P(),
    )
    out_specs = (P(None, None, ("band", "date"), None), P(None, None, ("band", "date"), None))
    return jax.shard_map(shards, mesh=mesh, in_specs=in_specs, out_specs=out_specs, check_vma=False)
```

```python
import functools

import jax
import jax.numpy as jnp
from jax import lax
from jax.experimental import pallas as pl
from jax.experimental.pallas import tpu as pltpu
from jax.sharding import PartitionSpec as P

TAPS = 4
LANES = 128
WIDE = 256
CARRY_SCALE = 16.0


def edges_kernel(own_ref, kept_ref, cross_ref, pair_ref):
    even = lax.rem(lax.axis_index("band"), 2) == 0
    for index in range(own_ref.shape[0]):
        kept_ref[index] = own_ref[index]
        rows = own_ref[index].astype(jnp.float32)
        bottom, top = rows[:2], rows[rows.shape[0] - 2 :]
        pair_ref[index] = jnp.where(even, top, bottom).astype(jnp.bfloat16)
        cross_ref[index] = jnp.where(even, bottom, top).astype(jnp.bfloat16)


def taps_kernel(tap_ref):
    row = lax.broadcasted_iota(jnp.int32, tap_ref.shape, 0)
    tap_ref[...] = row - lax.broadcasted_iota(jnp.int32, tap_ref.shape, 1) // 4


def fill_tables(tap_ref, lon_ref, table_ref):
    dense = lon_ref.shape[1]
    for tile in range(pl.cdiv(dense, WIDE)):
        low_x = tile * WIDE
        width = min(WIDE, dense - low_x)
        base = low_x // 4 % LANES
        rows = width // 4 + 8
        depth_here = LANES if base + rows <= LANES else 2 * LANES
        columns = slice(low_x, low_x + width)
        offset = tap_ref[:rows, :width] - lon_ref[TAPS : TAPS + 1, columns].astype(jnp.int32)
        block = jnp.zeros((rows, width), jnp.float32)
        for tap in range(TAPS):
            block = jnp.where(offset == tap, lon_ref[tap : tap + 1, columns], block)
        parts = [block]
        if base:
            parts.insert(0, jnp.zeros((base, width), jnp.float32))
        if depth_here > base + rows:
            parts.append(jnp.zeros((depth_here - base - rows, width), jnp.float32))
        table_ref[tile, :depth_here, :width] = jnp.concatenate(parts, axis=0).astype(jnp.bfloat16)


def widened(lhs_ref, table_ref, tile, low_x, width):
    base = low_x // 4 % LANES
    begin = low_x // 4 - base
    depth = LANES if base + width // 4 + 8 <= LANES else 2 * LANES
    lhs = jnp.concatenate([lhs_ref[0, :, begin : begin + depth], lhs_ref[1, :, begin : begin + depth]], axis=1)
    table = table_ref[tile, :depth, :width]
    return jnp.dot(lhs, jnp.concatenate([table, table], axis=0), preferred_element_type=jnp.float32)


def wrapped_rows(rows, depth):
    sparse = rows.shape[1]
    filler = jnp.zeros((rows.shape[0], depth - sparse - 4), jnp.float32)
    return jnp.concatenate([rows[:, sparse - 1 :], rows, rows[:, :3], filler], axis=1)


def error_kernel(
    own_ref,
    cross_ref,
    pair_ref,
    truth_ref,
    tap_ref,
    lon_ref,
    lat_ref,
    out_ref,
    fine_ref,
    lhs_ref,
    table_ref,
):
    fields, coarse_rows, sparse = own_ref.shape
    _, fine_rows, dense = truth_ref.shape
    pairs = out_ref.shape[2]
    dates = fields // pairs
    ratio = fine_rows // coarse_rows
    span = 8 // ratio
    depth = lhs_ref.shape[2]
    tiles = pl.cdiv(dense, WIDE)
    band = lax.axis_index("band")
    even = lax.rem(band, 2) == 0
    lowest = band == 0
    highest = band == lax.axis_size("band") - 1

    fill_tables(tap_ref, lon_ref, table_ref)

    weights = lat_ref[...].T
    lat = [
        [
            jnp.broadcast_to(weights[8 * group : 8 * group + 8, tap : tap + 1], (8, LANES))
            for tap in range(TAPS + 1)
        ]
        for group in range(fine_rows // 8)
    ]
    lat = [[jnp.concatenate([w] * (depth // LANES), axis=1) for w in group] for group in lat]

    upper_half = lax.broadcasted_iota(jnp.int32, (8, depth), 0) < ratio
    for pair in range(pairs):
        for date in range(dates):
            index = date * pairs + pair
            paired = pair_ref[index].astype(jnp.float32)
            crossed = cross_ref[index].astype(jnp.float32)
            low = jnp.where(lowest, 0.0, jnp.where(even, crossed, paired))
            high = jnp.where(highest, 0.0, jnp.where(even, paired, crossed))
            rows8 = jnp.concatenate([low, own_ref[index].astype(jnp.float32), high], axis=0)
            wrapped = wrapped_rows(rows8, depth)
            spread = [jnp.broadcast_to(wrapped[i : i + 1], (8, depth)) for i in range(coarse_rows + 4)]
            mixed = [jnp.where(upper_half, spread[i], spread[i + 1]) for i in range(coarse_rows + 3)]
            both = []
            for group in range(fine_rows // 8):
                total = lat[group][0] * mixed[span * group]
                for tap in range(1, TAPS + 1):
                    total = total + lat[group][tap] * mixed[span * group + tap]
                both.append(total)
            both = jnp.concatenate(both, axis=0)
            upper = both.astype(jnp.bfloat16)
            rest = (both - upper.astype(jnp.float32)).astype(jnp.bfloat16)
            at = (pair * dates + date) * fine_rows
            lhs_ref[0, at : at + fine_rows, :] = upper
            lhs_ref[1, at : at + fine_rows, :] = rest

    for tile in range(tiles):
        low_x = tile * WIDE
        width = min(WIDE, dense - low_x)
        columns = slice(low_x, low_x + width)
        fine_ref[:, columns] = widened(lhs_ref, table_ref, tile, low_x, width)
        for pair in range(pairs):
            total = 0.0
            for date in range(dates):
                at = (pair * dates + date) * fine_rows
                actual = truth_ref[date * pairs + pair, :, columns].astype(jnp.float32)
                error = fine_ref[at : at + fine_rows, columns] - actual
                total = total + error * error
            store_by_owner(out_ref, pair, columns, total)


def store_by_owner(out_ref, pair, columns, values):
    _, halves, _, owned, _ = out_ref.shape
    for owner in range(2 * halves):
        out_ref[owner % 2, owner // 2, pair, :, columns] = values[owner * owned : (owner + 1) * owned]


def anomaly_kernel(fine_ref, truth_ref, normal_ref, out_ref):
    fields, fine_rows, dense = truth_ref.shape
    pairs = normal_ref.shape[0]
    dates = fields // pairs
    for low_x in range(0, dense, WIDE):
        columns = slice(low_x, min(low_x + WIDE, dense))
        for pair in range(pairs):
            normal = normal_ref[pair, :, columns].astype(jnp.float32)
            total = 0.0
            for date in range(dates):
                at = (pair * dates + date) * fine_rows
                actual = truth_ref[date * pairs + pair, :, columns].astype(jnp.float32)
                total = total + (fine_ref[at : at + fine_rows, columns] - normal) * (actual - normal)
            store_by_owner(out_ref, pair, columns, total)


def edge_rows(own):
    fields, _, sparse = own.shape
    vmem = pl.BlockSpec(memory_space=pltpu.VMEM)
    edges = jax.ShapeDtypeStruct((fields, 2, sparse), jnp.bfloat16)
    return pl.pallas_call(
        edges_kernel,
        out_shape=[jax.ShapeDtypeStruct(own.shape, own.dtype), edges, edges],
        in_specs=[vmem],
        out_specs=[vmem] * 3,
        compiler_params=pltpu.CompilerParams(vmem_limit_bytes=8 * 1024 * 1024),
        cost_estimate=pl.CostEstimate(flops=100_000_000, bytes_accessed=200_000, transcendentals=0),
    )(own)


def lat_tap_weights(starts, weights, first_coarse, ratio):
    rows = starts.shape[0]
    late = starts > first_coarse + lax.iota(jnp.int32, rows) // ratio - 2
    by_tap = weights.T
    early = jnp.pad(by_tap, ((0, 8 - TAPS), (0, LANES - rows)))
    shifted = jnp.pad(by_tap, ((1, 7 - TAPS), (0, LANES - rows)))
    return jnp.where(jnp.pad(late, (0, LANES - rows))[None], shifted, early)


def error_map(own, crossed, paired, truth, taps, lon, lat, pairs, owners):
    fields, _, sparse = own.shape
    _, fine_rows, dense = truth.shape
    depth = pl.cdiv(sparse + 4, LANES) * LANES
    vmem = pl.BlockSpec(memory_space=pltpu.VMEM)
    return pl.pallas_call(
        error_kernel,
        out_shape=[
            jax.ShapeDtypeStruct((2, owners // 2, pairs, fine_rows // owners, dense), jnp.float32),
            jax.ShapeDtypeStruct((fields * fine_rows, dense), jnp.float32),
        ],
        in_specs=[vmem] * 7,
        out_specs=[vmem] * 2,
        scratch_shapes=[
            pltpu.VMEM((2, fields * fine_rows, depth), jnp.bfloat16),
            pltpu.VMEM((pl.cdiv(dense, WIDE), 2 * LANES, WIDE), jnp.bfloat16),
        ],
        compiler_params=pltpu.CompilerParams(vmem_limit_bytes=24 * 1024 * 1024),
        cost_estimate=pl.CostEstimate(flops=1_000_000_000, bytes_accessed=4_000_000, transcendentals=0),
    )(own, crossed, paired, truth, taps, lon, lat)


def anomaly_map(fine, truth, normal, owners):
    pairs, fine_rows, dense = normal.shape
    vmem = pl.BlockSpec(memory_space=pltpu.VMEM)
    return pl.pallas_call(
        anomaly_kernel,
        out_shape=jax.ShapeDtypeStruct((2, owners // 2, pairs, fine_rows // owners, dense), jnp.float32),
        in_specs=[vmem] * 3,
        out_specs=vmem,
        compiler_params=pltpu.CompilerParams(vmem_limit_bytes=24 * 1024 * 1024),
        cost_estimate=pl.CostEstimate(flops=500_000_000, bytes_accessed=4_000_000, transcendentals=0),
    )(fine, truth, normal)


def first_core():
    return lax.rem(lax.axis_index("date"), 2) == 0


def lower_chip():
    return lax.axis_index("date") < lax.axis_size("date") // 2


def by_owner(ref, entries, lower):
    blocks = [ref[entry] for entry in entries]
    half = blocks[0].shape[0] // 2
    blocks = [jnp.where(lower, block[:half], block[half:]) for block in blocks]
    owned = half // 2
    return (
        jnp.concatenate([block[:owned] for block in blocks], axis=0),
        jnp.concatenate([block[owned:] for block in blocks], axis=0),
    )


def packed_tiles(entries, dense):
    full, tail = divmod(dense, LANES)
    return entries * full + (pl.cdiv(entries, LANES // tail) if tail else 0)


def pack_rows(blocks, out_ref):
    rows, dense = blocks[0].shape
    full, tail = divmod(dense, LANES)
    for at, block in enumerate(blocks):
        for tile in range(full):
            out_ref[at * full + tile] = block[:, tile * LANES : (tile + 1) * LANES].astype(out_ref.dtype)
    if tail:
        share = LANES // tail
        tails = [block[:, full * LANES :] for block in blocks]
        tails += [jnp.zeros((rows, tail), blocks[0].dtype)] * (-len(tails) % share)
        filler = [jnp.zeros((rows, LANES - share * tail), blocks[0].dtype)] if LANES % tail else []
        for at in range(0, len(tails), share):
            joined = jnp.concatenate(tails[at : at + share] + filler, axis=1)
            out_ref[len(blocks) * full + at // share] = joined.astype(out_ref.dtype)


def unpacked_rows(ref, at, entries, dense, low_x, width):
    full, tail = divmod(dense, LANES)
    parts = [
        ref[at * full + tile].astype(jnp.float32)
        for tile in range(low_x // LANES, min((low_x + width) // LANES, full))
    ]
    if low_x + width > full * LANES:
        share = LANES // tail
        start = at % share * tail
        parts.append(ref[entries * full + at // share].astype(jnp.float32)[:, start : start + tail])
    return jnp.concatenate(parts, axis=1)


def tile_entries(pairs, dates):
    return [[date * pairs + pair, date * pairs + pair + 1] for pair in range(0, pairs, 2) for date in range(dates)]


def away_kernel(dates, truth_ref, own_ref, _, straight_ref, crossed_ref, kept_ref):
    first = first_core()
    straight, crossed = [], []
    for entries in tile_entries(truth_ref.shape[0] // dates, dates):
        one, two = by_owner(truth_ref, entries, jnp.logical_not(lower_chip()))
        straight.append(jnp.where(first, one, two))
        crossed.append(jnp.where(first, two, one))
    pack_rows(straight, straight_ref)
    pack_rows(crossed, crossed_ref)
    for index in range(own_ref.shape[0]):
        kept_ref[index] = own_ref[index]


def home_kernel(dates, truth_ref, normal_ref, mine_ref, sibling_ref, normals_ref):
    pairs = normal_ref.shape[0]
    first = first_core()
    lower = lower_chip()
    for at, entries in enumerate(tile_entries(pairs, dates)):
        one, two = by_owner(truth_ref, entries, lower)
        mine_ref[at] = jnp.where(first, one, two).astype(mine_ref.dtype)
        sibling_ref[at] = jnp.where(first, two, one).astype(sibling_ref.dtype)
    for pair in range(0, pairs, 2):
        one, two = by_owner(normal_ref, [pair, pair + 1], lower)
        normals_ref[pair // 2] = jnp.where(first, one, two).astype(jnp.float32)


def shift_rows_kernel(own_ref, peer_ref, both_ref, rows_ref):
    lower = lower_chip()
    fields, coarse_rows, _ = own_ref.shape
    for index in range(2 * fields):
        block = (own_ref if index < fields else peer_ref)[index % fields]
        both_ref[index] = block
        block = block.astype(jnp.float32)
        rows_ref[index] = jnp.where(lower, block[coarse_rows - 2 :], block[:2]).astype(jnp.bfloat16)


def latitude_step(dates, coarse_ref, halo_ref, lat_ref, lhs_ref):
    fields = coarse_ref.shape[0] // 2
    pairs = fields // dates
    depth = lhs_ref.shape[2]
    rows = 2 * lhs_ref.shape[1] // (2 * fields)
    owned = rows // 2
    band = lax.axis_index("band")
    lower = lower_chip()
    first = first_core()
    outside = jnp.logical_or(
        jnp.logical_and(lower, band == 0),
        jnp.logical_and(jnp.logical_not(lower), band == lax.axis_size("band") - 1),
    )
    weights = lat_ref[...].T
    weights = jnp.where(lower, weights[: 2 * owned], weights[2 * owned : 4 * owned])
    weights = jnp.where(first, weights[:owned], weights[owned:])
    weights = jnp.concatenate([weights, weights], axis=0)
    lat = [jnp.broadcast_to(weights[:, tap : tap + 1], (rows, depth)) for tap in range(TAPS + 1)]
    first_pair = lax.broadcasted_iota(jnp.int32, (rows, depth), 0) < owned
    pending = []
    at = 0
    for side in range(2):
        for entries in tile_entries(pairs, dates):
            sources = []
            for entry in entries:
                index = side * fields + entry
                inner = coarse_ref[index].astype(jnp.float32)
                edge = jnp.where(outside, 0.0, halo_ref[index].astype(jnp.float32))
                below = jnp.concatenate([edge, inner], axis=0)
                above = jnp.concatenate([inner, edge], axis=0)
                wrapped = wrapped_rows(jnp.where(lower, below, above), depth)
                sources.append(jnp.where(first, wrapped[: TAPS + 1], wrapped[1 : TAPS + 2]))
            total = 0.0
            for tap in range(TAPS + 1):
                one, two = [jnp.broadcast_to(source[tap : tap + 1], (rows, depth)) for source in sources]
                total = total + lat[tap] * jnp.where(first_pair, one, two)
            pending.append(total)
            at += rows
            if len(pending) * rows == 16:
                block = jnp.concatenate(pending, axis=0)
                upper = block.astype(jnp.bfloat16)
                lhs_ref[0, at - 16 : at] = upper
                lhs_ref[1, at - 16 : at] = (block - upper.astype(jnp.float32)).astype(jnp.bfloat16)
                pending = []


def column_blocks(dense):
    for tile in range(pl.cdiv(dense, WIDE)):
        low_x = tile * WIDE
        width = min(WIDE, dense - low_x)
        yield tile, low_x, width, slice(low_x, low_x + width)


def added(sums, fine, actual, normal):
    error = fine - actual
    return sums[0] + error * error, sums[1] + (fine - normal) * (actual - normal)


def own_dates_kernel(
    coarse_ref,
    halo_ref,
    truth_ref,
    normals_ref,
    lat_ref,
    table_ref,
    sums_ref,
    away_ref,
    lhs_ref,
    fine_ref,
):
    tiles, rows, dense = truth_ref.shape
    dates = tiles // normals_ref.shape[0]
    latitude_step(dates, coarse_ref, halo_ref, lat_ref, lhs_ref)
    for tile, low_x, width, columns in column_blocks(dense):
        fine_ref[:, :width] = widened(lhs_ref, table_ref, tile, low_x, width)
        away_ref[:, columns] = fine_ref[tiles * rows :, :width]
        for pair in range(normals_ref.shape[0]):
            normal = normals_ref[pair, :, columns]
            sums = (0.0, 0.0)
            for at in range(pair * dates, (pair + 1) * dates):
                actual = truth_ref[at, :, columns].astype(jnp.float32)
                sums = added(sums, fine_ref[at * rows : (at + 1) * rows, :width], actual, normal)
            sums_ref[0, pair, :, columns], sums_ref[1, pair, :, columns] = sums


def sibling_dates_kernel(
    coarse_ref,
    halo_ref,
    truth_ref,
    normals_ref,
    lat_ref,
    table_ref,
    before_ref,
    straight_fine_ref,
    straight_ref,
    sums_ref,
    away_ref,
    lhs_ref,
    fine_ref,
):
    tiles, rows, dense = truth_ref.shape
    dates = tiles // normals_ref.shape[0]
    latitude_step(dates, coarse_ref, halo_ref, lat_ref, lhs_ref)
    for tile, low_x, width, columns in column_blocks(dense):
        fine_ref[:, :width] = widened(lhs_ref, table_ref, tile, low_x, width)
        away_ref[:, columns] = fine_ref[tiles * rows :, :width]
        for pair in range(normals_ref.shape[0]):
            normal = normals_ref[pair, :, columns]
            sums = (before_ref[0, pair, :, columns], before_ref[1, pair, :, columns])
            for at in range(pair * dates, (pair + 1) * dates):
                span = slice(at * rows, (at + 1) * rows)
                actual = truth_ref[at, :, columns].astype(jnp.float32)
                sums = added(sums, fine_ref[span, :width], actual, normal)
                actual = unpacked_rows(straight_ref, at, tiles, dense, low_x, width)
                sums = added(sums, straight_fine_ref[span, columns], actual, normal)
            sums_ref[0, pair, :, columns], sums_ref[1, pair, :, columns] = sums


def mean_kernel(dates, count, before_ref, fine_ref, crossed_ref, normals_ref, *refs):
    *results, held_ref, sems = refs
    tiles, rows, dense = normals_ref.shape
    owned = rows // 2
    copies = []
    for pair in range(tiles):
        for _, low_x, width, columns in column_blocks(dense):
            normal = normals_ref[pair, :, columns]
            sums = (before_ref[0, pair, :, columns], before_ref[1, pair, :, columns])
            for at in range(pair * dates, (pair + 1) * dates):
                actual = unpacked_rows(crossed_ref, at, tiles * dates, dense, low_x, width)
                sums = added(sums, fine_ref[at * rows : (at + 1) * rows, columns], actual, normal)
            for kind, total in enumerate(sums):
                total = total * (1.0 / count)
                held_ref[kind, 2 * pair, :, columns] = total[:owned]
                held_ref[kind, 2 * pair + 1, :, columns] = total[owned:]
        done = pl.ds(2 * pair, 2)
        for kind, out_ref in enumerate(results):
            copy = pltpu.make_async_copy(held_ref.at[kind, done], out_ref.at[done], sems.at[len(copies)])
            copy.start()
            copies.append(copy)
    for copy in copies:
        copy.wait()


def kernel_call(kernel, out_shape, scratch, megabytes, flops, *operands, out_space=pltpu.VMEM):
    vmem = pl.BlockSpec(memory_space=pltpu.VMEM)
    return pl.pallas_call(
        kernel,
        out_shape=out_shape,
        in_specs=[vmem] * len(operands),
        out_specs=[pl.BlockSpec(memory_space=out_space)] * len(out_shape),
        scratch_shapes=scratch,
        compiler_params=pltpu.CompilerParams(vmem_limit_bytes=megabytes * 1024 * 1024),
        cost_estimate=pl.CostEstimate(flops=flops, bytes_accessed=0, transcendentals=0),
    )(*operands)


def two_chip_maps(model_prognosis, analysis_truth, expected_normal, taps, lon_weights, lat_weights):
    bands = lax.axis_size("band")
    groups = lax.axis_size("date")
    dates, leads, variables, coarse_rows, sparse = model_prognosis.shape
    fine_rows, dense = analysis_truth.shape[3:]
    owned = fine_rows // groups
    rows = 2 * owned
    pairs = leads * variables
    fields = dates * pairs
    tiles = fields // 2
    depth = pl.cdiv(sparse + 4, LANES) * LANES
    float32, bfloat16 = jnp.float32, jnp.bfloat16
    straight_way = [(i, (i + 2) % groups) for i in range(groups)]
    crossed_way = [(i, (i + 2) % groups ^ 1) for i in range(groups)]
    sibling_way = [(i, i ^ 1) for i in range(groups)]

    own = model_prognosis.reshape(fields, coarse_rows, sparse)
    truth = analysis_truth.reshape(fields, fine_rows, dense)
    normal = expected_normal.reshape(pairs, fine_rows, dense)
    peer = lax.ppermute(model_prognosis, "date", straight_way).reshape(own.shape)

    packed = jax.ShapeDtypeStruct((packed_tiles(tiles, dense), rows, LANES), bfloat16)
    straight, crossed, own = kernel_call(
        functools.partial(away_kernel, dates),
        [packed, packed, jax.ShapeDtypeStruct(own.shape, own.dtype)],
        [],
        8,
        100_000_000,
        truth,
        own,
        taps,
    )
    straight = lax.ppermute(straight, "date", straight_way)
    crossed = lax.ppermute(crossed, "date", crossed_way)
    plain = jax.ShapeDtypeStruct((tiles, rows, dense), bfloat16)
    mine, sibling, normals = kernel_call(
        functools.partial(home_kernel, dates),
        [plain, plain, jax.ShapeDtypeStruct((pairs // 2, rows, dense), float32)],
        [],
        12,
        100_000_000,
        truth,
        normal,
    )
    sibling = lax.ppermute(sibling, "date", sibling_way)

    chain = []
    for group in range(groups):
        for band in range(bands):
            to = band + (1 if group < groups // 2 else -1)
            if 0 <= to < bands:
                chain.append((group * bands + band, group * bands + to))
    coarse, edges = kernel_call(
        shift_rows_kernel,
        [
            jax.ShapeDtypeStruct((2 * fields, coarse_rows, sparse), bfloat16),
            jax.ShapeDtypeStruct((2 * fields, 2, sparse), bfloat16),
        ],
        [],
        8,
        100_000_000,
        own,
        peer,
    )
    halo = lax.ppermute(edges, ("date", "band"), chain)
    sibling_coarse = lax.ppermute(coarse, "date", sibling_way)
    sibling_halo = lax.ppermute(halo, "date", sibling_way)

    sums = jax.ShapeDtypeStruct((2, pairs // 2, rows, dense), float32)
    away = jax.ShapeDtypeStruct((tiles * rows, dense), float32)
    table = jax.ShapeDtypeStruct((pl.cdiv(dense, WIDE), 2 * LANES, WIDE), bfloat16)
    scratch = [
        pltpu.VMEM((2, 2 * tiles * rows, depth), bfloat16),
        pltpu.VMEM((2 * tiles * rows, WIDE), float32),
    ]
    (table,) = kernel_call(fill_tables, [table], [], 8, 4_000_000_000, taps, lon_weights)
    own_sums, straight_fine = kernel_call(
        own_dates_kernel,
        [sums, away],
        scratch,
        20,
        0,
        coarse,
        halo,
        mine,
        normals,
        lat_weights,
        table,
    )
    chip_sums, crossed_fine = kernel_call(
        sibling_dates_kernel,
        [sums, away],
        scratch,
        20,
        0,
        sibling_coarse,
        sibling_halo,
        sibling,
        normals,
        lat_weights,
        table,
        own_sums,
        straight_fine,
        straight,
    )
    out = jax.ShapeDtypeStruct((pairs, owned, dense), float32)
    results = kernel_call(
        functools.partial(mean_kernel, dates, dates * groups),
        [out, out],
        [pltpu.VMEM((2,) + out.shape, float32), pltpu.SemaphoreType.DMA((pairs,))],
        16,
        0,
        chip_sums,
        crossed_fine,
        crossed,
        normals,
        out_space=pl.ANY,
    )
    return tuple(result.reshape(leads, variables, owned, dense) for result in results)


def shards(
    model_prognosis,
    analysis_truth,
    expected_normal,
    parallel_first_indices,
    parallel_blend_factors,
    meridian_first_indices,
    meridian_blend_factors,
):
    bands = lax.axis_size("band")
    groups = lax.axis_size("date")
    halves = groups // 2
    dates = model_prognosis.shape[0]
    group = lax.axis_index("date")
    core = lax.rem(group, 2)
    half = lax.div(group, 2)

    coarse_rows = model_prognosis.shape[3]
    lat_weights = lat_tap_weights(
        parallel_first_indices,
        parallel_blend_factors,
        lax.axis_index("band") * coarse_rows,
        analysis_truth.shape[3] // coarse_rows,
    )
    dense = meridian_first_indices.shape[0]
    late = meridian_first_indices == lax.iota(jnp.int32, dense) // 4
    lon_weights = jnp.where(
        lax.broadcasted_iota(jnp.int32, (8, dense), 0) < TAPS,
        jnp.pad(meridian_blend_factors, ((0, 8 - TAPS), (0, 0))).astype(jnp.float32),
        late.astype(jnp.float32)[None],
    )
    (taps,) = kernel_call(
        taps_kernel, [jax.ShapeDtypeStruct((WIDE // 4 + 8, WIDE), jnp.int32)], [], 8, 2_000_000_000
    )
    tall = 2 * analysis_truth.shape[3] == 8 * groups
    if halves == 2 and tall and expected_normal.shape[0] * expected_normal.shape[1] % 2 == 0:
        return two_chip_maps(model_prognosis, analysis_truth, expected_normal, taps, lon_weights, lat_weights)

    own = model_prognosis.reshape((-1,) + model_prognosis.shape[3:])
    own, to_cross, to_pair = edge_rows(own)
    across = [(i, min(max(i + (1 if i % 2 else -1), 0), bands - 1)) for i in range(bands)]
    paired = lax.ppermute(to_pair, "band", [(i, i ^ 1) for i in range(bands)])
    crossed = lax.ppermute(to_cross, "band", across)
    truth = analysis_truth.reshape((-1,) + analysis_truth.shape[3:])
    normal = expected_normal.reshape((-1,) + expected_normal.shape[2:])
    error, fine = error_map(own, crossed, paired, truth, taps, lon_weights, lat_weights, normal.shape[0], groups)
    anomaly = anomaly_map(fine, truth, normal, groups)

    def packed(values):
        return (values * CARRY_SCALE).astype(jnp.float16)

    def unpacked(values):
        return values.astype(jnp.float32) / CARRY_SCALE

    def row_block(values, index):
        return lax.dynamic_index_in_dim(values, index, 0, keepdims=False)

    def mean_over_dates(maps):
        swapped = lax.ppermute(packed(row_block(maps, 1 - core)), "date", [(i, i ^ 1) for i in range(groups)])

        def chip_sum(index):
            mine = lax.dynamic_slice(maps, (core, index, 0, 0, 0), (1, 1) + maps.shape[2:])[0, 0]
            return mine + unpacked(row_block(swapped, index))

        pieces = []
        for step in range(1, halves):
            piece = packed(chip_sum(lax.rem(half + step, halves)))
            ring = [(i, (i + 2 * step) % groups) for i in range(groups)]
            pieces.append(lax.ppermute(piece, "date", ring))
        total = chip_sum(half)
        for piece in pieces:
            total = total + unpacked(piece)
        total = total / (dates * groups)
        return total.reshape(expected_normal.shape[:2] + total.shape[1:])

    return (mean_over_dates(error), mean_over_dates(anomaly))


def solution(mesh):
    in_specs = (
        P("date", None, None, "band", None),
        P("date", None, None, "band", None),
        P(None, None, "band", None),
        P("band"),
        P("band", None),
        P(),
        P(),
    )
    out_specs = (P(None, None, ("band", "date"), None), P(None, None, ("band", "date"), None))
    return jax.shard_map(shards, mesh=mesh, in_specs=in_specs, out_specs=out_specs, check_vma=False)
```
